32 devices in a mesh: dp: 8 (over z, core), seq: 4 (over y, x).
Axes of the slice: x: 2, y: 2, z: 4, core: 2. Of those that a mesh axis runs over, the one named last changes fastest.
Arguments:
- tokens: bfloat16 [8, 1024, 2048], P('dp', 'seq'), may hold values from -6 to 6
- doc_ids: int32 [8, 1024], P('dp', 'seq'), may hold values from 0 to 1023, as said below
- pad_mask: int32 [8, 1024], P('dp', 'seq'), may hold values from 0 to 1, as said below
- attn_norm_gain: bfloat16 [2048], replicated, may hold values from 0.5 to 1.5
- attn_norm_bias: bfloat16 [2048], replicated, may hold values from -3 to 3
- qkv_weight: bfloat16 [2304, 2048], P(('dp', 'seq')), may hold values from -0.125 to 0.125
- query_bias: bfloat16 [2048], replicated, may hold values from -3 to 3
- value_bias: bfloat16 [128], replicated, may hold values from -3 to 3
- out_weight: bfloat16 [2048, 2048], P(('dp', 'seq')), may hold values from -2 to 2
- out_bias: bfloat16 [2048], replicated, may hold values from -3 to 3
- mlp_norm_gain: bfloat16 [2048], replicated, may hold values from 0.5 to 1.5
- mlp_norm_bias: bfloat16 [2048], replicated, may hold values from -3 to 3
- fc_weight: bfloat16 [8192, 2048], P(('dp', 'seq')), may hold values from -0.125 to 0.125
- fc_bias: bfloat16 [8192], replicated, may hold values from -3 to 3
- proj_weight: bfloat16 [8192, 2048], P(('dp', 'seq')), may hold values from -0.0625 to 0.0625
- proj_bias: bfloat16 [2048], replicated, may hold values from -3 to 3
- cotangent: bfloat16 [8, 1024, 2048], P('dp', 'seq'), may hold values from -6 to 6
Outputs:
- block_out: bfloat16 [8, 1024, 2048], P('dp', 'seq')
- tokens_grad: bfloat16 [8, 1024, 2048], P('dp', 'seq')
- attn_norm_gain_grad: float32 [2048], replicated
- attn_norm_bias_grad: float32 [2048], replicated
- qkv_weight_grad: float32 [2304, 2048], P(('dp', 'seq'))
- query_bias_grad: float32 [2048], replicated
- value_bias_grad: float32 [128], replicated
- out_weight_grad: float32 [2048, 2048], P(('dp', 'seq'))
- out_bias_grad: float32 [2048], replicated
- mlp_norm_gain_grad: float32 [2048], replicated
- mlp_norm_bias_grad: float32 [2048], replicated
- fc_weight_grad: float32 [8192, 2048], P(('dp', 'seq'))
- fc_bias_grad: float32 [8192], replicated
- proj_weight_grad: float32 [8192, 2048], P(('dp', 'seq'))
- proj_bias_grad: float32 [2048], replicated
The draws below stay inside these ranges and needn't reach their ends.
Inputs may be any that keep to these rules, and one draw needn't show every extreme that they name: `doc_ids`: along each row the ids never fall. In every row one document begins within the first 256 positions and ends within the last 256. Padding positions carry the id 1024 - 1. `pad_mask`: every row ends with a run of zeros, 1 to 255 long, and all its other positions are 1.
All inputs are finite; a program needn't handle non-finite values.
Results may differ from the reference program's by a relative error of at most 0.015.
Values may be sent and summed in bfloat16 or wider, within the bound.
No kernel may reach another device: no remote copies, remote signals or barrier semaphores. Data moves between devices by JAX's collectives and lax.ppermute only.
A program may use at most 256 MiB of HBM per device.

```python
import jax
import jax.numpy as jnp
from jax import lax

HEADS = 16
HDIM = 128
FF = 8192
D = 2048
QKV = 2304
TOK_DEV = 256
BATCH = 8
SEQ = 1024


def packing(key):
    open_key, close_key, tail_key, split_key = jax.random.split(key, 4)
    opening = jax.random.randint(open_key, (BATCH, 1), 0, TOK_DEV)
    closing = jax.random.randint(close_key, (BATCH, 1), SEQ - TOK_DEV, SEQ - TOK_DEV // 2)
    pad_start = closing + 1 + jax.random.randint(tail_key, (BATCH, 1), 0, SEQ - 1 - closing)
    position = jnp.arange(SEQ, dtype=jnp.int32)[None, :]
    random_cut = jax.random.randint(split_key, (BATCH, SEQ), 0, 8) == 0
    outside = (position < opening) | (position > closing + 1)
    boundary = random_cut & outside | (position == opening) | (position == closing + 1) | (position == pad_start)
    boundary = boundary & (position > 0)
    documents = jnp.cumsum(boundary.astype(jnp.int32), axis=1).astype(jnp.int32)
    living = (position < pad_start).astype(jnp.int32)
    documents = jnp.where(living == 1, documents, jnp.int32(SEQ - 1)).astype(jnp.int32)
    return (documents, living)


def draw_doc_ids(key, part):
    shared = packing(key)
    return shared[0]


def draw_pad_mask(key, part):
    shared = packing(key)
    return shared[1]


def spiked(drawn, stream_key, source, target, shards_of, factor):
    def block_of(axis_at):
        return (jnp.arange(drawn.shape[axis_at]) // (drawn.shape[axis_at] // shards_of)).reshape((-1,) + (1,) * (drawn.ndim - 1 - axis_at))

    first = jax.random.permutation(stream_key, shards_of)[block_of(target)]
    second = (block_of(target) + shards_of // 2) % shards_of
    return jnp.where((block_of(source) == first) | (block_of(source) == second), factor * drawn, drawn)


def block_scale(key, dims, cuts, low, high):
    loudness, own = 1.0, jax.random.fold_in(key, 6)
    for axis_at, shards_of in cuts:
        heights = jnp.exp(jax.random.uniform(jax.random.fold_in(own, axis_at), (shards_of,), jnp.float32, low / len(cuts), high / len(cuts)))
        loudness = loudness * jnp.repeat(heights, dims[axis_at] // shards_of).reshape([-1 if axis == axis_at else 1 for axis in range(len(dims))])
    return loudness


def scatter_about(key, shape, scale, bound, cuts=(), kind=jnp.bfloat16):
    drawn = jax.random.normal(key, shape, jnp.float32) * scale
    if len(cuts) > 0:
        drawn = block_scale(key, shape, cuts, -0.22, 0.18) * drawn
    return jnp.clip(drawn, min=-bound, max=bound).astype(kind)


def bell_draw_with(key, extent, scale, reach, shards, heavy, kind=jnp.bfloat16):
    values = scale * jax.random.normal(key, extent, jnp.float32)
    if shards:
        values = values * block_scale(key, extent, shards, -0.22, 0.18)
    return jnp.clip(spiked(values, jax.random.fold_in(key, 3), *heavy), -reach, reach).astype(kind)


def setup_inputs(seed: int = 0) -> dict:
    splits = jax.random.split(jax.random.key(seed), 18)
    return {
        "tokens": scatter_about(splits[0], (BATCH, SEQ, D), 1.0, 6.0, ((0, 8), (1, 4))),
        "doc_ids": draw_doc_ids(jax.random.fold_in(splits[17], 71), 0),
        "pad_mask": draw_pad_mask(jax.random.fold_in(splits[17], 71), 0),
        "attn_norm_gain": jnp.clip(1.0 + 0.1 * jax.random.normal(splits[3], (D,), jnp.float32), 0.5, 1.5).astype(jnp.bfloat16),
        "attn_norm_bias": scatter_about(splits[4], (D,), 0.5, 3.0),
        "qkv_weight": scatter_about(splits[5], (QKV, D), D ** -0.5, 0.125, ((0, 32),)),
        "query_bias": scatter_about(splits[6], (D,), 0.5, 3.0),
        "value_bias": scatter_about(splits[7], (HDIM,), 0.5, 3.0),
        "out_weight": scatter_about(splits[8], (D, D), (D * 4 // SEQ) ** -0.5, 2.0, ((0, 32),)),
        "out_bias": scatter_about(splits[9], (D,), 0.5, 3.0),
        "mlp_norm_gain": jnp.clip(1.0 + 0.1 * jax.random.normal(splits[10], (D,), jnp.float32), 0.5, 1.5).astype(jnp.bfloat16),
        "mlp_norm_bias": scatter_about(splits[11], (D,), 0.5, 3.0),
        "fc_weight": scatter_about(splits[12], (FF, D), D ** -0.5, 0.125, ((0, 32),)),
        "fc_bias": scatter_about(splits[13], (FF,), 0.5, 3.0),
        "proj_weight": scatter_about(splits[14], (FF, D), FF ** -0.5, 0.0625, ((0, 32),)),
        "proj_bias": scatter_about(splits[15], (D,), 0.5, 3.0),
        "cotangent": bell_draw_with(splits[16], (BATCH, SEQ, D), 1.0, 6.0, ((0, 8), (1, 4)), (1, 2, 4, 2.0)),
    }


@jax.custom_vjp
def low(v):
    return lax.optimization_barrier(v.astype(jnp.bfloat16)).astype(jnp.float32)

@jax.custom_vjp
def low_back(v):
    return v

def low_keep(v):
    return (low(v), None)

def low_pass(kept, grad):
    return (grad,)

def back_keep(v):
    return (v, None)

def back_low(kept, grad):
    return (low(grad),)
low.defvjp(low_keep, low_pass)
low_back.defvjp(back_keep, back_low)
EPSILON = 1e-05
NEGATIVE = -1e+30
PRECISE = lax.Precision.HIGHEST

def matmul(left, right):
    return jnp.dot(left, right, precision=PRECISE)

def layer_norm(values, gain, shift):
    center = lax.optimization_barrier(jnp.mean(values, -1, keepdims=True))
    shifted = values - center
    spread = lax.optimization_barrier(jnp.mean(shifted * shifted, -1, keepdims=True))
    return shifted * lax.rsqrt(spread + EPSILON) * gain + shift

def row_forward(params, row_tokens, row_docs, row_live):
    gain_one, shift_one, qkv_matrix, query_shift, value_shift, out_matrix, out_shift, gain_two, shift_two, fc_matrix, fc_shift, proj_matrix, proj_shift = params
    hidden_one = low(layer_norm(row_tokens, gain_one, shift_one))
    qkv = low_back(matmul(hidden_one, qkv_matrix.T))
    query = low(qkv[:, :D] + query_shift).reshape(SEQ, HEADS, HDIM)
    keys = low(qkv[:, D:D + HDIM])
    values = low(qkv[:, D + HDIM:] + value_shift)
    scores = low_back(jnp.einsum('shd,td->hst', query, keys, precision=PRECISE) * HDIM ** (-0.5))
    position = jnp.arange(SEQ)
    causal = position[None, :] <= position[:, None]
    same_doc = row_docs[None, :] == row_docs[:, None]
    usable = (row_live[None, :] == 1) | (position[None, :] == position[:, None])
    allowed = (causal & same_doc & usable)[None]
    masked = jnp.where(allowed, scores, NEGATIVE)
    highest = lax.optimization_barrier(jnp.max(masked, -1, keepdims=True))
    weights = jnp.where(allowed, jnp.exp(masked - highest), 0.0)
    probs = weights / lax.optimization_barrier(jnp.sum(weights, -1, keepdims=True))
    attn = jnp.einsum('hst,td->shd', probs, values, precision=PRECISE).reshape(SEQ, D)
    attn = low(low_back(attn))
    middle = row_tokens + low_back(matmul(attn, out_matrix.T)) + out_shift
    hidden_two = low(layer_norm(middle, gain_two, shift_two))
    pre = low_back(matmul(hidden_two, fc_matrix.T)) + fc_shift
    act = low(jax.nn.gelu(pre, approximate=True))
    return middle + low_back(matmul(act, proj_matrix)) + proj_shift

def reference(tokens, doc_ids, pad_mask, attn_norm_gain, attn_norm_bias, qkv_weight, query_bias, value_bias, out_weight, out_bias, mlp_norm_gain, mlp_norm_bias, fc_weight, fc_bias, proj_weight, proj_bias, cotangent):
    params = tuple((p.astype(jnp.float32) for p in (attn_norm_gain, attn_norm_bias, qkv_weight, query_bias, value_bias, out_weight, out_bias, mlp_norm_gain, mlp_norm_bias, fc_weight, fc_bias, proj_weight, proj_bias)))

    def step(totals, row):
        row_tokens, row_docs, row_live, row_cot = row

        def forward(weights_now, inputs_now):
            return row_forward(weights_now, inputs_now, row_docs, row_live)
        result, pullback = jax.vjp(forward, params, row_tokens.astype(jnp.float32))
        grads, grad_input = pullback(row_cot.astype(jnp.float32))
        totals = jax.tree.map(jnp.add, totals, grads)
        return (totals, (result.astype(jnp.bfloat16), grad_input.astype(jnp.bfloat16)))
    zeros = jax.tree.map(jnp.zeros_like, params)
    totals, (outputs, input_grads) = lax.scan(step, zeros, (tokens, doc_ids, pad_mask, cotangent))
    return (outputs, input_grads, totals[0], totals[1], totals[2], totals[3], totals[4], totals[5], totals[6], totals[7], totals[8], totals[9], totals[10], totals[11], totals[12])
```

```python
import jax
import jax.numpy as jnp
from jax import lax
from jax.experimental import pallas as pl
from jax.experimental.pallas import tpu as pltpu
from jax.sharding import PartitionSpec as P

HEADS = 16
HDIM = 128
EPSILON = 1e-05
NEGATIVE = -1e30
BF = jnp.bfloat16
F32 = jnp.float32


def dot_nt(left, right):
    return lax.dot_general(left, right, (((1,), (1,)), ((), ())), preferred_element_type=F32)


def dot_nn(left, right):
    return lax.dot_general(left, right, (((1,), (0,)), ((), ())), preferred_element_type=F32)


def dot_tn(left, right):
    return lax.dot_general(left, right, (((0,), (0,)), ((), ())), preferred_element_type=F32)


def normalize(values):
    center = jnp.mean(values, -1, keepdims=True)
    shifted = values - center
    inverse = lax.rsqrt(jnp.mean(shifted * shifted, -1, keepdims=True) + EPSILON)
    return (shifted * inverse, inverse)


def norm_back(grad_normed, normed, inverse):
    first_mean = jnp.mean(grad_normed, -1, keepdims=True)
    second_mean = jnp.mean(grad_normed * normed, -1, keepdims=True)
    return inverse * (grad_normed - first_mean - normed * second_mean)


def gelu_tanh(values):
    return jax.nn.gelu(values, approximate=True)


FREE = pl.CostEstimate(flops=0, bytes_accessed=0, transcendentals=0)
TILE = 256
ANY = pl.BlockSpec(memory_space=pl.ANY)


def call(kernel, name, out_shape, scratch, inputs):
    return pl.pallas_call(
        kernel,
        name=name,
        out_shape=out_shape,
        in_specs=[ANY] * len(inputs),
        out_specs=jax.tree.map(lambda _: ANY, out_shape),
        scratch_shapes=scratch,
        cost_estimate=FREE,
        compiler_params=pltpu.CompilerParams(vmem_limit_bytes=44 * 1024 * 1024),
    )(*inputs)


def start_rows(pieces, buffer, sems):
    copies, row = [], 0
    for index, piece in enumerate(pieces):
        count = piece.shape[0]
        copy = pltpu.make_async_copy(piece, buffer.at[pl.ds(row, count)], sems.at[index])
        copy.start()
        copies.append((row, count, copy))
        row += count
    return copies


def wait_rows(copies, first, last):
    for row, _, copy in copies:
        if first <= row < last:
            copy.wait()


def join_rows(pieces):
    rows, width = sum(p.shape[0] for p in pieces), pieces[0].shape[1]

    def kernel(*refs):
        out_ref, buffer, in_sem, out_sem = refs[len(pieces) :]
        sent = []
        for index, (row, count, copy) in enumerate(start_rows(refs[: len(pieces)], buffer, in_sem)):
            copy.wait()
            part = pl.ds(row, count)
            sent.append(pltpu.make_async_copy(buffer.at[part], out_ref.at[part], out_sem.at[index]))
            sent[-1].start()
        for copy in sent:
            copy.wait()

    return call(
        kernel,
        "join_rows",
        jax.ShapeDtypeStruct((rows, width), pieces[0].dtype),
        [
            pltpu.VMEM((rows, width), pieces[0].dtype),
            pltpu.SemaphoreType.DMA((len(pieces),)),
            pltpu.SemaphoreType.DMA((len(pieces),)),
        ],
        tuple(pieces),
    )


def row_tile(rows):
    return min(rows, 512)


def slope(values):
    inner = 0.7978845608028654 * (values + 0.044715 * values * values * values)
    curve = jnp.tanh(inner)
    return 0.5 * (1.0 + curve) + 0.5 * values * (1.0 - curve * curve) * 0.7978845608028654 * (
        1.0 + 3 * 0.044715 * values * values
    )


def hidden_forward(pieces, slots, shift):
    rows, width = sum(p.shape[0] for p in pieces), pieces[0].shape[1]
    units = sum(s.shape[0] for s in slots)
    step = row_tile(rows)

    def kernel(*refs):
        piece_refs, slot_refs = refs[: len(pieces)], refs[len(pieces) : len(pieces) + len(slots)]
        shift_hbm, pre_ref, act_ref, x, w, bias, pre_buf, act_buf, x_sem, w_sem, b_sem, out_sem = refs[
            len(pieces) + len(slots) :
        ]
        w_copies = start_rows(slot_refs, w, w_sem)
        x_copies = start_rows(piece_refs, x, x_sem)
        bias_copy = pltpu.make_async_copy(shift_hbm, bias, b_sem)
        bias_copy.start()
        bias_copy.wait()
        wait_rows(x_copies, 0, rows)
        sent = []
        for tile in range(units // TILE):
            slot = tile % 2
            columns = pl.ds(tile * TILE, TILE)
            wait_rows(w_copies, tile * TILE, (tile + 1) * TILE)
            if tile >= 2:
                for copy in sent[tile - 2]:
                    copy.wait()

            @pl.loop(0, rows // step)
            def _(index):
                part = pl.ds(index * step, step)
                pre = dot_nt(x[part], w[columns]) + bias[:, columns]
                pre_buf[slot, part] = pre
                act_buf[slot, part] = gelu_tanh(pre).astype(BF)

            sent.append(
                (
                    pltpu.make_async_copy(pre_buf.at[slot], pre_ref.at[:, columns], out_sem.at[slot, 0]),
                    pltpu.make_async_copy(act_buf.at[slot], act_ref.at[:, columns], out_sem.at[slot, 1]),
                )
            )
            for copy in sent[tile]:
                copy.start()
        for pair in sent[-2:]:
            for copy in pair:
                copy.wait()

    return call(
        kernel,
        "hidden_forward",
        (jax.ShapeDtypeStruct((rows, units), F32), jax.ShapeDtypeStruct((rows, units), BF)),
        [
            pltpu.VMEM((rows, width), BF),
            pltpu.VMEM((units, width), BF),
            pltpu.VMEM((1, units), F32),
            pltpu.VMEM((2, rows, TILE), F32),
            pltpu.VMEM((2, rows, TILE), BF),
            pltpu.SemaphoreType.DMA((len(pieces),)),
            pltpu.SemaphoreType.DMA((len(slots),)),
            pltpu.SemaphoreType.DMA,
            pltpu.SemaphoreType.DMA((2, 2)),
        ],
        (*pieces, *slots, shift.reshape(1, units)),
    )


def hidden_backward(pieces, slots, pre):
    rows, width = sum(p.shape[0] for p in pieces), pieces[0].shape[1]
    units = sum(s.shape[0] for s in slots)
    step = row_tile(rows)

    def kernel(*refs):
        piece_refs, slot_refs = refs[: len(pieces)], refs[len(pieces) : len(pieces) + len(slots)]
        pre_ref, grad_ref, sum_ref, x, w, sums, pre_buf, out_buf, x_sem, w_sem, p_sem, out_sem, s_sem = refs[
            len(pieces) + len(slots) :
        ]
        w_copies = start_rows(slot_refs, w, w_sem)
        x_copies = start_rows(piece_refs, x, x_sem)
        tiles = units // TILE

        def pre_copy(tile):
            return pltpu.make_async_copy(
                pre_ref.at[:, pl.ds(tile * TILE, TILE)], pre_buf.at[tile % 2], p_sem.at[tile % 2]
            )

        pre_copy(0).start()
        wait_rows(x_copies, 0, rows)
        sent = []
        for tile in range(tiles):
            slot = tile % 2
            columns = pl.ds(tile * TILE, TILE)
            wait_rows(w_copies, tile * TILE, (tile + 1) * TILE)
            pre_copy(tile).wait()
            if tile + 1 < tiles:
                pre_copy(tile + 1).start()
            if tile >= 2:
                sent[tile - 2].wait()
            sums[:, columns] = jnp.zeros((1, TILE), F32)

            @pl.loop(0, rows // step)
            def _(index):
                part = pl.ds(index * step, step)
                grad = dot_nt(x[part], w[columns]) * slope(pre_buf[slot, part])
                out_buf[slot, part] = grad.astype(BF)
                sums[:, columns] += jnp.sum(grad, 0, keepdims=True)

            sent.append(pltpu.make_async_copy(out_buf.at[slot], grad_ref.at[:, columns], out_sem.at[slot]))
            sent[tile].start()
        last = pltpu.make_async_copy(sums, sum_ref, s_sem)
        last.start()
        for copy in sent[-2:]:
            copy.wait()
        last.wait()

    grad, sums = call(
        kernel,
        "hidden_backward",
        (jax.ShapeDtypeStruct((rows, units), BF), jax.ShapeDtypeStruct((1, units), F32)),
        [
            pltpu.VMEM((rows, width), BF),
            pltpu.VMEM((units, width), BF),
            pltpu.VMEM((1, units), F32),
            pltpu.VMEM((2, rows, TILE), F32),
            pltpu.VMEM((2, rows, TILE), BF),
            pltpu.SemaphoreType.DMA((len(pieces),)),
            pltpu.SemaphoreType.DMA((len(slots),)),
            pltpu.SemaphoreType.DMA((2,)),
            pltpu.SemaphoreType.DMA((2,)),
            pltpu.SemaphoreType.DMA,
        ],
        (*pieces, *slots, pre),
    )
    return grad, sums.reshape(units)


def hidden_sum(lefts, slots, tok, order, cuts):
    rows = lefts[0].shape[0]
    half = lefts[0].shape[1]
    width = slots[0].shape[1]
    depth = half * len(lefts)
    wide = min(width, 1024)

    def kernel(*refs):
        left_refs, slot_refs = refs[: len(lefts)], refs[len(lefts) : len(lefts) + len(slots)]
        rest = refs[len(lefts) + len(slots) :]
        own_ref, other_refs = rest[0], rest[1 : 1 + len(order) * cuts]
        x, w, own_buf, out_buf, x_sem, w_sem, out_sem = rest[1 + len(order) * cuts :]
        x_copies = []
        for index, left in enumerate(left_refs):
            x_copies.append(pltpu.make_async_copy(left, x.at[index], x_sem.at[index]))
            x_copies[-1].start()
        w_copies = start_rows(slot_refs, w, w_sem)
        for copy in x_copies:
            copy.wait()
        wait_rows(w_copies, 0, depth)

        def product(block, columns):
            part = pl.ds(block * tok, tok)
            total = dot_nn(x[0, part], w[pl.ds(0, half), columns])
            for index in range(1, len(lefts)):
                total = total + dot_nn(x[index, part], w[pl.ds(index * half, half), columns])
            return total

        sent = []
        for count, block in enumerate(order):
            slot = count % 2
            if count >= 2:
                for copy in sent[count - 2]:
                    copy.wait()

            @pl.loop(0, width // wide)
            def _(index):
                columns = pl.ds(pl.multiple_of(index * wide, wide), wide)
                out_buf[slot, :, columns] = product(block, columns).astype(BF)

            size = tok // cuts
            sent.append(
                [
                    pltpu.make_async_copy(
                        out_buf.at[slot, pl.ds(cut * size, size)],
                        other_refs[count * cuts + cut],
                        out_sem.at[slot, cut],
                    )
                    for cut in range(cuts)
                ]
            )
            for copy in sent[count]:
                copy.start()

        @pl.loop(0, width // wide)
        def _(index):
            columns = pl.ds(pl.multiple_of(index * wide, wide), wide)
            own_buf[:, columns] = product(0, columns)

        own_copy = pltpu.make_async_copy(own_buf, own_ref, out_sem.at[2, 0])
        own_copy.start()
        for copies in sent[-2:]:
            for copy in copies:
                copy.wait()
        own_copy.wait()

    return call(
        kernel,
        "hidden_sum",
        tuple(
            [jax.ShapeDtypeStruct((tok, width), F32)]
            + [jax.ShapeDtypeStruct((tok // cuts, width), BF)] * (len(order) * cuts)
        ),
        [
            pltpu.VMEM((len(lefts), rows, half), BF),
            pltpu.VMEM((depth, width), BF),
            pltpu.VMEM((tok, width), F32),
            pltpu.VMEM((2, tok, width), BF),
            pltpu.SemaphoreType.DMA((len(lefts),)),
            pltpu.SemaphoreType.DMA((len(slots),)),
            pltpu.SemaphoreType.DMA((3, cuts)),
        ],
        (*lefts, *slots),
    )


def weight_terms(left, pieces, outs):
    rows, units = left.shape
    width = pieces[0].shape[1]
    size = units // outs
    step = min(rows, 1024)

    def kernel(*refs):
        left_ref, piece_refs = refs[0], refs[1 : 1 + len(pieces)]
        out_refs = refs[1 + len(pieces) : 1 + len(pieces) + outs]
        l, x, out_buf, l_sem, x_sem, out_sem = refs[1 + len(pieces) + outs :]
        l_copy = pltpu.make_async_copy(left_ref, l, l_sem)
        l_copy.start()
        x_copies = start_rows(piece_refs, x, x_sem)
        l_copy.wait()
        wait_rows(x_copies, 0, rows)
        sent = []
        for tile in range(units // TILE):
            slot = tile % 2
            if tile >= 2:
                for copy in sent[tile - 2]:
                    copy.wait()

            columns = pl.ds(tile * TILE, TILE)
            wide = min(width, 1024)

            @pl.loop(0, width // wide)
            def _(index):
                span = pl.ds(pl.multiple_of(index * wide, wide), wide)
                out_buf[slot, :, span] = dot_tn(l[:, columns], x[:, span]).astype(BF)

            copies, row = [], tile * TILE
            while row < (tile + 1) * TILE:
                count = min(size - row % size, TILE)
                copies.append(
                    pltpu.make_async_copy(
                        out_buf.at[slot, pl.ds(row - tile * TILE, count)],
                        out_refs[row // size].at[pl.ds(row % size, count)],
                        out_sem.at[slot, len(copies)],
                    )
                )
                row += count
            for copy in copies:
                copy.start()
            sent.append(copies)
        for copies in sent[-2:]:
            for copy in copies:
                copy.wait()

    return call(
        kernel,
        "weight_terms",
        tuple([jax.ShapeDtypeStruct((size, width), BF)] * outs),
        [
            pltpu.VMEM((rows, units), BF),
            pltpu.VMEM((rows, width), BF),
            pltpu.VMEM((2, TILE, width), BF),
            pltpu.SemaphoreType.DMA,
            pltpu.SemaphoreType.DMA((len(pieces),)),
            pltpu.SemaphoreType.DMA((2, max(1, TILE // size))),
        ],
        (left, *pieces),
    )


def after(value, *needed):
    return lax.optimization_barrier((value, needed))[0]


def add_wide(left, right):
    return left.astype(F32) + right.astype(F32)


def add_low(left, right):
    return add_wide(left, right).astype(BF)


class Links:
    def __init__(self):
        self.seq_n = lax.axis_size("seq")
        self.dp_n = lax.axis_size("dp")
        self.z_n = self.dp_n // 2
        half = self.seq_n // 2
        self.ring = list(range(half)) + list(range(self.seq_n - 1, half - 1, -1))
        self.seq = lax.axis_index("seq")
        dp = lax.axis_index("dp")
        self.z = dp // 2
        self.core = dp % 2
        self.chips = list(range(0, self.z_n, 2)) + list(range(self.z_n - 1, 0, -2))
        self.chip_place = [self.chips.index(z) for z in range(self.z_n)]
        self.chip_pos = jnp.where(self.z % 2 == 0, self.z // 2, self.z_n - 1 - self.z // 2)
        self.place = [self.ring.index(s) for s in range(self.seq_n)]
        self.pos = jnp.where(self.seq < half, self.seq, self.seq_n - 1 + half - self.seq)

    def seq_at(self, rel):
        n, place = self.seq_n, (self.pos + rel) % self.seq_n
        return jnp.where(place < n // 2, place, n - 1 + n // 2 - place)

    def from_rel(self, value, rel):
        n = self.seq_n
        pairs = [(self.ring[(p + rel) % n], self.ring[p]) for p in range(n)]
        return lax.ppermute(value, "seq", pairs)

    def swap_core(self, value):
        pairs = [(i, i ^ 1) for i in range(self.dp_n)]
        return lax.ppermute(value, "dp", pairs)

    def z_next(self, value):
        pairs = [(self.chips[p - 1], self.chips[p]) for p in range(self.z_n)]
        return lax.ppermute(value, "dp", [(2 * i + c, 2 * j + c) for i, j in pairs for c in range(2)])

    def z_back(self, value):
        pairs = [(self.chips[p], self.chips[p - 1]) for p in range(self.z_n)]
        return lax.ppermute(value, "dp", [(2 * i + c, 2 * j + c) for i, j in pairs for c in range(2)])

    def gather_direct(self, value):
        return [value] + [self.from_rel(value, r) for r in range(1, self.seq_n)]

    def gather_near(self, value):
        if self.seq_n != 4:
            return self.gather_direct(value)
        return [value, self.from_rel(value, 1), None, self.from_rel(value, 3)]

    def gather_far(self, blocks):
        if self.seq_n != 4:
            return blocks
        half = blocks[0].shape[0] // 2
        top = self.from_rel(blocks[1][:half], 1)
        low = self.from_rel(blocks[3][half:], 3)
        return [blocks[0], blocks[1], top, low, blocks[3]]

    def exchange(self, parts):
        n = self.seq_n
        got = [parts[0]] + [None] * (n - 1)
        for r in range(1, n):
            got[n - r] = self.from_rel(parts[r], n - r)
        return got

    @property
    def sum_order(self):
        return (2, 1, 3) if self.seq_n == 4 else tuple(range(1, self.seq_n))

    @property
    def sum_cuts(self):
        return 2 if self.seq_n == 4 else 1

    def sum_far(self, parts):
        if self.seq_n != 4:
            return self.exchange(list(parts))[1:]
        far_top, far_low, right_top, right_low, left_top, left_low = parts[1:]
        return [
            self.from_rel(far_top, 3),
            self.from_rel(far_low, 1),
            self.from_rel(right_low, 3),
            self.from_rel(left_top, 1),
        ]

    def sum_near(self, parts, far, *needed):
        if self.seq_n != 4:
            return far
        return [
            self.from_rel(after(add_low(parts[3], far[0]), needed), 3),
            self.from_rel(after(add_low(parts[6], far[1]), needed), 1),
        ]

    def sum_end(self, own, far, near):
        if self.seq_n != 4:
            for member in near:
                own = own + member.astype(F32)
            return own
        half = own.shape[0] // 2
        return jnp.concatenate(
            [
                own[:half] + add_wide(near[0], far[3]),
                own[half:] + add_wide(far[2], near[1]),
            ],
            0,
        )

    def chips_ordered(self, blocks):
        n = self.z_n
        return [
            lax.select_n(self.z, *[blocks[(self.chip_place[z] - self.chip_place[k]) % n] for z in range(n)])
            for k in range(n)
        ]

    def chip_before(self, m):
        n, place = self.z_n, (self.chip_pos - m) % self.z_n
        return jnp.where(place < (n + 1) // 2, 2 * place, 2 * (n - 1 - place) + 1)

    def chip_sum(self, parts, m, came, *needed):
        return self.z_back(after(self.chip_total(parts, m, came).astype(BF), needed))

    def chip_total(self, parts, m, came):
        total = add_wide(*parts[m]) if isinstance(parts[m], tuple) else parts[m].astype(F32)
        return total if came is None else total + came.astype(F32)

    def other_seq(self, value, bit):
        return lax.ppermute(value, "seq", [(i, i ^ bit) for i in range(self.seq_n)])

    def other_dp(self, value, bit):
        return lax.ppermute(value, "dp", [(i, i ^ bit) for i in range(self.dp_n)])


def shards(
    tokens,
    doc_ids,
    pad_mask,
    attn_norm_gain,
    attn_norm_bias,
    qkv_weight,
    query_bias,
    value_bias,
    out_weight,
    out_bias,
    mlp_norm_gain,
    mlp_norm_bias,
    fc_weight,
    fc_bias,
    proj_weight,
    proj_bias,
    cotangent,
):
    links = Links()
    seq_n, dp_n, z_n = links.seq_n, links.dp_n, links.z_n
    tok = tokens.shape[1]
    width = tokens.shape[2]
    scale = HDIM ** (-0.5)
    gain_one = attn_norm_gain.astype(F32)
    shift_one = attn_norm_bias.astype(F32)
    out_shift = out_bias.astype(F32)
    gain_two = mlp_norm_gain.astype(F32)
    shift_two = mlp_norm_bias.astype(F32)
    proj_shift = proj_bias.astype(F32)

    docs = doc_ids[0]
    codes = jnp.where(pad_mask[0] == 1, docs, -1)
    codes = jnp.stack([codes // 128, codes % 128] + [jnp.zeros_like(codes)] * 14).astype(BF)

    units = fc_weight.shape[0]
    split = z_n * units

    block_index = jnp.arange(dp_n)
    owner = 2 * links.chip_before(block_index % z_n) + (links.core ^ (block_index // z_n))
    owner = owner[:, None] == jnp.arange(dp_n)[None, :]
    own_seq = jnp.arange(seq_n) == links.seq
    fc_shift = fc_bias.reshape(dp_n, seq_n, units).astype(F32)
    fc_shift = jnp.sum(jnp.where(own_seq[None, :, None], fc_shift, 0.0), 1)
    fc_shift = jnp.sum(jnp.where(owner[:, :, None], fc_shift[None], 0.0), 1).reshape(-1)
    qkv_rows = qkv_weight.shape[0]
    qkv_shift = jnp.concatenate(
        [query_bias.astype(F32), jnp.zeros((HDIM,), F32), value_bias.astype(F32)]
    ).reshape(dp_n, seq_n, qkv_rows)
    qkv_shift = jnp.sum(jnp.where(own_seq[None, :, None], qkv_shift, 0.0), 1).reshape(-1, 1)

    qkv_chips = [qkv_weight, links.z_next(qkv_weight)]
    grad_low = cotangent.reshape(tok, width)

    def norm_one(member):
        flat = member.reshape(tok, width).astype(F32)
        normed, inverse = normalize(flat)
        return (normed * gain_one + shift_one).astype(BF), normed, inverse

    hidden_one, normed_one, inverse_one = norm_one(tokens)
    ones = links.gather_near(after(hidden_one, qkv_chips[1]))
    qkv_chips[1] = after(qkv_chips[1], hidden_one)
    for _ in range(z_n - 2):
        qkv_chips.append(links.z_next(qkv_chips[-1]))
    fc_chips = [fc_weight, links.z_next(after(fc_weight, qkv_chips))]
    qkv_chips = after(qkv_chips, ones[1], ones[-1], qkv_shift, fc_shift)
    out_full = lax.all_gather(out_weight, ("dp", "seq"), axis=0, tiled=True)

    mine = jnp.stack(links.chips_ordered(qkv_chips), 0)
    other = links.swap_core(mine)

    def both_cores(mine, other):
        first = links.core == 0
        part = jnp.stack([jnp.where(first, mine, other), jnp.where(first, other, mine)], 1)
        return part.reshape(dp_n * qkv_rows, width)

    qkv_part = both_cores(mine, other)
    ones = links.gather_far(ones)

    def columns_of(part, shift, *blocks):
        return [(dot_nt(part, member) + shift).astype(BF) for member in blocks]

    far_place = seq_n // 2
    near_places = [r for r in range(seq_n) if r != far_place]
    near_columns = columns_of(qkv_part, qkv_shift, *ones[:far_place], *ones[1 - far_place :])
    far_rows = ones[far_place : far_place + len(ones) - seq_n + 1]
    far_columns = columns_of(after(qkv_part, near_columns), qkv_shift, jnp.concatenate(far_rows, 0))
    columns = dict(zip(near_places, near_columns)) | {far_place: far_columns[0]}
    got = links.exchange([columns[r] for r in range(seq_n)])

    def assemble(*got):
        got = [member.reshape(dp_n, qkv_rows, tok) for member in got]
        return jnp.stack(
            [
                lax.select_n(links.pos, *[got[(links.place[s] - p) % seq_n] for p in range(seq_n)])
                for s in range(seq_n)
            ],
            1,
        ).reshape(-1, tok)

    qkv = assemble(*got)
    query = qkv[:width].reshape(HEADS, HDIM, tok)
    pairs = links.gather_direct(jnp.concatenate([qkv[width:], codes], 0))
    fc_chips.append(links.z_next(after(fc_chips[1], pairs)))
    grads = links.gather_near(after(grad_low, pairs))

    spot = jnp.arange(tok, dtype=jnp.int32)

    def masked_scores(query, pairs):
        codes_all = [
            (member[2 * HDIM].astype(F32) * 128 + member[2 * HDIM + 1].astype(F32)).astype(jnp.int32)
            for member in pairs
        ]
        allowed = []
        for r in range(seq_n):
            place = links.seq_at(r)
            same = codes_all[r][:, None] == docs[None, :]
            if r == 0:
                allowed.append((same & (spot[:, None] < spot[None, :])) | (spot[:, None] == spot[None, :]))
            else:
                allowed.append(same & (place < links.seq))
        allowed = jnp.concatenate(allowed, 0)[None]
        keys = jnp.concatenate([member[:HDIM] for member in pairs], 1)
        values = jnp.concatenate([member[HDIM : 2 * HDIM] for member in pairs], 1)
        scores = jnp.einsum("dk,hdq->hkq", keys, query, preferred_element_type=F32) * scale
        return allowed, keys, values, jnp.where(allowed, scores, NEGATIVE)

    def attend(query, pairs):
        allowed, keys, values, scores = masked_scores(query, pairs)
        highest = jnp.max(scores, 1, keepdims=True)
        weights = jnp.where(allowed, jnp.exp(scores - highest), 0.0)
        total = jnp.sum(weights, 1, keepdims=True)
        attn = jnp.einsum("dk,hkq->hdq", values, weights.astype(BF), preferred_element_type=F32) / total
        return attn, highest + jnp.log(total), attn.reshape(width, tok).astype(BF).T

    attn, log_total, attn_low = attend(query, pairs)

    def norm_two(attn_low, out_full, tokens):
        flat = tokens.reshape(tok, width).astype(F32)
        middle = flat + dot_nt(attn_low, out_full) + out_shift
        normed, inverse = normalize(middle)
        return middle, normed, inverse, (normed * gain_two + shift_two).astype(BF)

    middle, normed_two, inverse_two, hidden_two = norm_two(attn_low, out_full, tokens)
    twos = links.gather_near(after(hidden_two, grads[1], grads[-1]))
    for _ in range(z_n - 3):
        fc_chips.append(links.z_next(after(fc_chips[-1], hidden_two)))
    proj_chips = [proj_weight, links.z_next(after(proj_weight, fc_chips[2], hidden_two))]

    twos = links.gather_far(after(twos, proj_chips))
    proj_chips.append(links.z_next(after(proj_chips[-1], twos[1], twos[-1])))
    fc_chips = after(fc_chips, twos[1], twos[-1])
    fc_other = links.swap_core(join_rows(fc_chips))
    grads = links.gather_far(after(grads, twos))

    pre_mine, act_mine = hidden_forward(twos, fc_chips, fc_shift[:split])
    ready = act_mine[:8, :HDIM]
    pre_other, act_other = hidden_forward(after(twos, ready, proj_chips), [fc_other], fc_shift[split:])
    for _ in range(z_n - 3):
        proj_chips.append(links.z_next(after(proj_chips[-1], ready)))
    attns = links.gather_near(after(attn_low, grads, ready))
    grads = after(grads, act_other)

    def core_terms(own, came):
        return [(own[m], came[m * units : (m + 1) * units]) for m in range(z_n)]

    (proj_sent,) = weight_terms(act_other, grads, 1)
    proj_came = links.swap_core(proj_sent)
    proj_own = weight_terms(after(act_mine, proj_sent, proj_chips, attns[1], attns[-1]), grads, z_n)
    proj_terms = core_terms(proj_own, proj_came)
    proj_chips = after(proj_chips, proj_own)
    proj_mine = join_rows(proj_chips)
    proj_other = links.swap_core(proj_mine)
    proj_sum = links.chip_sum(proj_terms, z_n - 1, None)
    proj_sum_first = proj_sum
    attns = links.gather_far(after(attns, proj_own))

    grad_mine, bias_mine = hidden_backward(grads, proj_chips, pre_mine)
    grad_other, bias_other = hidden_backward(after(grads, bias_mine, attns), [proj_other], pre_other)
    proj_sum = links.chip_sum(proj_terms, z_n - 2, proj_sum, grad_other)
    fc_bias_sum = jnp.concatenate([bias_mine, bias_other])
    hidden_parts = hidden_sum(
        (after(grad_mine, proj_sum_first), grad_other),
        [*fc_chips, fc_other],
        tok,
        links.sum_order,
        links.sum_cuts,
    )
    hidden_far = links.sum_far(after(hidden_parts, attns))
    (fc_sent,) = weight_terms(after(grad_other, hidden_parts, proj_sum), twos, 1)
    fc_came = links.swap_core(fc_sent)
    fc_own = weight_terms(after(grad_mine, fc_sent, hidden_far), twos, z_n)
    hidden_near = links.sum_near(hidden_parts, hidden_far)
    fc_terms = core_terms(after(fc_own, proj_sum), fc_came)
    for m in range(z_n - 3, 0, -1):
        proj_sum = links.chip_sum(proj_terms, m, proj_sum, hidden_parts)
    fc_sum = links.chip_sum(fc_terms, z_n - 1, None, proj_sum)
    mlp_parts = hidden_sum(
        (after(act_mine, fc_own, proj_sum), act_other), [proj_mine, proj_other], tok, tuple(range(1, seq_n)), 1
    )
    hidden_near = after(hidden_near, mlp_parts, proj_sum)

    def middle_back(parts, far, near, normed_two, inverse_two, grad_low):
        grad_hidden = links.sum_end(parts, far, near)
        grad_out = grad_low.astype(F32)
        grad_middle = grad_out + norm_back(grad_hidden * gain_two, normed_two, inverse_two)
        sums = [
            jnp.sum(grad_middle, 0),
            jnp.sum(grad_hidden * normed_two, 0),
            jnp.sum(grad_hidden, 0),
            jnp.sum(grad_out, 0),
        ]
        low = grad_middle.astype(BF)
        return grad_middle, low, low.T, sums

    grad_middle, grad_middle_low, grad_middle_turned, early = middle_back(hidden_parts[0], hidden_far, hidden_near, normed_two, inverse_two, grad_low
    )

    def to_owners(member, needed=()):
        member = member.reshape(dp_n, seq_n, -1, tok)
        sent = [
            lax.dynamic_index_in_dim(member, links.seq_at(r), 1, False).reshape(-1, tok) for r in range(seq_n)
        ]
        return links.exchange(after(sent, needed))

    mlp_came = [links.from_rel(mlp_parts[r], seq_n - r) for r in range(1, seq_n) if r != far_place]
    out_columns = to_owners(grad_middle_turned, mlp_came)
    proj_grad = links.chip_total(proj_terms, 0, after(proj_sum, grad_middle_low))

    def ordered_parts(columns, rows):
        part = dot_nn(jnp.concatenate(columns, 1), jnp.concatenate(rows, 0))
        part = part.reshape(z_n, 2, -1, width)
        sent = lax.dynamic_index_in_dim(part, 1 - links.core, 1, False).astype(BF)
        return sent, lax.dynamic_index_in_dim(part, links.core, 1, False)

    def ordered_terms(kept, came):
        kept = (kept + came.astype(F32)).astype(BF)
        return [lax.dynamic_index_in_dim(kept, links.chip_before(m), 0, False) for m in range(z_n)]

    def attend_back(out_full, grad_middle_low, query, pairs, attn, log_total):
        grad_attn = lax.dot_general(
            out_full, grad_middle_low, (((0,), (1,)), ((), ())), preferred_element_type=F32
        )
        grad_attn_low = grad_attn.astype(BF).reshape(HEADS, HDIM, tok)
        delta = jnp.sum(grad_attn_low.astype(F32) * attn, 1, keepdims=True)
        allowed, keys, values, scores = masked_scores(query, pairs)
        probs = jnp.where(allowed, jnp.exp(scores - log_total), 0.0)
        grad_probs = jnp.einsum("dk,hdq->hkq", values, grad_attn_low, preferred_element_type=F32)
        grad_scores = (probs * (grad_probs - delta)).astype(BF)
        grad_query = jnp.einsum("dk,hkq->hdq", keys, grad_scores, preferred_element_type=F32) * scale
        grad_keys = jnp.einsum("hkq,hdq->dk", grad_scores, query, preferred_element_type=F32) * scale
        grad_values = jnp.einsum("hkq,hdq->dk", probs.astype(BF), grad_attn_low, preferred_element_type=F32)
        grad_pair = jnp.concatenate([grad_keys, grad_values], 0)
        parts = [grad_pair[:, r * tok : (r + 1) * tok] for r in range(seq_n)]
        grad_query = grad_query.reshape(width, tok)
        return grad_query.astype(BF), jnp.sum(grad_query, 1), [parts[0]] + [part.astype(BF) for part in parts[1:]]

    grad_middle_low = after(grad_middle_low, fc_sum)
    grad_query, query_sum, parts = attend_back(out_full, grad_middle_low, query, pairs, attn, log_total
    )
    fc_sum = links.chip_sum(fc_terms, z_n - 2, fc_sum, grad_middle_low)
    came = links.exchange(parts)
    out_sent, out_kept = ordered_parts(after(out_columns, parts), attns)
    out_came = links.swap_core(out_sent)
    qkv_full = lax.all_gather(after(qkv_weight, got), ("dp", "seq"), axis=0, tiled=True)

    def all_grads(grad_query, came):
        grad_pair = came[0]
        for member in came[1:]:
            grad_pair = grad_pair + member.astype(F32)
        return jnp.concatenate([grad_query, grad_pair.astype(BF)], 0), jnp.sum(grad_pair[HDIM:], 1)

    grad_qkv, value_sum = all_grads(grad_query, after(came, out_sent))
    qkv_columns = to_owners(grad_qkv)
    out_terms = ordered_terms(after(out_kept, grad_qkv, fc_sum), out_came)
    for m in range(z_n - 3, 0, -1):
        fc_sum = links.chip_sum(fc_terms, m, fc_sum, parts)
    def tokens_back(grad_qkv, qkv_full, grad_middle, normed_one, inverse_one):
        grad_hidden = dot_tn(grad_qkv, qkv_full)
        back = grad_middle + norm_back(grad_hidden * gain_one, normed_one, inverse_one)
        return back.astype(BF), [jnp.sum(grad_hidden * normed_one, 0), jnp.sum(grad_hidden, 0)]

    tokens_grad, late = tokens_back(
        after(grad_qkv, out_terms), qkv_full, grad_middle, normed_one, inverse_one
    )
    out_sum = links.chip_sum(out_terms, z_n - 1, None, fc_sum)
    tokens_grad = tokens_grad.reshape(tokens.shape)
    fc_bias_sum = jnp.sum(jnp.where(owner[:, :, None], fc_bias_sum.reshape(dp_n, 1, units), 0.0), 0)
    fc_bias_sum = jnp.where(own_seq[None, :, None], fc_bias_sum[:, None, :], 0.0).reshape(-1)
    sums = jnp.concatenate(early + late + [query_sum, fc_bias_sum, value_sum])
    bit = 1
    while bit < seq_n:
        sums = sums + links.other_seq(sums, bit)
        bit *= 2
    mlp_came.append(links.from_rel(after(mlp_parts[far_place], sums), seq_n - far_place))
    sums = sums + links.other_dp(sums, 1)
    qkv_sent, qkv_kept = ordered_parts(after(qkv_columns, tokens_grad), ones)
    qkv_came = links.swap_core(after(qkv_sent, out_sum))
    for m in range(z_n - 2, 0, -1):
        out_sum = links.chip_sum(out_terms, m, out_sum)
    qkv_terms = ordered_terms(qkv_kept, qkv_came)
    qkv_sum = links.chip_sum(qkv_terms, z_n - 1, None)
    bit = 2
    for m in range(z_n - 2, 0, -1):
        moved = links.other_dp(sums, bit) if bit < dp_n else 0.0
        bit *= 2
        qkv_sum = links.chip_sum(qkv_terms, m, qkv_sum)
        sums = after(sums, qkv_sum) + moved
    while bit < dp_n:
        sums = sums + links.other_dp(sums, bit)
        bit *= 2
    fc_grad = links.chip_total(fc_terms, 0, after(fc_sum, qkv_terms))
    out_grad = links.chip_total(out_terms, 0, after(out_sum, fc_grad))
    mlp = sum(member.astype(F32) for member in [mlp_parts[0], *after(mlp_came, out_grad)])
    block_out = (middle + mlp + proj_shift).astype(BF).reshape(tokens.shape)
    qkv_grad = links.chip_total(qkv_terms, 0, after(qkv_sum, block_out))

    wide = [sums[i * width : (i + 1) * width] for i in range(7)]
    fc_bias_grad = sums[7 * width : 7 * width + fc_bias.shape[0]]
    value_bias_grad = sums[7 * width + fc_bias.shape[0] :]
    return (
        block_out,
        tokens_grad,
        wide[4],
        wide[5],
        qkv_grad,
        wide[6],
        value_bias_grad,
        out_grad,
        wide[0],
        wide[1],
        wide[2],
        fc_grad,
        fc_bias_grad,
        proj_grad,
        wide[3],
    )


def solution(mesh):
    rows = P(("dp", "seq"), None)
    act = P("dp", "seq", None)
    return jax.shard_map(
        shards,
        mesh=mesh,
        in_specs=(
            act,
            P("dp", "seq"),
            P("dp", "seq"),
            P(),
            P(),
            rows,
            P(),
            P(),
            rows,
            P(),
            P(),
            P(),
            rows,
            P(),
            rows,
            P(),
            act,
        ),
        out_specs=(
            act,
            act,
            P(),
            P(),
            rows,
            P(),
            P(),
            rows,
            P(),
            P(),
            P(),
            rows,
            P(),
            rows,
            P(),
        ),
        check_vma=False,
    )
```

```python
import jax
import jax.numpy as jnp
from jax import lax
from jax.experimental import pallas as pl
from jax.experimental.pallas import tpu as pltpu
from jax.sharding import PartitionSpec as P

HEADS = 16
HDIM = 128
EPSILON = 1e-05
NEGATIVE = -1e30
BF = jnp.bfloat16
F32 = jnp.float32


def dot_nt(left, right):
    return lax.dot_general(left, right, (((1,), (1,)), ((), ())), preferred_element_type=F32)


def dot_nn(left, right):
    return lax.dot_general(left, right, (((1,), (0,)), ((), ())), preferred_element_type=F32)


def dot_tn(left, right):
    return lax.dot_general(left, right, (((0,), (0,)), ((), ())), preferred_element_type=F32)


def normalize(values):
    center = jnp.mean(values, -1, keepdims=True)
    shifted = values - center
    inverse = lax.rsqrt(jnp.mean(shifted * shifted, -1, keepdims=True) + EPSILON)
    return (shifted * inverse, inverse)


def norm_back(grad_normed, normed, inverse):
    first_mean = jnp.mean(grad_normed, -1, keepdims=True)
    second_mean = jnp.mean(grad_normed * normed, -1, keepdims=True)
    return inverse * (grad_normed - first_mean - normed * second_mean)


def gelu_tanh(values):
    return jax.nn.gelu(values, approximate=True)


FREE = pl.CostEstimate(flops=0, bytes_accessed=0, transcendentals=0)
TILE = 256
ANY = pl.BlockSpec(memory_space=pl.ANY)


def cost(flops, arrays):
    moved = sum(leaf.size * jnp.dtype(leaf.dtype).itemsize for leaf in jax.tree.leaves(arrays))
    return pl.CostEstimate(flops=flops, bytes_accessed=moved, transcendentals=0)


def call(kernel, name, out_shape, scratch, inputs, flops=0):
    return pl.pallas_call(
        kernel,
        name=name,
        out_shape=out_shape,
        in_specs=[ANY] * len(inputs),
        out_specs=jax.tree.map(lambda _: ANY, out_shape),
        scratch_shapes=scratch,
        cost_estimate=cost(flops, (inputs, out_shape)),
        compiler_params=pltpu.CompilerParams(vmem_limit_bytes=44 * 1024 * 1024),
    )(*inputs)


def start_rows(pieces, buffer, sems):
    copies, row = [], 0
    for index, piece in enumerate(pieces):
        count = piece.shape[0]
        copy = pltpu.make_async_copy(piece, buffer.at[pl.ds(row, count)], sems.at[index])
        copy.start()
        copies.append((row, count, copy))
        row += count
    return copies


def wait_rows(copies, first, last):
    for row, _, copy in copies:
        if first <= row < last:
            copy.wait()


def join_rows(pieces):
    rows, width = sum(p.shape[0] for p in pieces), pieces[0].shape[1]

    def kernel(*refs):
        out_ref, buffer, in_sem, out_sem = refs[len(pieces) :]
        sent = []
        for index, (row, count, copy) in enumerate(start_rows(refs[: len(pieces)], buffer, in_sem)):
            copy.wait()
            part = pl.ds(row, count)
            sent.append(pltpu.make_async_copy(buffer.at[part], out_ref.at[part], out_sem.at[index]))
            sent[-1].start()
        for copy in sent:
            copy.wait()

    return call(
        kernel,
        "join_rows",
        jax.ShapeDtypeStruct((rows, width), pieces[0].dtype),
        [
            pltpu.VMEM((rows, width), pieces[0].dtype),
            pltpu.SemaphoreType.DMA((len(pieces),)),
            pltpu.SemaphoreType.DMA((len(pieces),)),
        ],
        tuple(pieces),
    )


def add_terms(members, rows, kind=BF):
    width = members[0][0].shape[1]
    step = min(rows, 64)

    def kernel(*refs):
        total = add_wide(refs[0][...], refs[1][...])
        for ref in refs[2:-1]:
            total = total + ref[...].astype(F32)
        refs[-1][...] = total.astype(kind)

    def spec(first):
        return pl.BlockSpec((step, width), lambda i: (i + first // step, 0))

    return pl.pallas_call(
        kernel,
        name="add_terms",
        grid=(rows // step,),
        out_shape=jax.ShapeDtypeStruct((rows, width), kind),
        in_specs=[spec(first) for _, first in members],
        out_specs=spec(0),
        cost_estimate=pl.CostEstimate(
            flops=0, bytes_accessed=2 * rows * width * (len(members) + 1), transcendentals=0
        ),
        compiler_params=pltpu.CompilerParams(vmem_limit_bytes=44 * 1024 * 1024),
    )(*[member for member, _ in members])


def gate(value, *needed):
    def kernel(value_ref, out_ref):
        out_ref[...] = value_ref[...]

    return pl.pallas_call(
        kernel,
        name="gate",
        out_shape=jax.ShapeDtypeStruct(value.shape, value.dtype),
        cost_estimate=FREE,
        compiler_params=pltpu.CompilerParams(vmem_limit_bytes=44 * 1024 * 1024),
    )(after(value, needed))


def row_tile(rows):
    return min(rows, 512)


def slope(values):
    inner = 0.7978845608028654 * (values + 0.044715 * values * values * values)
    curve = jnp.tanh(inner)
    return 0.5 * (1.0 + curve) + 0.5 * values * (1.0 - curve * curve) * 0.7978845608028654 * (
        1.0 + 3 * 0.044715 * values * values
    )


def hidden_forward(pieces, slots, shift):
    rows, width = sum(p.shape[0] for p in pieces), pieces[0].shape[1]
    units = sum(s.shape[0] for s in slots)
    step = row_tile(rows)

    def kernel(*refs):
        piece_refs, slot_refs = refs[: len(pieces)], refs[len(pieces) : len(pieces) + len(slots)]
        shift_hbm, pre_ref, act_ref, x, w, bias, pre_buf, act_buf, x_sem, w_sem, b_sem, out_sem = refs[
            len(pieces) + len(slots) :
        ]
        w_copies = start_rows(slot_refs, w, w_sem)
        x_copies = start_rows(piece_refs, x, x_sem)
        bias_copy = pltpu.make_async_copy(shift_hbm, bias, b_sem)
        bias_copy.start()
        bias_copy.wait()
        wait_rows(x_copies, 0, rows)
        sent = []
        for tile in range(units // TILE):
            slot = tile % 2
            columns = pl.ds(tile * TILE, TILE)
            wait_rows(w_copies, tile * TILE, (tile + 1) * TILE)
            if tile >= 2:
                for copy in sent[tile - 2]:
                    copy.wait()

            @pl.loop(0, rows // step)
            def _(index):
                part = pl.ds(index * step, step)
                pre = dot_nt(x[part], w[columns]) + bias[:, columns]
                pre_buf[slot, part] = pre
                act_buf[slot, part] = gelu_tanh(pre).astype(BF)

            sent.append(
                (
                    pltpu.make_async_copy(pre_buf.at[slot], pre_ref.at[:, columns], out_sem.at[slot, 0]),
                    pltpu.make_async_copy(act_buf.at[slot], act_ref.at[:, columns], out_sem.at[slot, 1]),
                )
            )
            for copy in sent[tile]:
                copy.start()
        for pair in sent[-2:]:
            for copy in pair:
                copy.wait()

    return call(
        kernel,
        "hidden_forward",
        (jax.ShapeDtypeStruct((rows, units), F32), jax.ShapeDtypeStruct((rows, units), BF)),
        [
            pltpu.VMEM((rows, width), BF),
            pltpu.VMEM((units, width), BF),
            pltpu.VMEM((1, units), F32),
            pltpu.VMEM((2, rows, TILE), F32),
            pltpu.VMEM((2, rows, TILE), BF),
            pltpu.SemaphoreType.DMA((len(pieces),)),
            pltpu.SemaphoreType.DMA((len(slots),)),
            pltpu.SemaphoreType.DMA,
            pltpu.SemaphoreType.DMA((2, 2)),
        ],
        (*pieces, *slots, shift.reshape(1, units)),
        2 * rows * units * width,
    )


def hidden_backward(pieces, slots, pre):
    rows, width = sum(p.shape[0] for p in pieces), pieces[0].shape[1]
    units = sum(s.shape[0] for s in slots)
    step = row_tile(rows)

    def kernel(*refs):
        piece_refs, slot_refs = refs[: len(pieces)], refs[len(pieces) : len(pieces) + len(slots)]
        pre_ref, grad_ref, sum_ref, x, w, sums, pre_buf, out_buf, x_sem, w_sem, p_sem, out_sem, s_sem = refs[
            len(pieces) + len(slots) :
        ]
        w_copies = start_rows(slot_refs, w, w_sem)
        x_copies = start_rows(piece_refs, x, x_sem)
        tiles = units // TILE

        def pre_copy(tile):
            return pltpu.make_async_copy(
                pre_ref.at[:, pl.ds(tile * TILE, TILE)], pre_buf.at[tile % 2], p_sem.at[tile % 2]
            )

        pre_copy(0).start()
        wait_rows(x_copies, 0, rows)
        sent = []
        for tile in range(tiles):
            slot = tile % 2
            columns = pl.ds(tile * TILE, TILE)
            wait_rows(w_copies, tile * TILE, (tile + 1) * TILE)
            pre_copy(tile).wait()
            if tile + 1 < tiles:
                pre_copy(tile + 1).start()
            if tile >= 2:
                sent[tile - 2].wait()
            sums[:, columns] = jnp.zeros((1, TILE), F32)

            @pl.loop(0, rows // step)
            def _(index):
                part = pl.ds(index * step, step)
                grad = dot_nt(x[part], w[columns]) * slope(pre_buf[slot, part])
                out_buf[slot, part] = grad.astype(BF)
                sums[:, columns] += jnp.sum(grad, 0, keepdims=True)

            sent.append(pltpu.make_async_copy(out_buf.at[slot], grad_ref.at[:, columns], out_sem.at[slot]))
            sent[tile].start()
        last = pltpu.make_async_copy(sums, sum_ref, s_sem)
        last.start()
        for copy in sent[-2:]:
            copy.wait()
        last.wait()

    grad, sums = call(
        kernel,
        "hidden_backward",
        (jax.ShapeDtypeStruct((rows, units), BF), jax.ShapeDtypeStruct((1, units), F32)),
        [
            pltpu.VMEM((rows, width), BF),
            pltpu.VMEM((units, width), BF),
            pltpu.VMEM((1, units), F32),
            pltpu.VMEM((2, rows, TILE), F32),
            pltpu.VMEM((2, rows, TILE), BF),
            pltpu.SemaphoreType.DMA((len(pieces),)),
            pltpu.SemaphoreType.DMA((len(slots),)),
            pltpu.SemaphoreType.DMA((2,)),
            pltpu.SemaphoreType.DMA((2,)),
            pltpu.SemaphoreType.DMA,
        ],
        (*pieces, *slots, pre),
        2 * rows * units * width,
    )
    return grad, sums.reshape(units)


def hidden_sum(lefts, slots, tok, order, cuts):
    rows = lefts[0].shape[0]
    half = lefts[0].shape[1]
    width = slots[0].shape[1]
    depth = half * len(lefts)
    wide = min(width, 1024)

    def kernel(*refs):
        left_refs, slot_refs = refs[: len(lefts)], refs[len(lefts) : len(lefts) + len(slots)]
        rest = refs[len(lefts) + len(slots) :]
        own_ref, other_refs = rest[0], rest[1 : 1 + len(order) * cuts]
        x, w, own_buf, out_buf, x_sem, w_sem, out_sem = rest[1 + len(order) * cuts :]
        x_copies = []
        for index, left in enumerate(left_refs):
            x_copies.append(pltpu.make_async_copy(left, x.at[index], x_sem.at[index]))
            x_copies[-1].start()
        w_copies = start_rows(slot_refs, w, w_sem)
        for copy in x_copies:
            copy.wait()
        wait_rows(w_copies, 0, depth)

        def product(block, columns):
            part = pl.ds(block * tok, tok)
            total = dot_nn(x[0, part], w[pl.ds(0, half), columns])
            for index in range(1, len(lefts)):
                total = total + dot_nn(x[index, part], w[pl.ds(index * half, half), columns])
            return total

        sent = []
        for count, block in enumerate(order):
            slot = count % 2
            if count >= 2:
                for copy in sent[count - 2]:
                    copy.wait()

            @pl.loop(0, width // wide)
            def _(index):
                columns = pl.ds(pl.multiple_of(index * wide, wide), wide)
                out_buf[slot, :, columns] = product(block, columns).astype(BF)

            size = tok // cuts
            sent.append(
                [
                    pltpu.make_async_copy(
                        out_buf.at[slot, pl.ds(cut * size, size)],
                        other_refs[count * cuts + cut],
                        out_sem.at[slot, cut],
                    )
                    for cut in range(cuts)
                ]
            )
            for copy in sent[count]:
                copy.start()

        @pl.loop(0, width // wide)
        def _(index):
            columns = pl.ds(pl.multiple_of(index * wide, wide), wide)
            own_buf[:, columns] = product(0, columns)

        own_copy = pltpu.make_async_copy(own_buf, own_ref, out_sem.at[2, 0])
        own_copy.start()
        for copies in sent[-2:]:
            for copy in copies:
                copy.wait()
        own_copy.wait()

    return call(
        kernel,
        "hidden_sum",
        tuple(
            [jax.ShapeDtypeStruct((tok, width), F32)]
            + [jax.ShapeDtypeStruct((tok // cuts, width), BF)] * (len(order) * cuts)
        ),
        [
            pltpu.VMEM((len(lefts), rows, half), BF),
            pltpu.VMEM((depth, width), BF),
            pltpu.VMEM((tok, width), F32),
            pltpu.VMEM((2, tok, width), BF),
            pltpu.SemaphoreType.DMA((len(lefts),)),
            pltpu.SemaphoreType.DMA((len(slots),)),
            pltpu.SemaphoreType.DMA((3, cuts)),
        ],
        (*lefts, *slots),
        2 * rows * depth * width,
    )


def weight_terms(left, pieces, slots, size):
    rows, units = left.shape
    width = pieces[0].shape[1]
    def kernel(*refs):
        left_ref, piece_refs = refs[0], refs[1 : 1 + len(pieces)]
        out_ref, l, x, out_buf, l_sem, x_sem, out_sem = refs[1 + len(pieces) :]
        l_copy = pltpu.make_async_copy(left_ref, l, l_sem)
        l_copy.start()
        x_copies = start_rows(piece_refs, x, x_sem)
        l_copy.wait()
        wait_rows(x_copies, 0, rows)
        sent = []
        wide = min(width, 1024)
        source = slots() if size == TILE else range(units // TILE)
        for tile in range(units // TILE):
            slot = tile % 2
            if tile >= 2:
                sent[tile - 2].wait()
            columns = pl.ds(pl.multiple_of(source[tile] * TILE, TILE), TILE)

            @pl.loop(0, width // wide)
            def _(index):
                span = pl.ds(pl.multiple_of(index * wide, wide), wide)
                out_buf[slot, :, span] = dot_tn(l[:, columns], x[:, span]).astype(BF)

            sent.append(
                pltpu.make_async_copy(
                    out_buf.at[slot], out_ref.at[pl.ds(tile * TILE, TILE)], out_sem.at[slot]
                )
            )
            sent[tile].start()
        for copy in sent[-2:]:
            copy.wait()

    return call(
        kernel,
        "weight_terms",
        jax.ShapeDtypeStruct((units, width), BF),
        [
            pltpu.VMEM((rows, units), BF),
            pltpu.VMEM((rows, width), BF),
            pltpu.VMEM((2, TILE, width), BF),
            pltpu.SemaphoreType.DMA,
            pltpu.SemaphoreType.DMA((len(pieces),)),
            pltpu.SemaphoreType.DMA((2,)),
        ],
        (left, *pieces),
        2 * rows * units * width,
    )


def after(value, *needed):
    return lax.optimization_barrier((value, needed))[0]


def add_wide(left, right):
    return left.astype(F32) + right.astype(F32)


def add_low(left, right):
    return add_wide(left, right).astype(BF)


class Links:
    def __init__(self):
        self.seq_n = lax.axis_size("seq")
        self.dp_n = lax.axis_size("dp")
        self.z_n = self.dp_n // 2
        half = self.seq_n // 2
        self.ring = list(range(half)) + list(range(self.seq_n - 1, half - 1, -1))
        self.seq = lax.axis_index("seq")
        dp = lax.axis_index("dp")
        self.z = dp // 2
        self.core = dp % 2
        self.chips = list(range(0, self.z_n, 2)) + list(range(self.z_n - 1, 0, -2))
        self.chip_place = [self.chips.index(z) for z in range(self.z_n)]
        self.chip_pos = jnp.where(self.z % 2 == 0, self.z // 2, self.z_n - 1 - self.z // 2)
        self.place = [self.ring.index(s) for s in range(self.seq_n)]
        self.pos = jnp.where(self.seq < half, self.seq, self.seq_n - 1 + half - self.seq)

    def seq_at(self, rel):
        n, place = self.seq_n, (self.pos + rel) % self.seq_n
        return jnp.where(place < n // 2, place, n - 1 + n // 2 - place)

    def from_rel(self, value, rel):
        n = self.seq_n
        pairs = [(self.ring[(p + rel) % n], self.ring[p]) for p in range(n)]
        return lax.ppermute(value, "seq", pairs)

    def swap_core(self, value):
        pairs = [(i, i ^ 1) for i in range(self.dp_n)]
        return lax.ppermute(value, "dp", pairs)

    def z_next(self, value):
        pairs = [(self.chips[p - 1], self.chips[p]) for p in range(self.z_n)]
        return lax.ppermute(value, "dp", [(2 * i + c, 2 * j + c) for i, j in pairs for c in range(2)])

    def z_back(self, value):
        pairs = [(self.chips[p], self.chips[p - 1]) for p in range(self.z_n)]
        return lax.ppermute(value, "dp", [(2 * i + c, 2 * j + c) for i, j in pairs for c in range(2)])

    def gather_direct(self, value):
        return [value] + [self.from_rel(value, r) for r in range(1, self.seq_n)]

    def gather_near(self, value):
        if self.seq_n != 4:
            return self.gather_direct(value)
        return [value, self.from_rel(value, 1), None, self.from_rel(value, 3)]

    def gather_far(self, blocks):
        if self.seq_n != 4:
            return blocks
        half = blocks[0].shape[0] // 2
        top = self.from_rel(blocks[1][:half], 1)
        low = self.from_rel(blocks[3][half:], 3)
        return [blocks[0], blocks[1], top, low, blocks[3]]

    def exchange(self, parts):
        n = self.seq_n
        got = [parts[0]] + [None] * (n - 1)
        for r in range(1, n):
            got[n - r] = self.from_rel(parts[r], n - r)
        return got

    @property
    def sum_order(self):
        return (2, 1, 3) if self.seq_n == 4 else tuple(range(1, self.seq_n))

    @property
    def sum_cuts(self):
        return 2 if self.seq_n == 4 else 1

    def sum_far(self, parts):
        if self.seq_n != 4:
            return self.exchange(list(parts))[1:]
        far_top, far_low, right_top, right_low, left_top, left_low = parts[1:]
        return [
            self.from_rel(far_top, 3),
            self.from_rel(far_low, 1),
            self.from_rel(right_low, 3),
            self.from_rel(left_top, 1),
        ]

    def sum_near(self, parts, far, *needed):
        if self.seq_n != 4:
            return far
        return [
            self.from_rel(after(add_low(parts[3], far[0]), needed), 3),
            self.from_rel(after(add_low(parts[6], far[1]), needed), 1),
        ]

    def sum_end(self, own, far, near):
        if self.seq_n != 4:
            for member in near:
                own = own + member.astype(F32)
            return own
        half = own.shape[0] // 2
        return jnp.concatenate(
            [
                own[:half] + add_wide(near[0], far[3]),
                own[half:] + add_wide(far[2], near[1]),
            ],
            0,
        )

    def chips_ordered(self, blocks):
        n = self.z_n
        return [
            lax.select_n(self.z, *[blocks[(self.chip_place[z] - self.chip_place[k]) % n] for z in range(n)])
            for k in range(n)
        ]

    def chip_before(self, m):
        n, place = self.z_n, (self.chip_pos - m) % self.z_n
        return jnp.where(place < (n + 1) // 2, 2 * place, 2 * (n - 1 - place) + 1)

    def other_chip(self, value, bits):
        pairs = [(2 * z + c, 2 * (z ^ bits) + c) for z in range(self.z_n) for c in range(2)]
        return lax.ppermute(value, "dp", pairs)

    def term_slots(self):
        if self.z_n != 4:
            return list(range(self.z_n))
        z = lax.axis_index("dp") // 2
        outer = (z == 0) | (z == 3)
        return [0, jnp.where(outer, 3, 1), jnp.where(outer, 1, 3), 2]

    def first_term(self, own, came, rows, *needed):
        own = after(own, needed)
        if rows % 64 == 0:
            return add_terms([(own, 2 * rows), (came, 2 * rows)], 2 * rows)
        return add_low(own[2 * rows :], came[2 * rows :])

    def first_move(self, term, *needed):
        return self.other_chip(after(term, needed), 1) if self.z_n == 4 else None

    def second_term(self, own, came, first, rows, *needed):
        own = after(own, needed)
        if self.z_n != 4:
            total = add_wide(own, came)
            moved = total[(self.z_n - 1) * rows :].astype(BF)
            for m in range(self.z_n - 2, 0, -1):
                moved = self.z_back(moved)
                moved = (total[m * rows : (m + 1) * rows] + moved.astype(F32)).astype(BF)
            return self.z_back(moved)
        if rows % 64 == 0:
            return add_terms([(own, rows), (came, rows), (first, rows)], rows)
        part = slice(rows, 2 * rows)
        return (add_wide(own[part], came[part]) + first[part].astype(F32)).astype(BF)

    def second_move(self, term, *needed):
        return self.other_chip(after(term, needed), 2) if self.z_n == 4 else term

    def chip_sum_end(self, own, came, first, second, rows, *needed):
        if rows % 64 == 0 and first is not None:
            members = [(after(own, needed), 0), (came, 0), (first, 0), (second, 0)]
            return add_terms(members, rows, F32)
        total = add_wide(own[:rows], came[:rows]) + second.astype(F32)
        return total if first is None else total + first[:rows].astype(F32)

    def other_seq(self, value, bit):
        return lax.ppermute(value, "seq", [(i, i ^ bit) for i in range(self.seq_n)])

    def other_dp(self, value, bit):
        return lax.ppermute(value, "dp", [(i, i ^ bit) for i in range(self.dp_n)])


def shards(
    tokens,
    doc_ids,
    pad_mask,
    attn_norm_gain,
    attn_norm_bias,
    qkv_weight,
    query_bias,
    value_bias,
    out_weight,
    out_bias,
    mlp_norm_gain,
    mlp_norm_bias,
    fc_weight,
    fc_bias,
    proj_weight,
    proj_bias,
    cotangent,
):
    links = Links()
    seq_n, dp_n, z_n = links.seq_n, links.dp_n, links.z_n
    tok = tokens.shape[1]
    width = tokens.shape[2]
    scale = HDIM ** (-0.5)
    gain_one = attn_norm_gain.astype(F32)
    shift_one = attn_norm_bias.astype(F32)
    out_shift = out_bias.astype(F32)
    gain_two = mlp_norm_gain.astype(F32)
    shift_two = mlp_norm_bias.astype(F32)
    proj_shift = proj_bias.astype(F32)

    docs = doc_ids[0]
    codes = jnp.where(pad_mask[0] == 1, docs, -1)
    codes = jnp.stack([codes // 128, codes % 128] + [jnp.zeros_like(codes)] * 14).astype(BF)

    units = fc_weight.shape[0]
    split = z_n * units

    block_index = jnp.arange(dp_n)
    owner = 2 * links.chip_before(block_index % z_n) + (links.core ^ (block_index // z_n))
    owner = owner[:, None] == jnp.arange(dp_n)[None, :]
    own_seq = jnp.arange(seq_n) == links.seq
    fc_shift = fc_bias.reshape(dp_n, seq_n, units).astype(F32)
    fc_shift = jnp.sum(jnp.where(own_seq[None, :, None], fc_shift, 0.0), 1)
    fc_shift = jnp.sum(jnp.where(owner[:, :, None], fc_shift[None], 0.0), 1).reshape(-1)
    qkv_rows = qkv_weight.shape[0]
    qkv_shift = jnp.concatenate(
        [query_bias.astype(F32), jnp.zeros((HDIM,), F32), value_bias.astype(F32)]
    ).reshape(dp_n, seq_n, qkv_rows)
    qkv_shift = jnp.sum(jnp.where(own_seq[None, :, None], qkv_shift, 0.0), 1).reshape(-1, 1)

    qkv_chips = [qkv_weight, links.z_next(qkv_weight)]
    grad_low = cotangent.reshape(tok, width)

    def norm_one(member):
        flat = member.reshape(tok, width).astype(F32)
        normed, inverse = normalize(flat)
        return (normed * gain_one + shift_one).astype(BF), normed, inverse

    hidden_one, normed_one, inverse_one = norm_one(tokens)
    ones = links.gather_near(after(hidden_one, qkv_chips[1]))
    qkv_chips[1] = after(qkv_chips[1], hidden_one)
    for _ in range(z_n - 2):
        qkv_chips.append(links.z_next(qkv_chips[-1]))
    fc_chips = [fc_weight, links.z_next(after(fc_weight, qkv_chips))]
    qkv_chips = after(qkv_chips, ones[1], ones[-1], qkv_shift, fc_shift)
    out_full = lax.all_gather(out_weight, ("dp", "seq"), axis=0, tiled=True)

    mine = jnp.stack(links.chips_ordered(qkv_chips), 0)
    other = links.swap_core(mine)

    def both_cores(mine, other):
        first = links.core == 0
        part = jnp.stack([jnp.where(first, mine, other), jnp.where(first, other, mine)], 1)
        return part.reshape(dp_n * qkv_rows, width)

    qkv_part = both_cores(mine, other)
    ones = links.gather_far(ones)

    def columns_of(part, shift, *blocks):
        return [(dot_nt(part, member) + shift).astype(BF) for member in blocks]

    far_place = seq_n // 2
    near_places = [r for r in range(seq_n) if r != far_place]
    near_columns = columns_of(qkv_part, qkv_shift, *ones[:far_place], *ones[1 - far_place :])
    far_rows = ones[far_place : far_place + len(ones) - seq_n + 1]
    far_columns = columns_of(after(qkv_part, near_columns), qkv_shift, jnp.concatenate(far_rows, 0))
    columns = dict(zip(near_places, near_columns)) | {far_place: far_columns[0]}
    got = links.exchange([columns[r] for r in range(seq_n)])

    def assemble(*got):
        got = [member.reshape(dp_n, qkv_rows, tok) for member in got]
        return jnp.stack(
            [
                lax.select_n(links.pos, *[got[(links.place[s] - p) % seq_n] for p in range(seq_n)])
                for s in range(seq_n)
            ],
            1,
        ).reshape(-1, tok)

    qkv = assemble(*got)
    query = qkv[:width].reshape(HEADS, HDIM, tok)
    pairs = links.gather_direct(jnp.concatenate([qkv[width:], codes], 0))
    fc_chips.append(links.z_next(after(fc_chips[1], pairs)))
    grads = links.gather_near(after(grad_low, pairs))

    spot = jnp.arange(tok, dtype=jnp.int32)

    def masked_scores(query, pairs):
        codes_all = [
            (member[2 * HDIM].astype(F32) * 128 + member[2 * HDIM + 1].astype(F32)).astype(jnp.int32)
            for member in pairs
        ]
        allowed = []
        for r in range(seq_n):
            place = links.seq_at(r)
            same = codes_all[r][:, None] == docs[None, :]
            if r == 0:
                allowed.append((same & (spot[:, None] < spot[None, :])) | (spot[:, None] == spot[None, :]))
            else:
                allowed.append(same & (place < links.seq))
        allowed = jnp.concatenate(allowed, 0)[None]
        keys = jnp.concatenate([member[:HDIM] for member in pairs], 1)
        values = jnp.concatenate([member[HDIM : 2 * HDIM] for member in pairs], 1)
        scores = jnp.einsum("dk,hdq->hkq", keys, query, preferred_element_type=F32) * scale
        return allowed, keys, values, jnp.where(allowed, scores, NEGATIVE)

    def attend(query, pairs):
        allowed, keys, values, scores = masked_scores(query, pairs)
        highest = jnp.max(scores, 1, keepdims=True)
        weights = jnp.where(allowed, jnp.exp(scores - highest), 0.0)
        total = jnp.sum(weights, 1, keepdims=True)
        attn = jnp.einsum("dk,hkq->hdq", values, weights.astype(BF), preferred_element_type=F32) / total
        return attn, highest + jnp.log(total), attn.reshape(width, tok).astype(BF).T

    attn, log_total, attn_low = attend(query, pairs)
    for _ in range(z_n - 3):
        fc_chips.append(links.z_next(after(fc_chips[-1], attn_low)))
    proj_chips = [proj_weight, links.z_next(after(proj_weight, fc_chips[2], attn_low))]

    def norm_two(attn_low, out_full, tokens):
        flat = tokens.reshape(tok, width).astype(F32)
        middle = flat + dot_nt(attn_low, out_full) + out_shift
        normed, inverse = normalize(middle)
        return middle, normed, inverse, (normed * gain_two + shift_two).astype(BF)

    middle, normed_two, inverse_two, hidden_two = norm_two(attn_low, out_full, tokens)
    twos = links.gather_near(after(hidden_two, grads[1], grads[-1]))

    twos = links.gather_far(twos)
    qkv_mine = lax.all_gather(after(mine, twos[1], twos[-1]), "seq", axis=0, tiled=True)
    qkv_mine = qkv_mine.reshape(-1, width)
    fc_chips = after(fc_chips, twos[1], twos[-1])
    fc_other = links.swap_core(join_rows(fc_chips))
    grads = links.gather_far(after(grads, twos))

    proj_chips.append(links.z_next(after(proj_chips[-1], twos)))
    pre_mine, act_mine = hidden_forward(after(twos, proj_chips[1]), fc_chips, fc_shift[:split])
    ready = act_mine[:8, :HDIM]
    pre_other, act_other = hidden_forward(after(twos, ready), [fc_other], fc_shift[split:])
    attns = links.gather_near(after(attn_low, grads, act_other))
    grads = after(grads, act_other)

    proj_sent = weight_terms(after(act_other, proj_chips[2]), grads, links.term_slots, units)
    proj_came = links.swap_core(proj_sent)
    proj_own = weight_terms(after(act_mine, proj_sent), grads, links.term_slots, units)
    for _ in range(z_n - 3):
        proj_chips.append(links.z_next(after(proj_chips[-1], act_other)))
    attns = links.gather_far(after(attns, proj_own))
    proj_term = links.first_term(proj_own, proj_came, units)
    proj_first = links.first_move(proj_term)
    proj_chips = after(proj_chips, proj_term, attns[1], attns[-1])
    proj_mine = join_rows(proj_chips)
    proj_other = links.swap_core(proj_mine)

    grad_mine, bias_mine = hidden_backward(grads, proj_chips, pre_mine)
    grad_other, bias_other = hidden_backward(after(grads, bias_mine), [proj_other], pre_other)
    fc_bias_sum = jnp.concatenate([bias_mine, bias_other])
    qkv_other = links.swap_core(after(qkv_mine, bias_mine))
    hidden_parts = hidden_sum(
        (after(grad_mine, attns), grad_other),
        [*fc_chips, fc_other],
        tok,
        links.sum_order,
        links.sum_cuts,
    )
    hidden_far = links.sum_far(after(hidden_parts, proj_first) if z_n == 4 else hidden_parts)
    proj_term = links.second_term(proj_own, proj_came, proj_first, units, hidden_parts)
    proj_second = links.second_move(proj_term)
    fc_sent = weight_terms(after(grad_other, hidden_far, proj_second), twos, links.term_slots, units)
    fc_came = links.swap_core(fc_sent)
    fc_own = weight_terms(after(grad_mine, fc_sent, hidden_far), twos, links.term_slots, units)
    hidden_near = links.sum_near(hidden_parts, hidden_far)
    fc_term = links.first_term(fc_own, fc_came, units)
    fc_first = links.first_move(fc_term)
    mlp_parts = hidden_sum(
        (after(act_mine, fc_term), act_other), [proj_mine, proj_other], tok, tuple(range(1, seq_n)), 1
    )
    mlp_came = [links.from_rel(mlp_parts[r], seq_n - r) for r in range(1, seq_n)]

    inverse_two = gate(inverse_two, mlp_parts)

    def middle_back(parts, far, near, normed_two, inverse_two, grad_low):
        grad_hidden = links.sum_end(parts, far, near)
        grad_out = grad_low.astype(F32)
        grad_middle = grad_out + norm_back(grad_hidden * gain_two, normed_two, inverse_two)
        sums = [
            jnp.sum(grad_middle, 0),
            jnp.sum(grad_hidden * normed_two, 0),
            jnp.sum(grad_hidden, 0),
            jnp.sum(grad_out, 0),
        ]
        low = grad_middle.astype(BF)
        return grad_middle, low, low.T, sums

    grad_middle, grad_middle_low, grad_middle_turned, early = middle_back(hidden_parts[0], hidden_far, hidden_near, normed_two, inverse_two, grad_low
    )

    def to_owners(member, needed=()):
        member = member.reshape(dp_n, seq_n, -1, tok)
        sent = [
            lax.dynamic_index_in_dim(member, links.seq_at(r), 1, False).reshape(-1, tok) for r in range(seq_n)
        ]
        return links.exchange(after(sent, needed))


    def ordered_parts(columns, rows):
        part = dot_nn(jnp.concatenate(columns, 1), jnp.concatenate(rows, 0))
        part = part.reshape(z_n, 2, -1, width)
        sent = lax.dynamic_index_in_dim(part, 1 - links.core, 1, False).astype(BF)
        return sent, lax.dynamic_index_in_dim(part, links.core, 1, False)

    def ordered_terms(kept, came):
        order = [links.z ^ k for k in (0, 2, 1, 3)] if z_n == 4 else [links.chip_before(m) for m in range(z_n)]
        return [
            jnp.concatenate([lax.dynamic_index_in_dim(member, k, 0, False) for k in order], 0)
            for member in (kept.astype(BF), came)
        ]

    def attend_back(out_full, grad_middle_low, query, pairs, attn, log_total):
        grad_attn = lax.dot_general(
            out_full, grad_middle_low, (((0,), (1,)), ((), ())), preferred_element_type=F32
        )
        grad_attn_low = grad_attn.astype(BF).reshape(HEADS, HDIM, tok)
        delta = jnp.sum(grad_attn_low.astype(F32) * attn, 1, keepdims=True)
        allowed, keys, values, scores = masked_scores(query, pairs)
        probs = jnp.where(allowed, jnp.exp(scores - log_total), 0.0)
        grad_probs = jnp.einsum("dk,hdq->hkq", values, grad_attn_low, preferred_element_type=F32)
        grad_scores = (probs * (grad_probs - delta)).astype(BF)
        grad_query = jnp.einsum("dk,hkq->hdq", keys, grad_scores, preferred_element_type=F32) * scale
        grad_keys = jnp.einsum("hkq,hdq->dk", grad_scores, query, preferred_element_type=F32) * scale
        grad_values = jnp.einsum("hkq,hdq->dk", probs.astype(BF), grad_attn_low, preferred_element_type=F32)
        grad_pair = jnp.concatenate([grad_keys, grad_values], 0)
        parts = [grad_pair[:, r * tok : (r + 1) * tok] for r in range(seq_n)]
        grad_query = grad_query.reshape(width, tok)
        return grad_query.astype(BF), jnp.sum(grad_query, 1), [parts[0]] + [part.astype(BF) for part in parts[1:]]

    log_total = gate(log_total, fc_first, grad_middle_low)
    grad_query, query_sum, parts = attend_back(out_full, grad_middle_low, query, pairs, attn, log_total
    )
    came = links.exchange(after(parts, mlp_came))
    fc_second = links.second_move(links.second_term(fc_own, fc_came, fc_first, units, parts))
    out_columns = to_owners(grad_middle_turned, came)
    out_sent, out_kept = ordered_parts(after(out_columns, parts), attns)
    out_came = links.swap_core(out_sent)

    def all_grads(grad_query, came):
        grad_pair = came[0]
        for member in came[1:]:
            grad_pair = grad_pair + member.astype(F32)
        return jnp.concatenate([grad_query, grad_pair.astype(BF)], 0), jnp.sum(grad_pair[HDIM:], 1)

    grad_qkv, value_sum = all_grads(grad_query, came)
    qkv_columns = to_owners(grad_qkv)
    out_rows = out_weight.shape[0]
    out_own, out_came = ordered_terms(out_kept, out_came)
    def tokens_back(grad_qkv, qkv_mine, qkv_other, grad_middle, normed_one, inverse_one):
        by_core = grad_qkv.reshape(z_n, 2, seq_n, qkv_rows, tok)

        def rows_of(core):
            rows = lax.dynamic_index_in_dim(by_core, core, 1, False)
            return rows.transpose(1, 0, 2, 3).reshape(-1, tok)

        grad_hidden = dot_tn(rows_of(links.core), qkv_mine) + dot_tn(rows_of(1 - links.core), qkv_other)
        back = grad_middle + norm_back(grad_hidden * gain_one, normed_one, inverse_one)
        return back.astype(BF), [jnp.sum(grad_hidden * normed_one, 0), jnp.sum(grad_hidden, 0)]

    tokens_grad, late = tokens_back(
        grad_qkv, qkv_mine, qkv_other, grad_middle, normed_one, inverse_one
    )
    out_first = links.first_move(links.first_term(out_own, out_came, out_rows))
    tokens_grad = tokens_grad.reshape(tokens.shape)
    fc_bias_sum = jnp.sum(jnp.where(owner[:, :, None], fc_bias_sum.reshape(dp_n, 1, units), 0.0), 0)
    fc_bias_sum = jnp.where(own_seq[None, :, None], fc_bias_sum[:, None, :], 0.0).reshape(-1)
    sums = jnp.concatenate(early + late + [query_sum, fc_bias_sum, value_sum])
    bit = 1
    while bit < seq_n:
        sums = sums + links.other_seq(sums, bit)
        bit *= 2
    sums = sums + links.other_dp(sums, 1)
    qkv_sent, qkv_kept = ordered_parts(after(qkv_columns, tokens_grad), ones)
    qkv_came = links.swap_core(qkv_sent)
    qkv_own, qkv_came = ordered_terms(qkv_kept, qkv_came)
    out_second = links.second_move(links.second_term(out_own, out_came, out_first, out_rows))
    qkv_first = links.first_move(links.first_term(qkv_own, qkv_came, qkv_rows), fc_second)
    bit = 2
    moved = links.other_dp(sums, bit)
    qkv_second = links.second_move(links.second_term(qkv_own, qkv_came, qkv_first, qkv_rows))
    sums = after(sums, qkv_second) + moved
    bit *= 2
    while bit < dp_n:
        sums = sums + links.other_dp(sums, bit)
        bit *= 2
    proj_grad = links.chip_sum_end(proj_own, proj_came, proj_first, proj_second, units, qkv_own)
    fc_grad = links.chip_sum_end(fc_own, fc_came, fc_first, fc_second, units, qkv_own)
    out_grad = links.chip_sum_end(out_own, out_came, out_first, out_second, out_rows)
    mlp = sum(member.astype(F32) for member in [mlp_parts[0], *after(mlp_came, fc_grad)])
    block_out = (middle + mlp + proj_shift).astype(BF).reshape(tokens.shape)
    qkv_grad = links.chip_sum_end(qkv_own, qkv_came, qkv_first, qkv_second, qkv_rows)

    wide = [sums[i * width : (i + 1) * width] for i in range(7)]
    fc_bias_grad = sums[7 * width : 7 * width + fc_bias.shape[0]]
    value_bias_grad = sums[7 * width + fc_bias.shape[0] :]
    return (
        block_out,
        tokens_grad,
        wide[4],
        wide[5],
        qkv_grad,
        wide[6],
        value_bias_grad,
        out_grad,
        wide[0],
        wide[1],
        wide[2],
        fc_grad,
        fc_bias_grad,
        proj_grad,
        wide[3],
    )


def solution(mesh):
    rows = P(("dp", "seq"), None)
    act = P("dp", "seq", None)
    return jax.shard_map(
        shards,
        mesh=mesh,
        in_specs=(
            act,
            P("dp", "seq"),
            P("dp", "seq"),
            P(),
            P(),
            rows,
            P(),
            P(),
            rows,
            P(),
            P(),
            P(),
            rows,
            P(),
            rows,
            P(),
            act,
        ),
        out_specs=(
            act,
            act,
            P(),
            P(),
            rows,
            P(),
            P(),
            rows,
            P(),
            P(),
            P(),
            rows,
            P(),
            rows,
            P(),
        ),
        check_vma=False,
    )
```

```python
import jax
import jax.numpy as jnp
from jax import lax
from jax.experimental import pallas as pl
from jax.experimental.pallas import tpu as pltpu
from jax.sharding import PartitionSpec as P

HEADS = 16
HDIM = 128
EPSILON = 1e-05
NEGATIVE = -1e30
BF = jnp.bfloat16
F32 = jnp.float32


def dot_nt(left, right):
    return lax.dot_general(left, right, (((1,), (1,)), ((), ())), preferred_element_type=F32)


def dot_nn(left, right):
    return lax.dot_general(left, right, (((1,), (0,)), ((), ())), preferred_element_type=F32)


def dot_tn(left, right):
    return lax.dot_general(left, right, (((0,), (0,)), ((), ())), preferred_element_type=F32)


def normalize(values):
    center = jnp.mean(values, -1, keepdims=True)
    shifted = values - center
    inverse = lax.rsqrt(jnp.mean(shifted * shifted, -1, keepdims=True) + EPSILON)
    return (shifted * inverse, inverse)


def norm_back(grad_normed, normed, inverse):
    first_mean = jnp.mean(grad_normed, -1, keepdims=True)
    second_mean = jnp.mean(grad_normed * normed, -1, keepdims=True)
    return inverse * (grad_normed - first_mean - normed * second_mean)


def gelu_tanh(values):
    return jax.nn.gelu(values, approximate=True)


FREE = pl.CostEstimate(flops=0, bytes_accessed=0, transcendentals=0)
TILE = 256
ANY = pl.BlockSpec(memory_space=pl.ANY)


def cost(flops, arrays):
    moved = sum(leaf.size * jnp.dtype(leaf.dtype).itemsize for leaf in jax.tree.leaves(arrays))
    return pl.CostEstimate(flops=flops, bytes_accessed=moved, transcendentals=0)


def call(kernel, name, out_shape, scratch, inputs, flops=None):
    estimate = cost(flops or 0, () if flops == 0 else (inputs, out_shape))
    return pl.pallas_call(
        kernel,
        name=name,
        out_shape=out_shape,
        in_specs=[ANY] * len(inputs),
        out_specs=jax.tree.map(lambda _: ANY, out_shape),
        scratch_shapes=scratch,
        cost_estimate=estimate,
        compiler_params=pltpu.CompilerParams(vmem_limit_bytes=44 * 1024 * 1024),
    )(*inputs)


def start_rows(pieces, buffer, sems):
    copies, row = [], 0
    for index, piece in enumerate(pieces):
        count = piece.shape[0]
        copy = pltpu.make_async_copy(piece, buffer.at[pl.ds(row, count)], sems.at[index])
        copy.start()
        copies.append((row, count, copy))
        row += count
    return copies


def wait_rows(copies, first, last):
    for row, _, copy in copies:
        if first <= row < last:
            copy.wait()


def join_rows(pieces):
    rows, width = sum(p.shape[0] for p in pieces), pieces[0].shape[1]

    def kernel(*refs):
        out_ref, buffer, in_sem, out_sem = refs[len(pieces) :]
        sent = []
        for index, (row, count, copy) in enumerate(start_rows(refs[: len(pieces)], buffer, in_sem)):
            copy.wait()
            part = pl.ds(row, count)
            sent.append(pltpu.make_async_copy(buffer.at[part], out_ref.at[part], out_sem.at[index]))
            sent[-1].start()
        for copy in sent:
            copy.wait()

    return call(
        kernel,
        "join_rows",
        jax.ShapeDtypeStruct((rows, width), pieces[0].dtype),
        [
            pltpu.VMEM((rows, width), pieces[0].dtype),
            pltpu.SemaphoreType.DMA((len(pieces),)),
            pltpu.SemaphoreType.DMA((len(pieces),)),
        ],
        tuple(pieces),
    )


def add_terms(members, rows, kind=BF):
    width = members[0][0].shape[1]
    step = min(rows, 64)

    def kernel(*refs):
        total = add_wide(refs[0][...], refs[1][...])
        for ref in refs[2:-1]:
            total = total + ref[...].astype(F32)
        refs[-1][...] = total.astype(kind)

    def spec(first):
        return pl.BlockSpec((step, width), lambda i: (i + first // step, 0))

    return pl.pallas_call(
        kernel,
        name="add_terms",
        grid=(rows // step,),
        out_shape=jax.ShapeDtypeStruct((rows, width), kind),
        in_specs=[spec(first) for _, first in members],
        out_specs=spec(0),
        cost_estimate=pl.CostEstimate(
            flops=0, bytes_accessed=2 * rows * width * (len(members) + 1), transcendentals=0
        ),
        compiler_params=pltpu.CompilerParams(vmem_limit_bytes=44 * 1024 * 1024),
    )(*[member for member, _ in members])


def gate(value, *needed):
    def kernel(value_ref, out_ref):
        out_ref[...] = value_ref[...]

    return pl.pallas_call(
        kernel,
        name="gate",
        out_shape=jax.ShapeDtypeStruct(value.shape, value.dtype),
        cost_estimate=FREE,
        compiler_params=pltpu.CompilerParams(vmem_limit_bytes=44 * 1024 * 1024),
    )(after(value, needed))


def row_tile(rows):
    return min(rows, 512)


def slope(values):
    inner = 0.7978845608028654 * (values + 0.044715 * values * values * values)
    curve = jnp.tanh(inner)
    return 0.5 * (1.0 + curve) + 0.5 * values * (1.0 - curve * curve) * 0.7978845608028654 * (
        1.0 + 3 * 0.044715 * values * values
    )


def hidden_forward(pieces, slots, shift):
    rows, width = sum(p.shape[0] for p in pieces), pieces[0].shape[1]
    units = sum(s.shape[0] for s in slots)
    step = row_tile(rows)

    def kernel(*refs):
        piece_refs, slot_refs = refs[: len(pieces)], refs[len(pieces) : len(pieces) + len(slots)]
        shift_hbm, pre_ref, act_ref, x, w, bias, pre_buf, act_buf, x_sem, w_sem, b_sem, out_sem = refs[
            len(pieces) + len(slots) :
        ]
        w_copies = start_rows(slot_refs, w, w_sem)
        x_copies = start_rows(piece_refs, x, x_sem)
        bias_copy = pltpu.make_async_copy(shift_hbm, bias, b_sem)
        bias_copy.start()
        bias_copy.wait()
        wait_rows(x_copies, 0, rows)
        sent = []
        for tile in range(units // TILE):
            slot = tile % 2
            columns = pl.ds(tile * TILE, TILE)
            wait_rows(w_copies, tile * TILE, (tile + 1) * TILE)
            if tile >= 2:
                for copy in sent[tile - 2]:
                    copy.wait()

            @pl.loop(0, rows // step)
            def _(index):
                part = pl.ds(index * step, step)
                pre = dot_nt(x[part], w[columns]) + bias[:, columns]
                pre_buf[slot, part] = pre
                act_buf[slot, part] = gelu_tanh(pre).astype(BF)

            sent.append(
                (
                    pltpu.make_async_copy(pre_buf.at[slot], pre_ref.at[:, columns], out_sem.at[slot, 0]),
                    pltpu.make_async_copy(act_buf.at[slot], act_ref.at[:, columns], out_sem.at[slot, 1]),
                )
            )
            for copy in sent[tile]:
                copy.start()
        for pair in sent[-2:]:
            for copy in pair:
                copy.wait()

    return call(
        kernel,
        "hidden_forward",
        (jax.ShapeDtypeStruct((rows, units), F32), jax.ShapeDtypeStruct((rows, units), BF)),
        [
            pltpu.VMEM((rows, width), BF),
            pltpu.VMEM((units, width), BF),
            pltpu.VMEM((1, units), F32),
            pltpu.VMEM((2, rows, TILE), F32),
            pltpu.VMEM((2, rows, TILE), BF),
            pltpu.SemaphoreType.DMA((len(pieces),)),
            pltpu.SemaphoreType.DMA((len(slots),)),
            pltpu.SemaphoreType.DMA,
            pltpu.SemaphoreType.DMA((2, 2)),
        ],
        (*pieces, *slots, shift.reshape(1, units)),
        2 * rows * units * width,
    )


def hidden_backward(pieces, slots, pre):
    rows, width = sum(p.shape[0] for p in pieces), pieces[0].shape[1]
    units = sum(s.shape[0] for s in slots)
    step = row_tile(rows)

    def kernel(*refs):
        piece_refs, slot_refs = refs[: len(pieces)], refs[len(pieces) : len(pieces) + len(slots)]
        pre_ref, grad_ref, sum_ref, x, w, sums, pre_buf, out_buf, x_sem, w_sem, p_sem, out_sem, s_sem = refs[
            len(pieces) + len(slots) :
        ]
        w_copies = start_rows(slot_refs, w, w_sem)
        x_copies = start_rows(piece_refs, x, x_sem)
        tiles = units // TILE

        def pre_copy(tile):
            return pltpu.make_async_copy(
                pre_ref.at[:, pl.ds(tile * TILE, TILE)], pre_buf.at[tile % 2], p_sem.at[tile % 2]
            )

        pre_copy(0).start()
        wait_rows(x_copies, 0, rows)
        sent = []
        for tile in range(tiles):
            slot = tile % 2
            columns = pl.ds(tile * TILE, TILE)
            wait_rows(w_copies, tile * TILE, (tile + 1) * TILE)
            pre_copy(tile).wait()
            if tile + 1 < tiles:
                pre_copy(tile + 1).start()
            if tile >= 2:
                sent[tile - 2].wait()
            sums[:, columns] = jnp.zeros((1, TILE), F32)

            @pl.loop(0, rows // step)
            def _(index):
                part = pl.ds(index * step, step)
                grad = dot_nt(x[part], w[columns]) * slope(pre_buf[slot, part])
                out_buf[slot, part] = grad.astype(BF)
                sums[:, columns] += jnp.sum(grad, 0, keepdims=True)

            sent.append(pltpu.make_async_copy(out_buf.at[slot], grad_ref.at[:, columns], out_sem.at[slot]))
            sent[tile].start()
        last = pltpu.make_async_copy(sums, sum_ref, s_sem)
        last.start()
        for copy in sent[-2:]:
            copy.wait()
        last.wait()

    grad, sums = call(
        kernel,
        "hidden_backward",
        (jax.ShapeDtypeStruct((rows, units), BF), jax.ShapeDtypeStruct((1, units), F32)),
        [
            pltpu.VMEM((rows, width), BF),
            pltpu.VMEM((units, width), BF),
            pltpu.VMEM((1, units), F32),
            pltpu.VMEM((2, rows, TILE), F32),
            pltpu.VMEM((2, rows, TILE), BF),
            pltpu.SemaphoreType.DMA((len(pieces),)),
            pltpu.SemaphoreType.DMA((len(slots),)),
            pltpu.SemaphoreType.DMA((2,)),
            pltpu.SemaphoreType.DMA((2,)),
            pltpu.SemaphoreType.DMA,
        ],
        (*pieces, *slots, pre),
        2 * rows * units * width,
    )
    return grad, sums.reshape(units)


def hidden_sum(lefts, slots, tok, order, cuts, flops):
    rows = lefts[0].shape[0]
    half = lefts[0].shape[1]
    width = slots[0].shape[1]
    depth = half * len(lefts)
    wide = min(width, 1024)

    def kernel(*refs):
        left_refs, slot_refs = refs[: len(lefts)], refs[len(lefts) : len(lefts) + len(slots)]
        rest = refs[len(lefts) + len(slots) :]
        own_ref, other_refs = rest[0], rest[1 : 1 + len(order) * cuts]
        x, w, own_buf, out_buf, x_sem, w_sem, out_sem = rest[1 + len(order) * cuts :]
        x_copies = []
        for index, left in enumerate(left_refs):
            x_copies.append(pltpu.make_async_copy(left, x.at[index], x_sem.at[index]))
            x_copies[-1].start()
        w_copies = start_rows(slot_refs, w, w_sem)
        for copy in x_copies:
            copy.wait()
        wait_rows(w_copies, 0, depth)

        def product(block, columns):
            part = pl.ds(block * tok, tok)
            total = dot_nn(x[0, part], w[pl.ds(0, half), columns])
            for index in range(1, len(lefts)):
                total = total + dot_nn(x[index, part], w[pl.ds(index * half, half), columns])
            return total

        sent = []
        for count, block in enumerate(order):
            slot = count % 2
            if count >= 2:
                for copy in sent[count - 2]:
                    copy.wait()

            @pl.loop(0, width // wide)
            def _(index):
                columns = pl.ds(pl.multiple_of(index * wide, wide), wide)
                out_buf[slot, :, columns] = product(block, columns).astype(BF)

            size = tok // cuts
            sent.append(
                [
                    pltpu.make_async_copy(
                        out_buf.at[slot, pl.ds(cut * size, size)],
                        other_refs[count * cuts + cut],
                        out_sem.at[slot, cut],
                    )
                    for cut in range(cuts)
                ]
            )
            for copy in sent[count]:
                copy.start()

        @pl.loop(0, width // wide)
        def _(index):
            columns = pl.ds(pl.multiple_of(index * wide, wide), wide)
            own_buf[:, columns] = product(0, columns)

        own_copy = pltpu.make_async_copy(own_buf, own_ref, out_sem.at[2, 0])
        own_copy.start()
        for copies in sent[-2:]:
            for copy in copies:
                copy.wait()
        own_copy.wait()

    return call(
        kernel,
        "hidden_sum",
        tuple(
            [jax.ShapeDtypeStruct((tok, width), F32)]
            + [jax.ShapeDtypeStruct((tok // cuts, width), BF)] * (len(order) * cuts)
        ),
        [
            pltpu.VMEM((len(lefts), rows, half), BF),
            pltpu.VMEM((depth, width), BF),
            pltpu.VMEM((tok, width), F32),
            pltpu.VMEM((2, tok, width), BF),
            pltpu.SemaphoreType.DMA((len(lefts),)),
            pltpu.SemaphoreType.DMA((len(slots),)),
            pltpu.SemaphoreType.DMA((3, cuts)),
        ],
        (*lefts, *slots),
        flops,
    )


def weight_terms(left, pieces, slots, size):
    rows, units = left.shape
    width = pieces[0].shape[1]
    def kernel(*refs):
        left_ref, piece_refs = refs[0], refs[1 : 1 + len(pieces)]
        out_ref, l, x, out_buf, l_sem, x_sem, out_sem = refs[1 + len(pieces) :]
        l_copy = pltpu.make_async_copy(left_ref, l, l_sem)
        l_copy.start()
        x_copies = start_rows(piece_refs, x, x_sem)
        l_copy.wait()
        wait_rows(x_copies, 0, rows)
        sent = []
        wide = min(width, 1024)
        source = slots() if size == TILE else range(units // TILE)
        for tile in range(units // TILE):
            slot = tile % 2
            if tile >= 2:
                sent[tile - 2].wait()
            columns = pl.ds(pl.multiple_of(source[tile] * TILE, TILE), TILE)

            @pl.loop(0, width // wide)
            def _(index):
                span = pl.ds(pl.multiple_of(index * wide, wide), wide)
                out_buf[slot, :, span] = dot_tn(l[:, columns], x[:, span]).astype(BF)

            sent.append(
                pltpu.make_async_copy(
                    out_buf.at[slot], out_ref.at[pl.ds(tile * TILE, TILE)], out_sem.at[slot]
                )
            )
            sent[tile].start()
        for copy in sent[-2:]:
            copy.wait()

    return call(
        kernel,
        "weight_terms",
        jax.ShapeDtypeStruct((units, width), BF),
        [
            pltpu.VMEM((rows, units), BF),
            pltpu.VMEM((rows, width), BF),
            pltpu.VMEM((2, TILE, width), BF),
            pltpu.SemaphoreType.DMA,
            pltpu.SemaphoreType.DMA((len(pieces),)),
            pltpu.SemaphoreType.DMA((2,)),
        ],
        (left, *pieces),
        2 * rows * units * width,
    )


def after(value, *needed):
    return lax.optimization_barrier((value, needed))[0]


def add_wide(left, right):
    return left.astype(F32) + right.astype(F32)


def add_low(left, right):
    return add_wide(left, right).astype(BF)


class Links:
    def __init__(self):
        self.seq_n = lax.axis_size("seq")
        self.dp_n = lax.axis_size("dp")
        self.z_n = self.dp_n // 2
        half = self.seq_n // 2
        self.ring = list(range(half)) + list(range(self.seq_n - 1, half - 1, -1))
        self.seq = lax.axis_index("seq")
        dp = lax.axis_index("dp")
        self.z = dp // 2
        self.core = dp % 2
        self.chips = list(range(0, self.z_n, 2)) + list(range(self.z_n - 1, 0, -2))
        self.chip_place = [self.chips.index(z) for z in range(self.z_n)]
        self.chip_pos = jnp.where(self.z % 2 == 0, self.z // 2, self.z_n - 1 - self.z // 2)
        self.place = [self.ring.index(s) for s in range(self.seq_n)]
        self.pos = jnp.where(self.seq < half, self.seq, self.seq_n - 1 + half - self.seq)

    def seq_at(self, rel):
        n, place = self.seq_n, (self.pos + rel) % self.seq_n
        return jnp.where(place < n // 2, place, n - 1 + n // 2 - place)

    def from_rel(self, value, rel):
        n = self.seq_n
        pairs = [(self.ring[(p + rel) % n], self.ring[p]) for p in range(n)]
        return lax.ppermute(value, "seq", pairs)

    def swap_core(self, value):
        pairs = [(i, i ^ 1) for i in range(self.dp_n)]
        return lax.ppermute(value, "dp", pairs)

    def z_next(self, value):
        pairs = [(self.chips[p - 1], self.chips[p]) for p in range(self.z_n)]
        return lax.ppermute(value, "dp", [(2 * i + c, 2 * j + c) for i, j in pairs for c in range(2)])

    def z_back(self, value):
        pairs = [(self.chips[p], self.chips[p - 1]) for p in range(self.z_n)]
        return lax.ppermute(value, "dp", [(2 * i + c, 2 * j + c) for i, j in pairs for c in range(2)])

    def gather_direct(self, value):
        return [value] + [self.from_rel(value, r) for r in range(1, self.seq_n)]

    def gather_near(self, value):
        if self.seq_n != 4:
            return self.gather_direct(value)
        return [value, self.from_rel(value, 1), None, self.from_rel(value, 3)]

    def gather_far(self, blocks):
        if self.seq_n != 4:
            return blocks
        half = blocks[0].shape[0] // 2
        top = self.from_rel(blocks[1][:half], 1)
        low = self.from_rel(blocks[3][half:], 3)
        return [blocks[0], blocks[1], top, low, blocks[3]]

    def exchange(self, parts):
        n = self.seq_n
        got = [parts[0]] + [None] * (n - 1)
        for r in range(1, n):
            got[n - r] = self.from_rel(parts[r], n - r)
        return got

    @property
    def sum_order(self):
        return (2, 1, 3) if self.seq_n == 4 else tuple(range(1, self.seq_n))

    @property
    def sum_cuts(self):
        return 2 if self.seq_n == 4 else 1

    def sum_far(self, parts):
        if self.seq_n != 4:
            return self.exchange(list(parts))[1:]
        far_top, far_low, right_top, right_low, left_top, left_low = parts[1:]
        return [
            self.from_rel(far_top, 3),
            self.from_rel(far_low, 1),
            self.from_rel(right_low, 3),
            self.from_rel(left_top, 1),
        ]

    def sum_near(self, parts, far, *needed):
        if self.seq_n != 4:
            return far
        return [
            self.from_rel(after(add_low(parts[3], far[0]), needed), 3),
            self.from_rel(after(add_low(parts[6], far[1]), needed), 1),
        ]

    def sum_end(self, own, far, near):
        if self.seq_n != 4:
            for member in near:
                own = own + member.astype(F32)
            return own
        half = own.shape[0] // 2
        return jnp.concatenate(
            [
                own[:half] + add_wide(near[0], far[3]),
                own[half:] + add_wide(far[2], near[1]),
            ],
            0,
        )

    def chips_ordered(self, blocks):
        n = self.z_n
        return [
            lax.select_n(self.z, *[blocks[(self.chip_place[z] - self.chip_place[k]) % n] for z in range(n)])
            for k in range(n)
        ]

    def chip_before(self, m):
        n, place = self.z_n, (self.chip_pos - m) % self.z_n
        return jnp.where(place < (n + 1) // 2, 2 * place, 2 * (n - 1 - place) + 1)

    def other_chip(self, value, bits):
        pairs = [(2 * z + c, 2 * (z ^ bits) + c) for z in range(self.z_n) for c in range(2)]
        return lax.ppermute(value, "dp", pairs)

    def term_slots(self):
        if self.z_n != 4:
            return list(range(self.z_n))
        z = lax.axis_index("dp") // 2
        outer = (z == 0) | (z == 3)
        return [0, jnp.where(outer, 3, 1), jnp.where(outer, 1, 3), 2]

    def first_term(self, own, came, rows, *needed):
        own = after(own, needed)
        if rows % 64 == 0:
            return add_terms([(own, 2 * rows), (came, 2 * rows)], 2 * rows)
        return add_low(own[2 * rows :], came[2 * rows :])

    def first_move(self, term, *needed):
        return self.other_chip(after(term, needed), 1) if self.z_n == 4 else None

    def second_term(self, own, came, first, rows, *needed):
        own = after(own, needed)
        if self.z_n != 4:
            total = add_wide(own, came)
            moved = total[(self.z_n - 1) * rows :].astype(BF)
            for m in range(self.z_n - 2, 0, -1):
                moved = self.z_back(moved)
                moved = (total[m * rows : (m + 1) * rows] + moved.astype(F32)).astype(BF)
            return self.z_back(moved)
        if rows % 64 == 0:
            return add_terms([(own, rows), (came, rows), (first, rows)], rows)
        part = slice(rows, 2 * rows)
        return (add_wide(own[part], came[part]) + first[part].astype(F32)).astype(BF)

    def second_move(self, term, *needed):
        return self.other_chip(after(term, needed), 2) if self.z_n == 4 else term

    def chip_sum_end(self, own, came, first, second, rows, *needed):
        if rows % 64 == 0 and first is not None:
            members = [(after(own, needed), 0), (came, 0), (first, 0), (second, 0)]
            return add_terms(members, rows, F32)
        total = add_wide(own[:rows], came[:rows]) + second.astype(F32)
        return total if first is None else total + first[:rows].astype(F32)

    def other_seq(self, value, bit):
        return lax.ppermute(value, "seq", [(i, i ^ bit) for i in range(self.seq_n)])

    def other_dp(self, value, bit):
        return lax.ppermute(value, "dp", [(i, i ^ bit) for i in range(self.dp_n)])


def shards(
    tokens,
    doc_ids,
    pad_mask,
    attn_norm_gain,
    attn_norm_bias,
    qkv_weight,
    query_bias,
    value_bias,
    out_weight,
    out_bias,
    mlp_norm_gain,
    mlp_norm_bias,
    fc_weight,
    fc_bias,
    proj_weight,
    proj_bias,
    cotangent,
):
    links = Links()
    seq_n, dp_n, z_n = links.seq_n, links.dp_n, links.z_n
    tok = tokens.shape[1]
    width = tokens.shape[2]
    scale = HDIM ** (-0.5)
    gain_one = attn_norm_gain.astype(F32)
    shift_one = attn_norm_bias.astype(F32)
    out_shift = out_bias.astype(F32)
    gain_two = mlp_norm_gain.astype(F32)
    shift_two = mlp_norm_bias.astype(F32)
    proj_shift = proj_bias.astype(F32)

    docs = doc_ids[0]
    codes = jnp.where(pad_mask[0] == 1, docs, -1)
    codes = jnp.stack([codes // 128, codes % 128] + [jnp.zeros_like(codes)] * 14).astype(BF)

    units = fc_weight.shape[0]
    split = z_n * units

    block_index = jnp.arange(dp_n)
    owner = 2 * links.chip_before(block_index % z_n) + (links.core ^ (block_index // z_n))
    owner = owner[:, None] == jnp.arange(dp_n)[None, :]
    own_seq = jnp.arange(seq_n) == links.seq
    fc_shift = fc_bias.reshape(dp_n, seq_n, units).astype(F32)
    fc_shift = jnp.sum(jnp.where(own_seq[None, :, None], fc_shift, 0.0), 1)
    fc_shift = jnp.sum(jnp.where(owner[:, :, None], fc_shift[None], 0.0), 1).reshape(-1)
    qkv_rows = qkv_weight.shape[0]
    qkv_shift = jnp.concatenate(
        [query_bias.astype(F32), jnp.zeros((HDIM,), F32), value_bias.astype(F32)]
    ).reshape(dp_n, seq_n, qkv_rows)
    qkv_shift = jnp.sum(jnp.where(own_seq[None, :, None], qkv_shift, 0.0), 1).reshape(-1, 1)

    qkv_chips = [qkv_weight, links.z_next(qkv_weight)]
    grad_low = cotangent.reshape(tok, width)

    def norm_one(member):
        flat = member.reshape(tok, width).astype(F32)
        normed, inverse = normalize(flat)
        return (normed * gain_one + shift_one).astype(BF), normed, inverse

    hidden_one, normed_one, inverse_one = norm_one(tokens)
    ones = links.gather_near(after(hidden_one, qkv_chips[1]))
    qkv_chips[1] = after(qkv_chips[1], hidden_one)
    for _ in range(z_n - 2):
        qkv_chips.append(links.z_next(qkv_chips[-1]))
    fc_chips = [fc_weight, links.z_next(after(fc_weight, qkv_chips))]
    qkv_chips = after(qkv_chips, ones[1], ones[-1], qkv_shift, fc_shift)
    out_full = lax.all_gather(out_weight, ("dp", "seq"), axis=0, tiled=True)

    mine = jnp.stack(links.chips_ordered(qkv_chips), 0)
    other = links.swap_core(mine)

    def both_cores(mine, other):
        first = links.core == 0
        part = jnp.stack([jnp.where(first, mine, other), jnp.where(first, other, mine)], 1)
        return part.reshape(dp_n * qkv_rows, width)

    qkv_part = both_cores(mine, other)
    ones = links.gather_far(ones)

    def columns_of(part, shift, *blocks):
        return [(dot_nt(part, member) + shift).astype(BF) for member in blocks]

    far_place = seq_n // 2
    near_places = [r for r in range(seq_n) if r != far_place]
    near_columns = columns_of(qkv_part, qkv_shift, *ones[:far_place], *ones[1 - far_place :])
    far_rows = ones[far_place : far_place + len(ones) - seq_n + 1]
    far_columns = columns_of(after(qkv_part, near_columns), qkv_shift, jnp.concatenate(far_rows, 0))
    columns = dict(zip(near_places, near_columns)) | {far_place: far_columns[0]}
    got = links.exchange([columns[r] for r in range(seq_n)])

    def assemble(*got):
        got = [member.reshape(dp_n, qkv_rows, tok) for member in got]
        return jnp.stack(
            [
                lax.select_n(links.pos, *[got[(links.place[s] - p) % seq_n] for p in range(seq_n)])
                for s in range(seq_n)
            ],
            1,
        ).reshape(-1, tok)

    qkv = assemble(*got)
    query = qkv[:width].reshape(HEADS, HDIM, tok)
    pairs = links.gather_direct(jnp.concatenate([qkv[width:], codes], 0))
    fc_chips.append(links.z_next(after(fc_chips[1], pairs)))
    grads = links.gather_near(after(grad_low, pairs))

    spot = jnp.arange(tok, dtype=jnp.int32)

    def masked_scores(query, pairs):
        codes_all = [
            (member[2 * HDIM].astype(F32) * 128 + member[2 * HDIM + 1].astype(F32)).astype(jnp.int32)
            for member in pairs
        ]
        allowed = []
        for r in range(seq_n):
            place = links.seq_at(r)
            same = codes_all[r][:, None] == docs[None, :]
            if r == 0:
                allowed.append((same & (spot[:, None] < spot[None, :])) | (spot[:, None] == spot[None, :]))
            else:
                allowed.append(same & (place < links.seq))
        allowed = jnp.concatenate(allowed, 0)[None]
        keys = jnp.concatenate([member[:HDIM] for member in pairs], 1)
        values = jnp.concatenate([member[HDIM : 2 * HDIM] for member in pairs], 1)
        scores = jnp.einsum("dk,hdq->hkq", keys, query, preferred_element_type=F32) * scale
        return allowed, keys, values, jnp.where(allowed, scores, NEGATIVE)

    def attend(query, pairs):
        allowed, keys, values, scores = masked_scores(query, pairs)
        highest = jnp.max(scores, 1, keepdims=True)
        weights = jnp.where(allowed, jnp.exp(scores - highest), 0.0)
        total = jnp.sum(weights, 1, keepdims=True)
        attn = jnp.einsum("dk,hkq->hdq", values, weights.astype(BF), preferred_element_type=F32) / total
        return attn, highest + jnp.log(total), attn.reshape(width, tok).astype(BF).T

    attn, log_total, attn_low = attend(query, pairs)
    for _ in range(z_n - 3):
        fc_chips.append(links.z_next(after(fc_chips[-1], attn_low)))
    proj_chips = [proj_weight, links.z_next(after(proj_weight, fc_chips[2], attn_low))]

    def norm_two(attn_low, out_full, tokens):
        flat = tokens.reshape(tok, width).astype(F32)
        middle = flat + dot_nt(attn_low, out_full) + out_shift
        normed, inverse = normalize(middle)
        return middle, normed, inverse, (normed * gain_two + shift_two).astype(BF)

    middle, normed_two, inverse_two, hidden_two = norm_two(attn_low, out_full, tokens)
    twos = links.gather_near(after(hidden_two, grads[1], grads[-1]))

    twos = links.gather_far(twos)
    qkv_mine = lax.all_gather(after(mine, twos[1], twos[-1]), "seq", axis=0, tiled=True)
    qkv_mine = qkv_mine.reshape(-1, width)
    fc_chips = after(fc_chips, twos[1], twos[-1])
    fc_other = links.swap_core(join_rows(fc_chips))
    grads = links.gather_far(after(grads, twos))

    proj_chips.append(links.z_next(after(proj_chips[-1], twos)))
    pre_mine, act_mine = hidden_forward(after(twos, proj_chips[1]), fc_chips, fc_shift[:split])
    ready = act_mine[:8, :HDIM]
    pre_other, act_other = hidden_forward(after(twos, ready), [fc_other], fc_shift[split:])
    attns = links.gather_near(after(attn_low, grads, act_other))
    grads = after(grads, act_other)

    proj_sent = weight_terms(after(act_other, proj_chips[2]), grads, links.term_slots, units)
    proj_came = links.swap_core(proj_sent)
    proj_own = weight_terms(after(act_mine, proj_sent), grads, links.term_slots, units)
    for _ in range(z_n - 3):
        proj_chips.append(links.z_next(after(proj_chips[-1], act_other)))
    attns = links.gather_far(after(attns, proj_own))
    proj_term = links.first_term(proj_own, proj_came, units)
    proj_first = links.first_move(proj_term)
    proj_chips = after(proj_chips, proj_term, attns[1], attns[-1])
    proj_mine = join_rows(proj_chips)
    proj_other = links.swap_core(proj_mine)

    grad_mine, bias_mine = hidden_backward(grads, proj_chips, pre_mine)
    grad_other, bias_other = hidden_backward(after(grads, bias_mine), [proj_other], pre_other)
    fc_bias_sum = jnp.concatenate([bias_mine, bias_other])
    qkv_other = links.swap_core(after(qkv_mine, bias_mine))
    hidden_parts = hidden_sum(
        (after(grad_mine, attns), grad_other),
        [*fc_chips, fc_other],
        tok,
        links.sum_order,
        links.sum_cuts,
        4 * seq_n * tok * split * width,
    )
    hidden_far = links.sum_far(after(hidden_parts, proj_first) if z_n == 4 else hidden_parts)
    proj_term = links.second_term(proj_own, proj_came, proj_first, units, hidden_parts)
    proj_second = links.second_move(proj_term)
    fc_sent = weight_terms(after(grad_other, hidden_far, proj_second), twos, links.term_slots, units)
    fc_came = links.swap_core(fc_sent)
    fc_own = weight_terms(after(grad_mine, fc_sent, hidden_far), twos, links.term_slots, units)
    hidden_near = links.sum_near(hidden_parts, hidden_far)
    fc_term = links.first_term(fc_own, fc_came, units)
    fc_first = links.first_move(fc_term)
    mlp_parts = hidden_sum(
        (after(act_mine, fc_term), act_other), [proj_mine, proj_other], tok, tuple(range(1, seq_n)), 1, 0
    )
    mlp_came = [links.from_rel(mlp_parts[r], seq_n - r) for r in range(1, seq_n)]

    inverse_two = gate(inverse_two, mlp_parts)

    def middle_back(parts, far, near, normed_two, inverse_two, grad_low):
        grad_hidden = links.sum_end(parts, far, near)
        grad_out = grad_low.astype(F32)
        grad_middle = grad_out + norm_back(grad_hidden * gain_two, normed_two, inverse_two)
        sums = [
            jnp.sum(grad_middle, 0),
            jnp.sum(grad_hidden * normed_two, 0),
            jnp.sum(grad_hidden, 0),
            jnp.sum(grad_out, 0),
        ]
        low = grad_middle.astype(BF)
        return grad_middle, low, low.T, sums

    grad_middle, grad_middle_low, grad_middle_turned, early = middle_back(hidden_parts[0], hidden_far, hidden_near, normed_two, inverse_two, grad_low
    )

    def to_owners(member, needed=()):
        member = member.reshape(dp_n, seq_n, -1, tok)
        sent = [
            lax.dynamic_index_in_dim(member, links.seq_at(r), 1, False).reshape(-1, tok) for r in range(seq_n)
        ]
        return links.exchange(after(sent, needed))


    def ordered_parts(columns, rows):
        part = dot_nn(jnp.concatenate(columns, 1), jnp.concatenate(rows, 0))
        part = part.reshape(z_n, 2, -1, width)
        sent = lax.dynamic_index_in_dim(part, 1 - links.core, 1, False).astype(BF)
        return sent, lax.dynamic_index_in_dim(part, links.core, 1, False)

    def ordered_terms(kept, came):
        order = [links.z ^ k for k in (0, 2, 1, 3)] if z_n == 4 else [links.chip_before(m) for m in range(z_n)]
        return [
            jnp.concatenate([lax.dynamic_index_in_dim(member, k, 0, False) for k in order], 0)
            for member in (kept.astype(BF), came)
        ]

    def attend_back(out_full, grad_middle_low, query, pairs, attn, log_total):
        grad_attn = lax.dot_general(
            out_full, grad_middle_low, (((0,), (1,)), ((), ())), preferred_element_type=F32
        )
        grad_attn_low = grad_attn.astype(BF).reshape(HEADS, HDIM, tok)
        delta = jnp.sum(grad_attn_low.astype(F32) * attn, 1, keepdims=True)
        allowed, keys, values, scores = masked_scores(query, pairs)
        probs = jnp.where(allowed, jnp.exp(scores - log_total), 0.0)
        grad_probs = jnp.einsum("dk,hdq->hkq", values, grad_attn_low, preferred_element_type=F32)
        grad_scores = (probs * (grad_probs - delta)).astype(BF)
        grad_query = jnp.einsum("dk,hkq->hdq", keys, grad_scores, preferred_element_type=F32) * scale
        grad_keys = jnp.einsum("hkq,hdq->dk", grad_scores, query, preferred_element_type=F32) * scale
        grad_values = jnp.einsum("hkq,hdq->dk", probs.astype(BF), grad_attn_low, preferred_element_type=F32)
        grad_pair = jnp.concatenate([grad_keys, grad_values], 0)
        parts = [grad_pair[:, r * tok : (r + 1) * tok] for r in range(seq_n)]
        grad_query = grad_query.reshape(width, tok)
        return grad_query.astype(BF), jnp.sum(grad_query, 1), [parts[0]] + [part.astype(BF) for part in parts[1:]]

    log_total = gate(log_total, fc_first, grad_middle_low)
    grad_query, query_sum, parts = attend_back(out_full, grad_middle_low, query, pairs, attn, log_total
    )
    came = links.exchange(after(parts, mlp_came))
    fc_second = links.second_move(links.second_term(fc_own, fc_came, fc_first, units, parts))
    out_columns = to_owners(grad_middle_turned, mlp_came)
    out_sent, out_kept = ordered_parts(after(out_columns, parts), attns)
    out_came = links.swap_core(out_sent)

    def all_grads(grad_query, came):
        grad_pair = came[0]
        for member in came[1:]:
            grad_pair = grad_pair + member.astype(F32)
        return jnp.concatenate([grad_query, grad_pair.astype(BF)], 0), jnp.sum(grad_pair[HDIM:], 1)

    grad_qkv, value_sum = all_grads(grad_query, came)
    qkv_columns = to_owners(grad_qkv)
    out_rows = out_weight.shape[0]
    out_own, out_came = ordered_terms(out_kept, out_came)
    def tokens_back(grad_qkv, qkv_mine, qkv_other, grad_middle, normed_one, inverse_one):
        by_core = grad_qkv.reshape(z_n, 2, seq_n, qkv_rows, tok)

        def rows_of(core):
            rows = lax.dynamic_index_in_dim(by_core, core, 1, False)
            return rows.transpose(1, 0, 2, 3).reshape(-1, tok)

        grad_hidden = dot_tn(rows_of(links.core), qkv_mine) + dot_tn(rows_of(1 - links.core), qkv_other)
        back = grad_middle + norm_back(grad_hidden * gain_one, normed_one, inverse_one)
        return back.astype(BF), [jnp.sum(grad_hidden * normed_one, 0), jnp.sum(grad_hidden, 0)]

    tokens_grad, late = tokens_back(
        grad_qkv, qkv_mine, qkv_other, grad_middle, normed_one, inverse_one
    )
    out_first = links.first_move(links.first_term(out_own, out_came, out_rows))
    tokens_grad = tokens_grad.reshape(tokens.shape)
    fc_bias_sum = jnp.sum(jnp.where(owner[:, :, None], fc_bias_sum.reshape(dp_n, 1, units), 0.0), 0)
    fc_bias_sum = jnp.where(own_seq[None, :, None], fc_bias_sum[:, None, :], 0.0).reshape(-1)
    sums = jnp.concatenate(early + late + [query_sum, fc_bias_sum, value_sum])
    qkv_sent, qkv_kept = ordered_parts(after(qkv_columns, tokens_grad), ones)
    qkv_came = links.swap_core(qkv_sent)
    qkv_own, qkv_came = ordered_terms(qkv_kept, qkv_came)
    out_second = links.second_move(links.second_term(out_own, out_came, out_first, out_rows))
    qkv_term = links.first_term(qkv_own, qkv_came, qkv_rows)
    qkv_first = links.first_move(qkv_term, fc_second)
    sums = after(sums, qkv_term)
    bit = 1
    while bit < seq_n:
        sums = sums + links.other_seq(sums, bit)
        bit *= 2
    sums = sums + links.other_dp(sums, 1)
    bit = 2
    moved = links.other_dp(sums, bit)
    qkv_second = links.second_move(links.second_term(qkv_own, qkv_came, qkv_first, qkv_rows))
    sums = after(sums, qkv_second) + moved
    bit *= 2
    while bit < dp_n:
        sums = sums + links.other_dp(sums, bit)
        bit *= 2
    proj_grad = links.chip_sum_end(proj_own, proj_came, proj_first, proj_second, units, qkv_first)
    fc_grad = links.chip_sum_end(fc_own, fc_came, fc_first, fc_second, units, qkv_first)
    out_grad = links.chip_sum_end(out_own, out_came, out_first, out_second, out_rows)
    mlp = sum(member.astype(F32) for member in [mlp_parts[0], *after(mlp_came, fc_grad)])
    block_out = (middle + mlp + proj_shift).astype(BF).reshape(tokens.shape)
    qkv_grad = links.chip_sum_end(qkv_own, qkv_came, qkv_first, qkv_second, qkv_rows)

    wide = [sums[i * width : (i + 1) * width] for i in range(7)]
    fc_bias_grad = sums[7 * width : 7 * width + fc_bias.shape[0]]
    value_bias_grad = sums[7 * width + fc_bias.shape[0] :]
    return (
        block_out,
        tokens_grad,
        wide[4],
        wide[5],
        qkv_grad,
        wide[6],
        value_bias_grad,
        out_grad,
        wide[0],
        wide[1],
        wide[2],
        fc_grad,
        fc_bias_grad,
        proj_grad,
        wide[3],
    )


def solution(mesh):
    rows = P(("dp", "seq"), None)
    act = P("dp", "seq", None)
    return jax.shard_map(
        shards,
        mesh=mesh,
        in_specs=(
            act,
            P("dp", "seq"),
            P("dp", "seq"),
            P(),
            P(),
            rows,
            P(),
            P(),
            rows,
            P(),
            P(),
            P(),
            rows,
            P(),
            rows,
            P(),
            act,
        ),
        out_specs=(
            act,
            act,
            P(),
            P(),
            rows,
            P(),
            P(),
            rows,
            P(),
            P(),
            P(),
            rows,
            P(),
            rows,
            P(),
        ),
        check_vma=False,
    )
```

```python
import jax
import jax.numpy as jnp
from jax import lax
from jax.experimental import pallas as pl
from jax.experimental.pallas import tpu as pltpu
from jax.sharding import PartitionSpec as P

HEADS = 16
HDIM = 128
EPSILON = 1e-05
NEGATIVE = -1e30
BF = jnp.bfloat16
F32 = jnp.float32


def dot_nt(left, right):
    return lax.dot_general(left, right, (((1,), (1,)), ((), ())), preferred_element_type=F32)


def dot_nn(left, right):
    return lax.dot_general(left, right, (((1,), (0,)), ((), ())), preferred_element_type=F32)


def dot_tn(left, right):
    return lax.dot_general(left, right, (((0,), (0,)), ((), ())), preferred_element_type=F32)


def normalize(values):
    center = jnp.mean(values, -1, keepdims=True)
    shifted = values - center
    inverse = lax.rsqrt(jnp.mean(shifted * shifted, -1, keepdims=True) + EPSILON)
    return (shifted * inverse, inverse)


def norm_back(grad_normed, normed, inverse):
    first_mean = jnp.mean(grad_normed, -1, keepdims=True)
    second_mean = jnp.mean(grad_normed * normed, -1, keepdims=True)
    return inverse * (grad_normed - first_mean - normed * second_mean)


def gelu_tanh(values):
    return jax.nn.gelu(values, approximate=True)


FREE = pl.CostEstimate(flops=0, bytes_accessed=0, transcendentals=0)
TILE = 256
ANY = pl.BlockSpec(memory_space=pl.ANY)


def cost(flops, arrays):
    moved = sum(leaf.size * jnp.dtype(leaf.dtype).itemsize for leaf in jax.tree.leaves(arrays))
    return pl.CostEstimate(flops=flops, bytes_accessed=moved, transcendentals=0)


def call(kernel, name, out_shape, scratch, inputs, flops=None):
    estimate = cost(flops or 0, () if flops == 0 else (inputs, out_shape))
    return pl.pallas_call(
        kernel,
        name=name,
        out_shape=out_shape,
        in_specs=[ANY] * len(inputs),
        out_specs=jax.tree.map(lambda _: ANY, out_shape),
        scratch_shapes=scratch,
        cost_estimate=estimate,
        compiler_params=pltpu.CompilerParams(vmem_limit_bytes=44 * 1024 * 1024),
    )(*inputs)


def start_rows(pieces, buffer, sems):
    copies, row = [], 0
    for index, piece in enumerate(pieces):
        count = piece.shape[0]
        copy = pltpu.make_async_copy(piece, buffer.at[pl.ds(row, count)], sems.at[index])
        copy.start()
        copies.append((row, count, copy))
        row += count
    return copies


def wait_rows(copies, first, last):
    for row, _, copy in copies:
        if first <= row < last:
            copy.wait()


def join_rows(pieces):
    rows, width = sum(p.shape[0] for p in pieces), pieces[0].shape[1]

    def kernel(*refs):
        out_ref, buffer, in_sem, out_sem = refs[len(pieces) :]
        sent = []
        for index, (row, count, copy) in enumerate(start_rows(refs[: len(pieces)], buffer, in_sem)):
            copy.wait()
            part = pl.ds(row, count)
            sent.append(pltpu.make_async_copy(buffer.at[part], out_ref.at[part], out_sem.at[index]))
            sent[-1].start()
        for copy in sent:
            copy.wait()

    return call(
        kernel,
        "join_rows",
        jax.ShapeDtypeStruct((rows, width), pieces[0].dtype),
        [
            pltpu.VMEM((rows, width), pieces[0].dtype),
            pltpu.SemaphoreType.DMA((len(pieces),)),
            pltpu.SemaphoreType.DMA((len(pieces),)),
        ],
        tuple(pieces),
    )


def add_terms(members, rows, kind=BF):
    width = members[0][0].shape[1]
    step = min(rows, 64)

    def kernel(*refs):
        total = add_wide(refs[0][...], refs[1][...])
        for ref in refs[2:-1]:
            total = total + ref[...].astype(F32)
        refs[-1][...] = total.astype(kind)

    def spec(first):
        return pl.BlockSpec((step, width), lambda i: (i + first // step, 0))

    return pl.pallas_call(
        kernel,
        name="add_terms",
        grid=(rows // step,),
        out_shape=jax.ShapeDtypeStruct((rows, width), kind),
        in_specs=[spec(first) for _, first in members],
        out_specs=spec(0),
        cost_estimate=pl.CostEstimate(
            flops=0, bytes_accessed=2 * rows * width * (len(members) + 1), transcendentals=0
        ),
        compiler_params=pltpu.CompilerParams(vmem_limit_bytes=44 * 1024 * 1024),
    )(*[member for member, _ in members])


def gate(value, *needed):
    def kernel(value_ref, out_ref):
        out_ref[...] = value_ref[...]

    return pl.pallas_call(
        kernel,
        name="gate",
        out_shape=jax.ShapeDtypeStruct(value.shape, value.dtype),
        cost_estimate=FREE,
        compiler_params=pltpu.CompilerParams(vmem_limit_bytes=44 * 1024 * 1024),
    )(after(value, needed))


def row_tile(rows):
    return min(rows, 512)


def slope(values):
    inner = 0.7978845608028654 * (values + 0.044715 * values * values * values)
    curve = jnp.tanh(inner)
    return 0.5 * (1.0 + curve) + 0.5 * values * (1.0 - curve * curve) * 0.7978845608028654 * (
        1.0 + 3 * 0.044715 * values * values
    )


def hidden_forward(pieces, slots, shift):
    rows, width = sum(p.shape[0] for p in pieces), pieces[0].shape[1]
    units = sum(s.shape[0] for s in slots)
    step = row_tile(rows)

    def kernel(*refs):
        piece_refs, slot_refs = refs[: len(pieces)], refs[len(pieces) : len(pieces) + len(slots)]
        shift_hbm, pre_ref, act_ref, x, w, bias, pre_buf, act_buf, x_sem, w_sem, b_sem, out_sem = refs[
            len(pieces) + len(slots) :
        ]
        w_copies = start_rows(slot_refs, w, w_sem)
        x_copies = start_rows(piece_refs, x, x_sem)
        bias_copy = pltpu.make_async_copy(shift_hbm, bias, b_sem)
        bias_copy.start()
        bias_copy.wait()
        wait_rows(x_copies, 0, rows)
        sent = []
        for tile in range(units // TILE):
            slot = tile % 2
            columns = pl.ds(tile * TILE, TILE)
            wait_rows(w_copies, tile * TILE, (tile + 1) * TILE)
            if tile >= 2:
                for copy in sent[tile - 2]:
                    copy.wait()

            @pl.loop(0, rows // step)
            def _(index):
                part = pl.ds(index * step, step)
                pre = dot_nt(x[part], w[columns]) + bias[:, columns]
                pre_buf[slot, part] = pre
                act_buf[slot, part] = gelu_tanh(pre).astype(BF)

            sent.append(
                (
                    pltpu.make_async_copy(pre_buf.at[slot], pre_ref.at[:, columns], out_sem.at[slot, 0]),
                    pltpu.make_async_copy(act_buf.at[slot], act_ref.at[:, columns], out_sem.at[slot, 1]),
                )
            )
            for copy in sent[tile]:
                copy.start()
        for pair in sent[-2:]:
            for copy in pair:
                copy.wait()

    return call(
        kernel,
        "hidden_forward",
        (jax.ShapeDtypeStruct((rows, units), F32), jax.ShapeDtypeStruct((rows, units), BF)),
        [
            pltpu.VMEM((rows, width), BF),
            pltpu.VMEM((units, width), BF),
            pltpu.VMEM((1, units), F32),
            pltpu.VMEM((2, rows, TILE), F32),
            pltpu.VMEM((2, rows, TILE), BF),
            pltpu.SemaphoreType.DMA((len(pieces),)),
            pltpu.SemaphoreType.DMA((len(slots),)),
            pltpu.SemaphoreType.DMA,
            pltpu.SemaphoreType.DMA((2, 2)),
        ],
        (*pieces, *slots, shift.reshape(1, units)),
        2 * rows * units * width,
    )


def hidden_backward(pieces, slots, pre):
    rows, width = sum(p.shape[0] for p in pieces), pieces[0].shape[1]
    units = sum(s.shape[0] for s in slots)
    step = row_tile(rows)

    def kernel(*refs):
        piece_refs, slot_refs = refs[: len(pieces)], refs[len(pieces) : len(pieces) + len(slots)]
        pre_ref, grad_ref, sum_ref, x, w, sums, pre_buf, out_buf, x_sem, w_sem, p_sem, out_sem, s_sem = refs[
            len(pieces) + len(slots) :
        ]
        w_copies = start_rows(slot_refs, w, w_sem)
        x_copies = start_rows(piece_refs, x, x_sem)
        tiles = units // TILE

        def pre_copy(tile):
            return pltpu.make_async_copy(
                pre_ref.at[:, pl.ds(tile * TILE, TILE)], pre_buf.at[tile % 2], p_sem.at[tile % 2]
            )

        pre_copy(0).start()
        wait_rows(x_copies, 0, rows)
        sent = []
        for tile in range(tiles):
            slot = tile % 2
            columns = pl.ds(tile * TILE, TILE)
            wait_rows(w_copies, tile * TILE, (tile + 1) * TILE)
            pre_copy(tile).wait()
            if tile + 1 < tiles:
                pre_copy(tile + 1).start()
            if tile >= 2:
                sent[tile - 2].wait()
            sums[:, columns] = jnp.zeros((1, TILE), F32)

            @pl.loop(0, rows // step)
            def _(index):
                part = pl.ds(index * step, step)
                grad = dot_nt(x[part], w[columns]) * slope(pre_buf[slot, part])
                out_buf[slot, part] = grad.astype(BF)
                sums[:, columns] += jnp.sum(grad, 0, keepdims=True)

            sent.append(pltpu.make_async_copy(out_buf.at[slot], grad_ref.at[:, columns], out_sem.at[slot]))
            sent[tile].start()
        last = pltpu.make_async_copy(sums, sum_ref, s_sem)
        last.start()
        for copy in sent[-2:]:
            copy.wait()
        last.wait()

    grad, sums = call(
        kernel,
        "hidden_backward",
        (jax.ShapeDtypeStruct((rows, units), BF), jax.ShapeDtypeStruct((1, units), F32)),
        [
            pltpu.VMEM((rows, width), BF),
            pltpu.VMEM((units, width), BF),
            pltpu.VMEM((1, units), F32),
            pltpu.VMEM((2, rows, TILE), F32),
            pltpu.VMEM((2, rows, TILE), BF),
            pltpu.SemaphoreType.DMA((len(pieces),)),
            pltpu.SemaphoreType.DMA((len(slots),)),
            pltpu.SemaphoreType.DMA((2,)),
            pltpu.SemaphoreType.DMA((2,)),
            pltpu.SemaphoreType.DMA,
        ],
        (*pieces, *slots, pre),
        2 * rows * units * width,
    )
    return grad, sums.reshape(units)


def hidden_sum(lefts, slots, tok, order, cuts, flops):
    rows = lefts[0].shape[0]
    half = lefts[0].shape[1]
    width = slots[0].shape[1]
    depth = half * len(lefts)
    wide = min(width, 1024)

    def kernel(*refs):
        left_refs, slot_refs = refs[: len(lefts)], refs[len(lefts) : len(lefts) + len(slots)]
        rest = refs[len(lefts) + len(slots) :]
        own_ref, other_refs = rest[0], rest[1 : 1 + len(order) * cuts]
        x, w, own_buf, out_buf, x_sem, w_sem, out_sem = rest[1 + len(order) * cuts :]
        x_copies = []
        for index, left in enumerate(left_refs):
            x_copies.append(pltpu.make_async_copy(left, x.at[index], x_sem.at[index]))
            x_copies[-1].start()
        w_copies = start_rows(slot_refs, w, w_sem)
        for copy in x_copies:
            copy.wait()
        wait_rows(w_copies, 0, depth)

        def product(block, columns):
            part = pl.ds(block * tok, tok)
            total = dot_nn(x[0, part], w[pl.ds(0, half), columns])
            for index in range(1, len(lefts)):
                total = total + dot_nn(x[index, part], w[pl.ds(index * half, half), columns])
            return total

        sent = []
        for count, block in enumerate(order):
            slot = count % 2
            if count >= 2:
                for copy in sent[count - 2]:
                    copy.wait()

            @pl.loop(0, width // wide)
            def _(index):
                columns = pl.ds(pl.multiple_of(index * wide, wide), wide)
                out_buf[slot, :, columns] = product(block, columns).astype(BF)

            size = tok // cuts
            sent.append(
                [
                    pltpu.make_async_copy(
                        out_buf.at[slot, pl.ds(cut * size, size)],
                        other_refs[count * cuts + cut],
                        out_sem.at[slot, cut],
                    )
                    for cut in range(cuts)
                ]
            )
            for copy in sent[count]:
                copy.start()

        @pl.loop(0, width // wide)
        def _(index):
            columns = pl.ds(pl.multiple_of(index * wide, wide), wide)
            own_buf[:, columns] = product(0, columns)

        own_copy = pltpu.make_async_copy(own_buf, own_ref, out_sem.at[2, 0])
        own_copy.start()
        for copies in sent[-2:]:
            for copy in copies:
                copy.wait()
        own_copy.wait()

    return call(
        kernel,
        "hidden_sum",
        tuple(
            [jax.ShapeDtypeStruct((tok, width), F32)]
            + [jax.ShapeDtypeStruct((tok // cuts, width), BF)] * (len(order) * cuts)
        ),
        [
            pltpu.VMEM((len(lefts), rows, half), BF),
            pltpu.VMEM((depth, width), BF),
            pltpu.VMEM((tok, width), F32),
            pltpu.VMEM((2, tok, width), BF),
            pltpu.SemaphoreType.DMA((len(lefts),)),
            pltpu.SemaphoreType.DMA((len(slots),)),
            pltpu.SemaphoreType.DMA((3, cuts)),
        ],
        (*lefts, *slots),
        flops,
    )


def weight_terms(left, pieces, slots, size):
    rows, units = left.shape
    width = pieces[0].shape[1]
    def kernel(*refs):
        left_ref, piece_refs = refs[0], refs[1 : 1 + len(pieces)]
        out_ref, l, x, out_buf, l_sem, x_sem, out_sem = refs[1 + len(pieces) :]
        l_copy = pltpu.make_async_copy(left_ref, l, l_sem)
        l_copy.start()
        x_copies = start_rows(piece_refs, x, x_sem)
        l_copy.wait()
        wait_rows(x_copies, 0, rows)
        sent = []
        wide = min(width, 1024)
        source = slots() if size == TILE else range(units // TILE)
        for tile in range(units // TILE):
            slot = tile % 2
            if tile >= 2:
                sent[tile - 2].wait()
            columns = pl.ds(pl.multiple_of(source[tile] * TILE, TILE), TILE)

            @pl.loop(0, width // wide)
            def _(index):
                span = pl.ds(pl.multiple_of(index * wide, wide), wide)
                out_buf[slot, :, span] = dot_tn(l[:, columns], x[:, span]).astype(BF)

            sent.append(
                pltpu.make_async_copy(
                    out_buf.at[slot], out_ref.at[pl.ds(tile * TILE, TILE)], out_sem.at[slot]
                )
            )
            sent[tile].start()
        for copy in sent[-2:]:
            copy.wait()

    return call(
        kernel,
        "weight_terms",
        jax.ShapeDtypeStruct((units, width), BF),
        [
            pltpu.VMEM((rows, units), BF),
            pltpu.VMEM((rows, width), BF),
            pltpu.VMEM((2, TILE, width), BF),
            pltpu.SemaphoreType.DMA,
            pltpu.SemaphoreType.DMA((len(pieces),)),
            pltpu.SemaphoreType.DMA((2,)),
        ],
        (left, *pieces),
        2 * rows * units * width,
    )


def after(value, *needed):
    return lax.optimization_barrier((value, needed))[0]


def add_wide(left, right):
    return left.astype(F32) + right.astype(F32)


def add_low(left, right):
    return add_wide(left, right).astype(BF)


class Links:
    def __init__(self):
        self.seq_n = lax.axis_size("seq")
        self.dp_n = lax.axis_size("dp")
        self.z_n = self.dp_n // 2
        half = self.seq_n // 2
        self.ring = list(range(half)) + list(range(self.seq_n - 1, half - 1, -1))
        self.seq = lax.axis_index("seq")
        dp = lax.axis_index("dp")
        self.z = dp // 2
        self.core = dp % 2
        self.chips = list(range(0, self.z_n, 2)) + list(range(self.z_n - 1, 0, -2))
        self.chip_place = [self.chips.index(z) for z in range(self.z_n)]
        self.chip_pos = jnp.where(self.z % 2 == 0, self.z // 2, self.z_n - 1 - self.z // 2)
        self.place = [self.ring.index(s) for s in range(self.seq_n)]
        self.pos = jnp.where(self.seq < half, self.seq, self.seq_n - 1 + half - self.seq)

    def seq_at(self, rel):
        n, place = self.seq_n, (self.pos + rel) % self.seq_n
        return jnp.where(place < n // 2, place, n - 1 + n // 2 - place)

    def from_rel(self, value, rel):
        n = self.seq_n
        pairs = [(self.ring[(p + rel) % n], self.ring[p]) for p in range(n)]
        return lax.ppermute(value, "seq", pairs)

    def swap_core(self, value):
        pairs = [(i, i ^ 1) for i in range(self.dp_n)]
        return lax.ppermute(value, "dp", pairs)

    def z_next(self, value):
        pairs = [(self.chips[p - 1], self.chips[p]) for p in range(self.z_n)]
        return lax.ppermute(value, "dp", [(2 * i + c, 2 * j + c) for i, j in pairs for c in range(2)])

    def z_back(self, value):
        pairs = [(self.chips[p], self.chips[p - 1]) for p in range(self.z_n)]
        return lax.ppermute(value, "dp", [(2 * i + c, 2 * j + c) for i, j in pairs for c in range(2)])

    def gather_direct(self, value):
        return [value] + [self.from_rel(value, r) for r in range(1, self.seq_n)]

    def gather_near(self, value):
        if self.seq_n != 4:
            return self.gather_direct(value)
        return [value, self.from_rel(value, 1), None, self.from_rel(value, 3)]

    def gather_far(self, blocks):
        if self.seq_n != 4:
            return blocks
        half = blocks[0].shape[0] // 2
        top = self.from_rel(blocks[1][:half], 1)
        low = self.from_rel(blocks[3][half:], 3)
        return [blocks[0], blocks[1], top, low, blocks[3]]

    def exchange(self, parts):
        n = self.seq_n
        got = [parts[0]] + [None] * (n - 1)
        for r in range(1, n):
            got[n - r] = self.from_rel(parts[r], n - r)
        return got

    @property
    def sum_order(self):
        return (2, 1, 3) if self.seq_n == 4 else tuple(range(1, self.seq_n))

    @property
    def sum_cuts(self):
        return 2 if self.seq_n == 4 else 1

    def sum_far(self, parts):
        if self.seq_n != 4:
            return self.exchange(list(parts))[1:]
        far_top, far_low, right_top, right_low, left_top, left_low = parts[1:]
        return [
            self.from_rel(far_top, 3),
            self.from_rel(far_low, 1),
            self.from_rel(right_low, 3),
            self.from_rel(left_top, 1),
        ]

    def sum_near(self, parts, far, *needed):
        if self.seq_n != 4:
            return far
        return [
            self.from_rel(after(add_low(parts[3], far[0]), needed), 3),
            self.from_rel(after(add_low(parts[6], far[1]), needed), 1),
        ]

    def sum_end(self, own, far, near):
        if self.seq_n != 4:
            for member in near:
                own = own + member.astype(F32)
            return own
        half = own.shape[0] // 2
        return jnp.concatenate(
            [
                own[:half] + add_wide(near[0], far[3]),
                own[half:] + add_wide(far[2], near[1]),
            ],
            0,
        )

    def chips_ordered(self, blocks):
        n = self.z_n
        return [
            lax.select_n(self.z, *[blocks[(self.chip_place[z] - self.chip_place[k]) % n] for z in range(n)])
            for k in range(n)
        ]

    def chip_before(self, m):
        n, place = self.z_n, (self.chip_pos - m) % self.z_n
        return jnp.where(place < (n + 1) // 2, 2 * place, 2 * (n - 1 - place) + 1)

    def other_chip(self, value, bits):
        pairs = [(2 * z + c, 2 * (z ^ bits) + c) for z in range(self.z_n) for c in range(2)]
        return lax.ppermute(value, "dp", pairs)

    def term_slots(self):
        if self.z_n != 4:
            return list(range(self.z_n))
        z = lax.axis_index("dp") // 2
        outer = (z == 0) | (z == 3)
        return [0, jnp.where(outer, 3, 1), jnp.where(outer, 1, 3), 2]

    def first_term(self, own, came, rows, *needed):
        own = after(own, needed)
        if rows % 64 == 0:
            return add_terms([(own, 2 * rows), (came, 2 * rows)], 2 * rows)
        return add_low(own[2 * rows :], came[2 * rows :])

    def first_move(self, term, *needed):
        return self.other_chip(after(term, needed), 1) if self.z_n == 4 else None

    def second_term(self, own, came, first, rows, *needed):
        own = after(own, needed)
        if self.z_n != 4:
            total = add_wide(own, came)
            moved = total[(self.z_n - 1) * rows :].astype(BF)
            for m in range(self.z_n - 2, 0, -1):
                moved = self.z_back(moved)
                moved = (total[m * rows : (m + 1) * rows] + moved.astype(F32)).astype(BF)
            return self.z_back(moved)
        if rows % 64 == 0:
            return add_terms([(own, rows), (came, rows), (first, rows)], rows)
        part = slice(rows, 2 * rows)
        return (add_wide(own[part], came[part]) + first[part].astype(F32)).astype(BF)

    def second_move(self, term, *needed):
        return self.other_chip(after(term, needed), 2) if self.z_n == 4 else term

    def chip_sum_end(self, own, came, first, second, rows, *needed):
        if rows % 64 == 0 and first is not None:
            members = [(after(own, needed), 0), (came, 0), (first, 0), (second, 0)]
            return add_terms(members, rows, F32)
        total = add_wide(own[:rows], came[:rows]) + second.astype(F32)
        return total if first is None else total + first[:rows].astype(F32)

    def other_seq(self, value, bit):
        return lax.ppermute(value, "seq", [(i, i ^ bit) for i in range(self.seq_n)])

    def other_dp(self, value, bit):
        return lax.ppermute(value, "dp", [(i, i ^ bit) for i in range(self.dp_n)])


def shards(
    tokens,
    doc_ids,
    pad_mask,
    attn_norm_gain,
    attn_norm_bias,
    qkv_weight,
    query_bias,
    value_bias,
    out_weight,
    out_bias,
    mlp_norm_gain,
    mlp_norm_bias,
    fc_weight,
    fc_bias,
    proj_weight,
    proj_bias,
    cotangent,
):
    links = Links()
    seq_n, dp_n, z_n = links.seq_n, links.dp_n, links.z_n
    tok = tokens.shape[1]
    width = tokens.shape[2]
    scale = HDIM ** (-0.5)
    gain_one = attn_norm_gain.astype(F32)
    shift_one = attn_norm_bias.astype(F32)
    out_shift = out_bias.astype(F32)
    gain_two = mlp_norm_gain.astype(F32)
    shift_two = mlp_norm_bias.astype(F32)
    proj_shift = proj_bias.astype(F32)

    docs = doc_ids[0]
    codes = jnp.where(pad_mask[0] == 1, docs, -1)
    codes = jnp.stack([codes // 128, codes % 128] + [jnp.zeros_like(codes)] * 14).astype(BF)

    units = fc_weight.shape[0]
    split = z_n * units

    block_index = jnp.arange(dp_n)
    owner = 2 * links.chip_before(block_index % z_n) + (links.core ^ (block_index // z_n))
    owner = owner[:, None] == jnp.arange(dp_n)[None, :]
    own_seq = jnp.arange(seq_n) == links.seq
    fc_shift = fc_bias.reshape(dp_n, seq_n, units).astype(F32)
    fc_shift = jnp.sum(jnp.where(own_seq[None, :, None], fc_shift, 0.0), 1)
    fc_shift = jnp.sum(jnp.where(owner[:, :, None], fc_shift[None], 0.0), 1).reshape(-1)
    qkv_rows = qkv_weight.shape[0]
    qkv_shift = jnp.concatenate(
        [query_bias.astype(F32), jnp.zeros((HDIM,), F32), value_bias.astype(F32)]
    ).reshape(dp_n, seq_n, qkv_rows)
    qkv_shift = jnp.sum(jnp.where(own_seq[None, :, None], qkv_shift, 0.0), 1).reshape(-1, 1)

    qkv_chips = [qkv_weight, links.z_next(qkv_weight)]
    grad_low = cotangent.reshape(tok, width)

    def norm_one(member):
        flat = member.reshape(tok, width).astype(F32)
        normed, inverse = normalize(flat)
        return (normed * gain_one + shift_one).astype(BF), normed, inverse

    hidden_one, normed_one, inverse_one = norm_one(tokens)
    ones = links.gather_near(after(hidden_one, qkv_chips[1]))
    qkv_chips[1] = after(qkv_chips[1], hidden_one)
    for _ in range(z_n - 2):
        qkv_chips.append(links.z_next(qkv_chips[-1]))
    fc_chips = [fc_weight, links.z_next(after(fc_weight, qkv_chips))]
    qkv_chips = after(qkv_chips, ones[1], ones[-1], qkv_shift, fc_shift)
    out_full = lax.all_gather(out_weight, ("dp", "seq"), axis=0, tiled=True)

    mine = jnp.stack(links.chips_ordered(qkv_chips), 0)
    other = links.swap_core(mine)

    def both_cores(mine, other):
        first = links.core == 0
        part = jnp.stack([jnp.where(first, mine, other), jnp.where(first, other, mine)], 1)
        return part.reshape(dp_n * qkv_rows, width)

    qkv_part = both_cores(mine, other)
    ones = links.gather_far(ones)

    def columns_of(part, shift, *blocks):
        return [(dot_nt(part, member) + shift).astype(BF) for member in blocks]

    far_place = seq_n // 2
    near_places = [r for r in range(seq_n) if r != far_place]
    near_columns = columns_of(qkv_part, qkv_shift, *ones[:far_place], *ones[1 - far_place :])
    far_rows = ones[far_place : far_place + len(ones) - seq_n + 1]
    far_columns = columns_of(after(qkv_part, near_columns), qkv_shift, jnp.concatenate(far_rows, 0))
    columns = dict(zip(near_places, near_columns)) | {far_place: far_columns[0]}
    got = links.exchange([columns[r] for r in range(seq_n)])

    def assemble(*got):
        got = [member.reshape(dp_n, qkv_rows, tok) for member in got]
        return jnp.stack(
            [
                lax.select_n(links.pos, *[got[(links.place[s] - p) % seq_n] for p in range(seq_n)])
                for s in range(seq_n)
            ],
            1,
        ).reshape(-1, tok)

    qkv = assemble(*got)
    query = qkv[:width].reshape(HEADS, HDIM, tok)
    pairs = links.gather_direct(jnp.concatenate([qkv[width:], codes], 0))
    fc_chips.append(links.z_next(after(fc_chips[1], pairs)))
    grads = links.gather_near(after(grad_low, pairs))

    spot = jnp.arange(tok, dtype=jnp.int32)

    def masked_scores(query, pairs):
        codes_all = [
            (member[2 * HDIM].astype(F32) * 128 + member[2 * HDIM + 1].astype(F32)).astype(jnp.int32)
            for member in pairs
        ]
        allowed = []
        for r in range(seq_n):
            place = links.seq_at(r)
            same = codes_all[r][:, None] == docs[None, :]
            if r == 0:
                allowed.append((same & (spot[:, None] < spot[None, :])) | (spot[:, None] == spot[None, :]))
            else:
                allowed.append(same & (place < links.seq))
        allowed = jnp.concatenate(allowed, 0)[None]
        keys = jnp.concatenate([member[:HDIM] for member in pairs], 1)
        values = jnp.concatenate([member[HDIM : 2 * HDIM] for member in pairs], 1)
        scores = jnp.einsum("dk,hdq->hkq", keys, query, preferred_element_type=F32) * scale
        return allowed, keys, values, jnp.where(allowed, scores, NEGATIVE)

    def attend(query, pairs):
        allowed, keys, values, scores = masked_scores(query, pairs)
        highest = jnp.max(scores, 1, keepdims=True)
        weights = jnp.where(allowed, jnp.exp(scores - highest), 0.0)
        total = jnp.sum(weights, 1, keepdims=True)
        attn = jnp.einsum("dk,hkq->hdq", values, weights.astype(BF), preferred_element_type=F32) / total
        return attn, highest + jnp.log(total), attn.reshape(width, tok).astype(BF).T

    attn, log_total, attn_low = attend(query, pairs)
    for _ in range(z_n - 3):
        fc_chips.append(links.z_next(after(fc_chips[-1], attn_low)))
    proj_chips = [proj_weight, links.z_next(after(proj_weight, fc_chips[2], attn_low))]

    def norm_two(attn_low, out_full, tokens):
        flat = tokens.reshape(tok, width).astype(F32)
        middle = flat + dot_nt(attn_low, out_full) + out_shift
        normed, inverse = normalize(middle)
        return middle, normed, inverse, (normed * gain_two + shift_two).astype(BF)

    middle, normed_two, inverse_two, hidden_two = norm_two(attn_low, out_full, tokens)
    twos = links.gather_near(after(hidden_two, grads[1], grads[-1]))

    twos = links.gather_far(twos)
    qkv_mine = lax.all_gather(after(mine, twos[1], twos[-1]), "seq", axis=0, tiled=True)
    qkv_mine = qkv_mine.reshape(-1, width)
    fc_chips = after(fc_chips, twos[1], twos[-1])
    fc_other = links.swap_core(join_rows(fc_chips))
    grads = links.gather_far(after(grads, twos))

    proj_chips.append(links.z_next(after(proj_chips[-1], twos)))
    pre_mine, act_mine = hidden_forward(after(twos, proj_chips[1]), fc_chips, fc_shift[:split])
    ready = act_mine[:8, :HDIM]
    pre_other, act_other = hidden_forward(after(twos, ready), [fc_other], fc_shift[split:])
    attns = links.gather_near(after(attn_low, grads, act_other))
    grads = after(grads, act_other)

    proj_sent = weight_terms(after(act_other, proj_chips[2]), grads, links.term_slots, units)
    proj_came = links.swap_core(proj_sent)
    proj_own = weight_terms(after(act_mine, proj_sent), grads, links.term_slots, units)
    for _ in range(z_n - 3):
        proj_chips.append(links.z_next(after(proj_chips[-1], act_other)))
    attns = links.gather_far(after(attns, proj_own))
    proj_term = links.first_term(proj_own, proj_came, units)
    proj_first = links.first_move(proj_term)
    proj_chips = after(proj_chips, proj_term, attns[1], attns[-1])
    proj_mine = join_rows(proj_chips)
    proj_other = links.swap_core(proj_mine)

    grad_mine, bias_mine = hidden_backward(grads, proj_chips, pre_mine)
    grad_other, bias_other = hidden_backward(after(grads, bias_mine), [proj_other], pre_other)
    fc_bias_sum = jnp.concatenate([bias_mine, bias_other])
    qkv_other = links.swap_core(after(qkv_mine, bias_mine))
    hidden_parts = hidden_sum(
        (after(grad_mine, attns), grad_other),
        [*fc_chips, fc_other],
        tok,
        links.sum_order,
        links.sum_cuts,
        4 * seq_n * tok * split * width,
    )
    hidden_far = links.sum_far(after(hidden_parts, proj_first) if z_n == 4 else hidden_parts)
    proj_term = links.second_term(proj_own, proj_came, proj_first, units, hidden_parts)
    proj_second = links.second_move(proj_term)
    fc_sent = weight_terms(after(grad_other, hidden_far, proj_second), twos, links.term_slots, units)
    fc_came = links.swap_core(fc_sent)
    fc_own = weight_terms(after(grad_mine, fc_sent, hidden_far), twos, links.term_slots, units)
    hidden_near = links.sum_near(hidden_parts, hidden_far)
    fc_term = links.first_term(fc_own, fc_came, units)
    fc_first = links.first_move(fc_term)
    mlp_parts = hidden_sum(
        (after(act_mine, fc_term), act_other), [proj_mine, proj_other], tok, tuple(range(1, seq_n)), 1, 0
    )
    mlp_came = [links.from_rel(mlp_parts[r], seq_n - r) for r in range(1, seq_n)]

    inverse_two = gate(inverse_two, mlp_parts)

    def middle_back(parts, far, near, normed_two, inverse_two, grad_low):
        grad_hidden = links.sum_end(parts, far, near)
        grad_out = grad_low.astype(F32)
        grad_middle = grad_out + norm_back(grad_hidden * gain_two, normed_two, inverse_two)
        sums = [
            jnp.sum(grad_middle, 0),
            jnp.sum(grad_hidden * normed_two, 0),
            jnp.sum(grad_hidden, 0),
            jnp.sum(grad_out, 0),
        ]
        low = grad_middle.astype(BF)
        return grad_middle, low, low.T, sums

    grad_middle, grad_middle_low, grad_middle_turned, early = middle_back(hidden_parts[0], hidden_far, hidden_near, normed_two, inverse_two, grad_low
    )

    def to_owners(member, needed=()):
        member = member.reshape(dp_n, seq_n, -1, tok)
        sent = [
            lax.dynamic_index_in_dim(member, links.seq_at(r), 1, False).reshape(-1, tok) for r in range(seq_n)
        ]
        return links.exchange(after(sent, needed))


    def ordered_parts(columns, rows):
        part = dot_nn(jnp.concatenate(columns, 1), jnp.concatenate(rows, 0))
        part = part.reshape(z_n, 2, -1, width)
        sent = lax.dynamic_index_in_dim(part, 1 - links.core, 1, False).astype(BF)
        return sent, lax.dynamic_index_in_dim(part, links.core, 1, False)

    def ordered_terms(kept, came):
        order = [links.z ^ k for k in (0, 2, 1, 3)] if z_n == 4 else [links.chip_before(m) for m in range(z_n)]
        return [
            jnp.concatenate([lax.dynamic_index_in_dim(member, k, 0, False) for k in order], 0)
            for member in (kept.astype(BF), came)
        ]

    def attend_back(out_full, grad_middle_low, query, pairs, attn, log_total):
        grad_attn = lax.dot_general(
            out_full, grad_middle_low, (((0,), (1,)), ((), ())), preferred_element_type=F32
        )
        grad_attn_low = grad_attn.astype(BF).reshape(HEADS, HDIM, tok)
        delta = jnp.sum(grad_attn_low.astype(F32) * attn, 1, keepdims=True)
        allowed, keys, values, scores = masked_scores(query, pairs)
        probs = jnp.where(allowed, jnp.exp(scores - log_total), 0.0)
        grad_probs = jnp.einsum("dk,hdq->hkq", values, grad_attn_low, preferred_element_type=F32)
        grad_scores = (probs * (grad_probs - delta)).astype(BF)
        grad_query = jnp.einsum("dk,hkq->hdq", keys, grad_scores, preferred_element_type=F32) * scale
        grad_keys = jnp.einsum("hkq,hdq->dk", grad_scores, query, preferred_element_type=F32) * scale
        grad_values = jnp.einsum("hkq,hdq->dk", probs.astype(BF), grad_attn_low, preferred_element_type=F32)
        grad_pair = jnp.concatenate([grad_keys, grad_values], 0)
        parts = [grad_pair[:, r * tok : (r + 1) * tok] for r in range(seq_n)]
        grad_query = grad_query.reshape(width, tok)
        return grad_query.astype(BF), jnp.sum(grad_query, 1), [parts[0]] + [part.astype(BF) for part in parts[1:]]

    grad_middle_low = gate(grad_middle_low, fc_first)
    grad_query, query_sum, parts = attend_back(out_full, grad_middle_low, query, pairs, attn, log_total
    )
    came = links.exchange(after(parts, mlp_came))
    fc_second = links.second_move(links.second_term(fc_own, fc_came, fc_first, units, parts))
    out_columns = to_owners(grad_middle_turned, mlp_came[:1])
    out_sent, out_kept = ordered_parts(after(out_columns, parts), attns)
    out_came = links.swap_core(out_sent)

    def all_grads(grad_query, came):
        grad_pair = came[0]
        for member in came[1:]:
            grad_pair = grad_pair + member.astype(F32)
        return jnp.concatenate([grad_query, grad_pair.astype(BF)], 0), jnp.sum(grad_pair[HDIM:], 1)

    grad_qkv, value_sum = all_grads(grad_query, came)
    qkv_columns = to_owners(grad_qkv)
    out_rows = out_weight.shape[0]
    out_own, out_came = ordered_terms(out_kept, out_came)
    def tokens_back(grad_qkv, qkv_mine, qkv_other, grad_middle, normed_one, inverse_one):
        by_core = grad_qkv.reshape(z_n, 2, seq_n, qkv_rows, tok)

        def rows_of(core):
            rows = lax.dynamic_index_in_dim(by_core, core, 1, False)
            return rows.transpose(1, 0, 2, 3).reshape(-1, tok)

        grad_hidden = dot_tn(rows_of(links.core), qkv_mine) + dot_tn(rows_of(1 - links.core), qkv_other)
        back = grad_middle + norm_back(grad_hidden * gain_one, normed_one, inverse_one)
        return back.astype(BF), [jnp.sum(grad_hidden * normed_one, 0), jnp.sum(grad_hidden, 0)]

    tokens_grad, late = tokens_back(
        grad_qkv, qkv_mine, qkv_other, grad_middle, normed_one, inverse_one
    )
    out_first = links.first_move(links.first_term(out_own, out_came, out_rows))
    tokens_grad = tokens_grad.reshape(tokens.shape)
    fc_bias_sum = jnp.sum(jnp.where(owner[:, :, None], fc_bias_sum.reshape(dp_n, 1, units), 0.0), 0)
    fc_bias_sum = jnp.where(own_seq[None, :, None], fc_bias_sum[:, None, :], 0.0).reshape(-1)
    sums = jnp.concatenate(early + late + [query_sum, fc_bias_sum, value_sum])
    qkv_sent, qkv_kept = ordered_parts(after(qkv_columns, tokens_grad), ones)
    qkv_came = links.swap_core(qkv_sent)
    qkv_own, qkv_came = ordered_terms(qkv_kept, qkv_came)
    out_second = links.second_move(links.second_term(out_own, out_came, out_first, out_rows))
    qkv_term = links.first_term(qkv_own, qkv_came, qkv_rows)
    qkv_first = links.first_move(qkv_term, fc_second)
    sums = after(sums, qkv_term)
    bit = 1
    while bit < seq_n:
        sums = sums + links.other_seq(sums, bit)
        bit *= 2
    sums = sums + links.other_dp(sums, 1)
    bit = 2
    moved = links.other_dp(sums, bit)
    qkv_second = links.second_move(links.second_term(qkv_own, qkv_came, qkv_first, qkv_rows))
    sums = after(sums, qkv_second) + moved
    bit *= 2
    while bit < dp_n:
        sums = sums + links.other_dp(sums, bit)
        bit *= 2
    proj_grad = links.chip_sum_end(proj_own, proj_came, proj_first, proj_second, units, qkv_first)
    fc_grad = links.chip_sum_end(fc_own, fc_came, fc_first, fc_second, units, qkv_first)
    out_grad = links.chip_sum_end(out_own, out_came, out_first, out_second, out_rows)
    mlp = sum(member.astype(F32) for member in [mlp_parts[0], *after(mlp_came, fc_grad)])
    block_out = (middle + mlp + proj_shift).astype(BF).reshape(tokens.shape)
    qkv_grad = links.chip_sum_end(qkv_own, qkv_came, qkv_first, qkv_second, qkv_rows)

    wide = [sums[i * width : (i + 1) * width] for i in range(7)]
    fc_bias_grad = sums[7 * width : 7 * width + fc_bias.shape[0]]
    value_bias_grad = sums[7 * width + fc_bias.shape[0] :]
    return (
        block_out,
        tokens_grad,
        wide[4],
        wide[5],
        qkv_grad,
        wide[6],
        value_bias_grad,
        out_grad,
        wide[0],
        wide[1],
        wide[2],
        fc_grad,
        fc_bias_grad,
        proj_grad,
        wide[3],
    )


def solution(mesh):
    rows = P(("dp", "seq"), None)
    act = P("dp", "seq", None)
    return jax.shard_map(
        shards,
        mesh=mesh,
        in_specs=(
            act,
            P("dp", "seq"),
            P("dp", "seq"),
            P(),
            P(),
            rows,
            P(),
            P(),
            rows,
            P(),
            P(),
            P(),
            rows,
            P(),
            rows,
            P(),
            act,
        ),
        out_specs=(
            act,
            act,
            P(),
            P(),
            rows,
            P(),
            P(),
            rows,
            P(),
            P(),
            P(),
            rows,
            P(),
            rows,
            P(),
        ),
        check_vma=False,
    )
```

```python
import jax
import jax.numpy as jnp
from jax import lax
from jax.experimental import pallas as pl
from jax.experimental.pallas import tpu as pltpu
from jax.sharding import PartitionSpec as P

HEADS = 16
HDIM = 128
EPSILON = 1e-05
NEGATIVE = -1e30
BF = jnp.bfloat16
F32 = jnp.float32


def dot_nt(left, right):
    return lax.dot_general(left, right, (((1,), (1,)), ((), ())), preferred_element_type=F32)


def dot_nn(left, right):
    return lax.dot_general(left, right, (((1,), (0,)), ((), ())), preferred_element_type=F32)


def dot_tn(left, right):
    return lax.dot_general(left, right, (((0,), (0,)), ((), ())), preferred_element_type=F32)


def normalize(values):
    center = jnp.mean(values, -1, keepdims=True)
    shifted = values - center
    inverse = lax.rsqrt(jnp.mean(shifted * shifted, -1, keepdims=True) + EPSILON)
    return (shifted * inverse, inverse)


def norm_back(grad_normed, normed, inverse):
    first_mean = jnp.mean(grad_normed, -1, keepdims=True)
    second_mean = jnp.mean(grad_normed * normed, -1, keepdims=True)
    return inverse * (grad_normed - first_mean - normed * second_mean)


def gelu_tanh(values):
    return jax.nn.gelu(values, approximate=True)


FREE = pl.CostEstimate(flops=0, bytes_accessed=0, transcendentals=0)
TILE = 256
ANY = pl.BlockSpec(memory_space=pl.ANY)


def cost(flops, arrays):
    moved = sum(leaf.size * jnp.dtype(leaf.dtype).itemsize for leaf in jax.tree.leaves(arrays))
    return pl.CostEstimate(flops=flops, bytes_accessed=moved, transcendentals=0)


def call(kernel, name, out_shape, scratch, inputs, flops=None):
    estimate = cost(flops or 0, () if flops == 0 else (inputs, out_shape))
    return pl.pallas_call(
        kernel,
        name=name,
        out_shape=out_shape,
        in_specs=[ANY] * len(inputs),
        out_specs=jax.tree.map(lambda _: ANY, out_shape),
        scratch_shapes=scratch,
        cost_estimate=estimate,
        compiler_params=pltpu.CompilerParams(vmem_limit_bytes=44 * 1024 * 1024),
    )(*inputs)


def start_rows(pieces, buffer, sems):
    copies, row = [], 0
    for index, piece in enumerate(pieces):
        count = piece.shape[0]
        copy = pltpu.make_async_copy(piece, buffer.at[pl.ds(row, count)], sems.at[index])
        copy.start()
        copies.append((row, count, copy))
        row += count
    return copies


def wait_rows(copies, first, last):
    for row, _, copy in copies:
        if first <= row < last:
            copy.wait()


def join_rows(pieces):
    rows, width = sum(p.shape[0] for p in pieces), pieces[0].shape[1]

    def kernel(*refs):
        out_ref, buffer, in_sem, out_sem = refs[len(pieces) :]
        sent = []
        for index, (row, count, copy) in enumerate(start_rows(refs[: len(pieces)], buffer, in_sem)):
            copy.wait()
            part = pl.ds(row, count)
            sent.append(pltpu.make_async_copy(buffer.at[part], out_ref.at[part], out_sem.at[index]))
            sent[-1].start()
        for copy in sent:
            copy.wait()

    return call(
        kernel,
        "join_rows",
        jax.ShapeDtypeStruct((rows, width), pieces[0].dtype),
        [
            pltpu.VMEM((rows, width), pieces[0].dtype),
            pltpu.SemaphoreType.DMA((len(pieces),)),
            pltpu.SemaphoreType.DMA((len(pieces),)),
        ],
        tuple(pieces),
    )


def add_terms(members, rows, kind=BF):
    width = members[0][0].shape[1]
    step = min(rows, 64)

    def kernel(*refs):
        total = add_wide(refs[0][...], refs[1][...])
        for ref in refs[2:-1]:
            total = total + ref[...].astype(F32)
        refs[-1][...] = total.astype(kind)

    def spec(first):
        return pl.BlockSpec((step, width), lambda i: (i + first // step, 0))

    return pl.pallas_call(
        kernel,
        name="add_terms",
        grid=(rows // step,),
        out_shape=jax.ShapeDtypeStruct((rows, width), kind),
        in_specs=[spec(first) for _, first in members],
        out_specs=spec(0),
        cost_estimate=pl.CostEstimate(
            flops=0, bytes_accessed=2 * rows * width * (len(members) + 1), transcendentals=0
        ),
        compiler_params=pltpu.CompilerParams(vmem_limit_bytes=44 * 1024 * 1024),
    )(*[member for member, _ in members])


def gate(value, *needed):
    def kernel(value_ref, out_ref):
        out_ref[...] = value_ref[...]

    return pl.pallas_call(
        kernel,
        name="gate",
        out_shape=jax.ShapeDtypeStruct(value.shape, value.dtype),
        cost_estimate=FREE,
        compiler_params=pltpu.CompilerParams(vmem_limit_bytes=44 * 1024 * 1024),
    )(after(value, needed))


def row_tile(rows):
    return min(rows, 512)


def slope(values):
    inner = 0.7978845608028654 * (values + 0.044715 * values * values * values)
    curve = jnp.tanh(inner)
    return 0.5 * (1.0 + curve) + 0.5 * values * (1.0 - curve * curve) * 0.7978845608028654 * (
        1.0 + 3 * 0.044715 * values * values
    )


def hidden_forward(pieces, slots, shift):
    rows, width = sum(p.shape[0] for p in pieces), pieces[0].shape[1]
    units = sum(s.shape[0] for s in slots)
    step = row_tile(rows)

    def kernel(*refs):
        piece_refs, slot_refs = refs[: len(pieces)], refs[len(pieces) : len(pieces) + len(slots)]
        shift_hbm, pre_ref, act_ref, x, w, bias, pre_buf, act_buf, x_sem, w_sem, b_sem, out_sem = refs[
            len(pieces) + len(slots) :
        ]
        w_copies = start_rows(slot_refs, w, w_sem)
        x_copies = start_rows(piece_refs, x, x_sem)
        bias_copy = pltpu.make_async_copy(shift_hbm, bias, b_sem)
        bias_copy.start()
        bias_copy.wait()
        wait_rows(x_copies, 0, rows)
        sent = []
        for tile in range(units // TILE):
            slot = tile % 2
            columns = pl.ds(tile * TILE, TILE)
            wait_rows(w_copies, tile * TILE, (tile + 1) * TILE)
            if tile >= 2:
                for copy in sent[tile - 2]:
                    copy.wait()

            @pl.loop(0, rows // step)
            def _(index):
                part = pl.ds(index * step, step)
                pre = dot_nt(x[part], w[columns]) + bias[:, columns]
                pre_buf[slot, part] = pre
                act_buf[slot, part] = gelu_tanh(pre).astype(BF)

            sent.append(
                (
                    pltpu.make_async_copy(pre_buf.at[slot], pre_ref.at[:, columns], out_sem.at[slot, 0]),
                    pltpu.make_async_copy(act_buf.at[slot], act_ref.at[:, columns], out_sem.at[slot, 1]),
                )
            )
            for copy in sent[tile]:
                copy.start()
        for pair in sent[-2:]:
            for copy in pair:
                copy.wait()

    return call(
        kernel,
        "hidden_forward",
        (jax.ShapeDtypeStruct((rows, units), F32), jax.ShapeDtypeStruct((rows, units), BF)),
        [
            pltpu.VMEM((rows, width), BF),
            pltpu.VMEM((units, width), BF),
            pltpu.VMEM((1, units), F32),
            pltpu.VMEM((2, rows, TILE), F32),
            pltpu.VMEM((2, rows, TILE), BF),
            pltpu.SemaphoreType.DMA((len(pieces),)),
            pltpu.SemaphoreType.DMA((len(slots),)),
            pltpu.SemaphoreType.DMA,
            pltpu.SemaphoreType.DMA((2, 2)),
        ],
        (*pieces, *slots, shift.reshape(1, units)),
        2 * rows * units * width,
    )


def hidden_backward(pieces, slots, pre):
    rows, width = sum(p.shape[0] for p in pieces), pieces[0].shape[1]
    units = sum(s.shape[0] for s in slots)
    step = row_tile(rows)

    def kernel(*refs):
        piece_refs, slot_refs = refs[: len(pieces)], refs[len(pieces) : len(pieces) + len(slots)]
        pre_ref, grad_ref, sum_ref, x, w, sums, pre_buf, out_buf, x_sem, w_sem, p_sem, out_sem, s_sem = refs[
            len(pieces) + len(slots) :
        ]
        w_copies = start_rows(slot_refs, w, w_sem)
        x_copies = start_rows(piece_refs, x, x_sem)
        tiles = units // TILE

        def pre_copy(tile):
            return pltpu.make_async_copy(
                pre_ref.at[:, pl.ds(tile * TILE, TILE)], pre_buf.at[tile % 2], p_sem.at[tile % 2]
            )

        pre_copy(0).start()
        wait_rows(x_copies, 0, rows)
        sent = []
        for tile in range(tiles):
            slot = tile % 2
            columns = pl.ds(tile * TILE, TILE)
            wait_rows(w_copies, tile * TILE, (tile + 1) * TILE)
            pre_copy(tile).wait()
            if tile + 1 < tiles:
                pre_copy(tile + 1).start()
            if tile >= 2:
                sent[tile - 2].wait()
            sums[:, columns] = jnp.zeros((1, TILE), F32)

            @pl.loop(0, rows // step)
            def _(index):
                part = pl.ds(index * step, step)
                grad = dot_nt(x[part], w[columns]) * slope(pre_buf[slot, part])
                out_buf[slot, part] = grad.astype(BF)
                sums[:, columns] += jnp.sum(grad, 0, keepdims=True)

            sent.append(pltpu.make_async_copy(out_buf.at[slot], grad_ref.at[:, columns], out_sem.at[slot]))
            sent[tile].start()
        last = pltpu.make_async_copy(sums, sum_ref, s_sem)
        last.start()
        for copy in sent[-2:]:
            copy.wait()
        last.wait()

    grad, sums = call(
        kernel,
        "hidden_backward",
        (jax.ShapeDtypeStruct((rows, units), BF), jax.ShapeDtypeStruct((1, units), F32)),
        [
            pltpu.VMEM((rows, width), BF),
            pltpu.VMEM((units, width), BF),
            pltpu.VMEM((1, units), F32),
            pltpu.VMEM((2, rows, TILE), F32),
            pltpu.VMEM((2, rows, TILE), BF),
            pltpu.SemaphoreType.DMA((len(pieces),)),
            pltpu.SemaphoreType.DMA((len(slots),)),
            pltpu.SemaphoreType.DMA((2,)),
            pltpu.SemaphoreType.DMA((2,)),
            pltpu.SemaphoreType.DMA,
        ],
        (*pieces, *slots, pre),
        2 * rows * units * width,
    )
    return grad, sums.reshape(units)


def hidden_sum(lefts, slots, tok, order, cuts, flops):
    rows = lefts[0].shape[0]
    half = lefts[0].shape[1]
    width = slots[0].shape[1]
    depth = half * len(lefts)
    wide = min(width, 1024)

    def kernel(*refs):
        left_refs, slot_refs = refs[: len(lefts)], refs[len(lefts) : len(lefts) + len(slots)]
        rest = refs[len(lefts) + len(slots) :]
        own_ref, other_refs = rest[0], rest[1 : 1 + len(order) * cuts]
        x, w, own_buf, out_buf, x_sem, w_sem, out_sem = rest[1 + len(order) * cuts :]
        x_copies = []
        for index, left in enumerate(left_refs):
            x_copies.append(pltpu.make_async_copy(left, x.at[index], x_sem.at[index]))
            x_copies[-1].start()
        w_copies = start_rows(slot_refs, w, w_sem)
        for copy in x_copies:
            copy.wait()
        wait_rows(w_copies, 0, depth)

        def product(block, columns):
            part = pl.ds(block * tok, tok)
            total = dot_nn(x[0, part], w[pl.ds(0, half), columns])
            for index in range(1, len(lefts)):
                total = total + dot_nn(x[index, part], w[pl.ds(index * half, half), columns])
            return total

        sent = []
        for count, block in enumerate(order):
            slot = count % 2
            if count >= 2:
                for copy in sent[count - 2]:
                    copy.wait()

            @pl.loop(0, width // wide)
            def _(index):
                columns = pl.ds(pl.multiple_of(index * wide, wide), wide)
                out_buf[slot, :, columns] = product(block, columns).astype(BF)

            size = tok // cuts
            sent.append(
                [
                    pltpu.make_async_copy(
                        out_buf.at[slot, pl.ds(cut * size, size)],
                        other_refs[count * cuts + cut],
                        out_sem.at[slot, cut],
                    )
                    for cut in range(cuts)
                ]
            )
            for copy in sent[count]:
                copy.start()

        @pl.loop(0, width // wide)
        def _(index):
            columns = pl.ds(pl.multiple_of(index * wide, wide), wide)
            own_buf[:, columns] = product(0, columns)

        own_copy = pltpu.make_async_copy(own_buf, own_ref, out_sem.at[2, 0])
        own_copy.start()
        for copies in sent[-2:]:
            for copy in copies:
                copy.wait()
        own_copy.wait()

    return call(
        kernel,
        "hidden_sum",
        tuple(
            [jax.ShapeDtypeStruct((tok, width), F32)]
            + [jax.ShapeDtypeStruct((tok // cuts, width), BF)] * (len(order) * cuts)
        ),
        [
            pltpu.VMEM((len(lefts), rows, half), BF),
            pltpu.VMEM((depth, width), BF),
            pltpu.VMEM((tok, width), F32),
            pltpu.VMEM((2, tok, width), BF),
            pltpu.SemaphoreType.DMA((len(lefts),)),
            pltpu.SemaphoreType.DMA((len(slots),)),
            pltpu.SemaphoreType.DMA((3, cuts)),
        ],
        (*lefts, *slots),
        flops,
    )


def weight_terms(left, pieces, slots, size):
    rows, units = left.shape
    width = pieces[0].shape[1]
    def kernel(*refs):
        left_ref, piece_refs = refs[0], refs[1 : 1 + len(pieces)]
        out_ref, l, x, out_buf, l_sem, x_sem, out_sem = refs[1 + len(pieces) :]
        l_copy = pltpu.make_async_copy(left_ref, l, l_sem)
        l_copy.start()
        x_copies = start_rows(piece_refs, x, x_sem)
        l_copy.wait()
        wait_rows(x_copies, 0, rows)
        sent = []
        wide = min(width, 1024)
        source = slots() if size == TILE else range(units // TILE)
        for tile in range(units // TILE):
            slot = tile % 2
            if tile >= 2:
                sent[tile - 2].wait()
            columns = pl.ds(pl.multiple_of(source[tile] * TILE, TILE), TILE)

            @pl.loop(0, width // wide)
            def _(index):
                span = pl.ds(pl.multiple_of(index * wide, wide), wide)
                out_buf[slot, :, span] = dot_tn(l[:, columns], x[:, span]).astype(BF)

            sent.append(
                pltpu.make_async_copy(
                    out_buf.at[slot], out_ref.at[pl.ds(tile * TILE, TILE)], out_sem.at[slot]
                )
            )
            sent[tile].start()
        for copy in sent[-2:]:
            copy.wait()

    return call(
        kernel,
        "weight_terms",
        jax.ShapeDtypeStruct((units, width), BF),
        [
            pltpu.VMEM((rows, units), BF),
            pltpu.VMEM((rows, width), BF),
            pltpu.VMEM((2, TILE, width), BF),
            pltpu.SemaphoreType.DMA,
            pltpu.SemaphoreType.DMA((len(pieces),)),
            pltpu.SemaphoreType.DMA((2,)),
        ],
        (left, *pieces),
        2 * rows * units * width,
    )


def after(value, *needed):
    return lax.optimization_barrier((value, needed))[0]


def add_wide(left, right):
    return left.astype(F32) + right.astype(F32)


def add_low(left, right):
    return add_wide(left, right).astype(BF)


class Links:
    def __init__(self):
        self.seq_n = lax.axis_size("seq")
        self.dp_n = lax.axis_size("dp")
        self.z_n = self.dp_n // 2
        half = self.seq_n // 2
        self.ring = list(range(half)) + list(range(self.seq_n - 1, half - 1, -1))
        self.seq = lax.axis_index("seq")
        dp = lax.axis_index("dp")
        self.z = dp // 2
        self.core = dp % 2
        self.chips = list(range(0, self.z_n, 2)) + list(range(self.z_n - 1, 0, -2))
        self.chip_place = [self.chips.index(z) for z in range(self.z_n)]
        self.chip_pos = jnp.where(self.z % 2 == 0, self.z // 2, self.z_n - 1 - self.z // 2)
        self.place = [self.ring.index(s) for s in range(self.seq_n)]
        self.pos = jnp.where(self.seq < half, self.seq, self.seq_n - 1 + half - self.seq)

    def seq_at(self, rel):
        n, place = self.seq_n, (self.pos + rel) % self.seq_n
        return jnp.where(place < n // 2, place, n - 1 + n // 2 - place)

    def from_rel(self, value, rel):
        n = self.seq_n
        pairs = [(self.ring[(p + rel) % n], self.ring[p]) for p in range(n)]
        return lax.ppermute(value, "seq", pairs)

    def swap_core(self, value):
        pairs = [(i, i ^ 1) for i in range(self.dp_n)]
        return lax.ppermute(value, "dp", pairs)

    def z_next(self, value):
        pairs = [(self.chips[p - 1], self.chips[p]) for p in range(self.z_n)]
        return lax.ppermute(value, "dp", [(2 * i + c, 2 * j + c) for i, j in pairs for c in range(2)])

    def z_back(self, value):
        pairs = [(self.chips[p], self.chips[p - 1]) for p in range(self.z_n)]
        return lax.ppermute(value, "dp", [(2 * i + c, 2 * j + c) for i, j in pairs for c in range(2)])

    def gather_direct(self, value):
        return [value] + [self.from_rel(value, r) for r in range(1, self.seq_n)]

    def gather_near(self, value):
        if self.seq_n != 4:
            return self.gather_direct(value)
        return [value, self.from_rel(value, 1), None, self.from_rel(value, 3)]

    def gather_far(self, blocks):
        if self.seq_n != 4:
            return blocks
        half = blocks[0].shape[0] // 2
        top = self.from_rel(blocks[1][:half], 1)
        low = self.from_rel(blocks[3][half:], 3)
        return [blocks[0], blocks[1], top, low, blocks[3]]

    def exchange(self, parts):
        n = self.seq_n
        got = [parts[0]] + [None] * (n - 1)
        for r in range(1, n):
            got[n - r] = self.from_rel(parts[r], n - r)
        return got

    @property
    def sum_order(self):
        return (2, 1, 3) if self.seq_n == 4 else tuple(range(1, self.seq_n))

    @property
    def sum_cuts(self):
        return 2 if self.seq_n == 4 else 1

    def sum_far(self, parts):
        if self.seq_n != 4:
            return self.exchange(list(parts))[1:]
        far_top, far_low, right_top, right_low, left_top, left_low = parts[1:]
        return [
            self.from_rel(far_top, 3),
            self.from_rel(far_low, 1),
            self.from_rel(right_low, 3),
            self.from_rel(left_top, 1),
        ]

    def sum_near(self, parts, far, *needed):
        if self.seq_n != 4:
            return far
        return [
            self.from_rel(after(add_low(parts[3], far[0]), needed), 3),
            self.from_rel(after(add_low(parts[6], far[1]), needed), 1),
        ]

    def sum_end(self, own, far, near):
        if self.seq_n != 4:
            for member in near:
                own = own + member.astype(F32)
            return own
        half = own.shape[0] // 2
        return jnp.concatenate(
            [
                own[:half] + add_wide(near[0], far[3]),
                own[half:] + add_wide(far[2], near[1]),
            ],
            0,
        )

    def chips_ordered(self, blocks):
        n = self.z_n
        return [
            lax.select_n(self.z, *[blocks[(self.chip_place[z] - self.chip_place[k]) % n] for z in range(n)])
            for k in range(n)
        ]

    def chip_before(self, m):
        n, place = self.z_n, (self.chip_pos - m) % self.z_n
        return jnp.where(place < (n + 1) // 2, 2 * place, 2 * (n - 1 - place) + 1)

    def other_chip(self, value, bits):
        pairs = [(2 * z + c, 2 * (z ^ bits) + c) for z in range(self.z_n) for c in range(2)]
        return lax.ppermute(value, "dp", pairs)

    def term_slots(self):
        if self.z_n != 4:
            return list(range(self.z_n))
        z = lax.axis_index("dp") // 2
        outer = (z == 0) | (z == 3)
        return [0, jnp.where(outer, 3, 1), jnp.where(outer, 1, 3), 2]

    def first_term(self, own, came, rows, *needed):
        own = after(own, needed)
        if rows % 64 == 0:
            return add_terms([(own, 2 * rows), (came, 2 * rows)], 2 * rows)
        return add_low(own[2 * rows :], came[2 * rows :])

    def first_move(self, term, *needed):
        return self.other_chip(after(term, needed), 1) if self.z_n == 4 else None

    def second_term(self, own, came, first, rows, *needed):
        own = after(own, needed)
        if self.z_n != 4:
            total = add_wide(own, came)
            moved = total[(self.z_n - 1) * rows :].astype(BF)
            for m in range(self.z_n - 2, 0, -1):
                moved = self.z_back(moved)
                moved = (total[m * rows : (m + 1) * rows] + moved.astype(F32)).astype(BF)
            return self.z_back(moved)
        if rows % 64 == 0:
            return add_terms([(own, rows), (came, rows), (first, rows)], rows)
        part = slice(rows, 2 * rows)
        return (add_wide(own[part], came[part]) + first[part].astype(F32)).astype(BF)

    def second_move(self, term, *needed):
        return self.other_chip(after(term, needed), 2) if self.z_n == 4 else term

    def chip_sum_end(self, own, came, first, second, rows, *needed):
        if rows % 64 == 0 and first is not None:
            members = [(after(own, needed), 0), (came, 0), (first, 0), (second, 0)]
            return add_terms(members, rows, F32)
        total = add_wide(own[:rows], came[:rows]) + second.astype(F32)
        return total if first is None else total + first[:rows].astype(F32)

    def other_seq(self, value, bit):
        return lax.ppermute(value, "seq", [(i, i ^ bit) for i in range(self.seq_n)])

    def other_dp(self, value, bit):
        return lax.ppermute(value, "dp", [(i, i ^ bit) for i in range(self.dp_n)])


def shards(
    tokens,
    doc_ids,
    pad_mask,
    attn_norm_gain,
    attn_norm_bias,
    qkv_weight,
    query_bias,
    value_bias,
    out_weight,
    out_bias,
    mlp_norm_gain,
    mlp_norm_bias,
    fc_weight,
    fc_bias,
    proj_weight,
    proj_bias,
    cotangent,
):
    links = Links()
    seq_n, dp_n, z_n = links.seq_n, links.dp_n, links.z_n
    tok = tokens.shape[1]
    width = tokens.shape[2]
    scale = HDIM ** (-0.5)
    gain_one = attn_norm_gain.astype(F32)
    shift_one = attn_norm_bias.astype(F32)
    out_shift = out_bias.astype(F32)
    gain_two = mlp_norm_gain.astype(F32)
    shift_two = mlp_norm_bias.astype(F32)
    proj_shift = proj_bias.astype(F32)

    docs = doc_ids[0]
    codes = jnp.where(pad_mask[0] == 1, docs, -1)
    codes = jnp.stack([codes // 128, codes % 128] + [jnp.zeros_like(codes)] * 14).astype(BF)

    units = fc_weight.shape[0]
    split = z_n * units

    block_index = jnp.arange(dp_n)
    owner = 2 * links.chip_before(block_index % z_n) + (links.core ^ (block_index // z_n))
    owner = owner[:, None] == jnp.arange(dp_n)[None, :]
    own_seq = jnp.arange(seq_n) == links.seq
    fc_shift = fc_bias.reshape(dp_n, seq_n, units).astype(F32)
    fc_shift = jnp.sum(jnp.where(own_seq[None, :, None], fc_shift, 0.0), 1)
    fc_shift = jnp.sum(jnp.where(owner[:, :, None], fc_shift[None], 0.0), 1).reshape(-1)
    qkv_rows = qkv_weight.shape[0]
    qkv_shift = jnp.concatenate(
        [query_bias.astype(F32), jnp.zeros((HDIM,), F32), value_bias.astype(F32)]
    ).reshape(dp_n, seq_n, qkv_rows)
    qkv_shift = jnp.sum(jnp.where(own_seq[None, :, None], qkv_shift, 0.0), 1).reshape(-1, 1)

    qkv_chips = [qkv_weight, links.z_next(qkv_weight)]
    grad_low = cotangent.reshape(tok, width)

    def norm_one(member):
        flat = member.reshape(tok, width).astype(F32)
        normed, inverse = normalize(flat)
        return (normed * gain_one + shift_one).astype(BF), normed, inverse

    hidden_one, normed_one, inverse_one = norm_one(tokens)
    ones = links.gather_near(after(hidden_one, qkv_chips[1]))
    qkv_chips[1] = after(qkv_chips[1], hidden_one)
    for _ in range(z_n - 2):
        qkv_chips.append(links.z_next(qkv_chips[-1]))
    fc_chips = [fc_weight, links.z_next(after(fc_weight, qkv_chips))]
    qkv_chips = after(qkv_chips, ones[1], ones[-1], qkv_shift, fc_shift)
    out_full = lax.all_gather(out_weight, ("dp", "seq"), axis=0, tiled=True)

    mine = jnp.stack(links.chips_ordered(qkv_chips), 0)
    other = links.swap_core(mine)

    def both_cores(mine, other):
        first = links.core == 0
        part = jnp.stack([jnp.where(first, mine, other), jnp.where(first, other, mine)], 1)
        return part.reshape(dp_n * qkv_rows, width)

    qkv_part = both_cores(mine, other)
    ones = links.gather_far(ones)

    def columns_of(part, shift, *blocks):
        return [(dot_nt(part, member) + shift).astype(BF) for member in blocks]

    far_place = seq_n // 2
    near_places = [r for r in range(seq_n) if r != far_place]
    near_columns = columns_of(qkv_part, qkv_shift, *ones[:far_place], *ones[1 - far_place :])
    far_rows = ones[far_place : far_place + len(ones) - seq_n + 1]
    far_columns = columns_of(after(qkv_part, near_columns), qkv_shift, jnp.concatenate(far_rows, 0))
    columns = dict(zip(near_places, near_columns)) | {far_place: far_columns[0]}
    got = links.exchange([columns[r] for r in range(seq_n)])

    def assemble(*got):
        got = [member.reshape(dp_n, qkv_rows, tok) for member in got]
        return jnp.stack(
            [
                lax.select_n(links.pos, *[got[(links.place[s] - p) % seq_n] for p in range(seq_n)])
                for s in range(seq_n)
            ],
            1,
        ).reshape(-1, tok)

    qkv = assemble(*got)
    query = qkv[:width].reshape(HEADS, HDIM, tok)
    pairs = links.gather_direct(jnp.concatenate([qkv[width:], codes], 0))
    fc_chips.append(links.z_next(after(fc_chips[1], pairs)))
    grads = links.gather_near(after(grad_low, pairs))

    spot = jnp.arange(tok, dtype=jnp.int32)

    def masked_scores(query, pairs):
        codes_all = [
            (member[2 * HDIM].astype(F32) * 128 + member[2 * HDIM + 1].astype(F32)).astype(jnp.int32)
            for member in pairs
        ]
        allowed = []
        for r in range(seq_n):
            place = links.seq_at(r)
            same = codes_all[r][:, None] == docs[None, :]
            if r == 0:
                allowed.append((same & (spot[:, None] < spot[None, :])) | (spot[:, None] == spot[None, :]))
            else:
                allowed.append(same & (place < links.seq))
        allowed = jnp.concatenate(allowed, 0)[None]
        keys = jnp.concatenate([member[:HDIM] for member in pairs], 1)
        values = jnp.concatenate([member[HDIM : 2 * HDIM] for member in pairs], 1)
        scores = jnp.einsum("dk,hdq->hkq", keys, query, preferred_element_type=F32) * scale
        return allowed, keys, values, jnp.where(allowed, scores, NEGATIVE)

    def attend(query, pairs):
        allowed, keys, values, scores = masked_scores(query, pairs)
        highest = jnp.max(scores, 1, keepdims=True)
        weights = jnp.where(allowed, jnp.exp(scores - highest), 0.0)
        total = jnp.sum(weights, 1, keepdims=True)
        attn = jnp.einsum("dk,hkq->hdq", values, weights.astype(BF), preferred_element_type=F32) / total
        return attn, highest + jnp.log(total), attn.reshape(width, tok).astype(BF).T

    attn, log_total, attn_low = attend(query, pairs)
    for _ in range(z_n - 3):
        fc_chips.append(links.z_next(after(fc_chips[-1], attn_low)))
    proj_chips = [proj_weight, links.z_next(after(proj_weight, fc_chips[2], attn_low))]

    def norm_two(attn_low, out_full, tokens):
        flat = tokens.reshape(tok, width).astype(F32)
        middle = flat + dot_nt(attn_low, out_full) + out_shift
        normed, inverse = normalize(middle)
        return middle, normed, inverse, (normed * gain_two + shift_two).astype(BF)

    middle, normed_two, inverse_two, hidden_two = norm_two(attn_low, out_full, tokens)
    twos = links.gather_near(after(hidden_two, grads[1], grads[-1]))

    twos = links.gather_far(twos)
    qkv_mine = lax.all_gather(after(mine, twos[1], twos[-1]), "seq", axis=0, tiled=True)
    qkv_mine = qkv_mine.reshape(-1, width)
    fc_chips = after(fc_chips, twos[1], twos[-1])
    fc_other = links.swap_core(join_rows(fc_chips))
    grads = links.gather_far(after(grads, twos))

    proj_chips.append(links.z_next(after(proj_chips[-1], twos)))
    pre_mine, act_mine = hidden_forward(after(twos, proj_chips[1]), fc_chips, fc_shift[:split])
    ready = act_mine[:8, :HDIM]
    pre_other, act_other = hidden_forward(after(twos, ready), [fc_other], fc_shift[split:])
    attns = links.gather_near(after(attn_low, grads, act_other))
    grads = after(grads, act_other)

    proj_sent = weight_terms(after(act_other, proj_chips[2]), grads, links.term_slots, units)
    proj_came = links.swap_core(proj_sent)
    proj_own = weight_terms(after(act_mine, proj_sent), grads, links.term_slots, units)
    for _ in range(z_n - 3):
        proj_chips.append(links.z_next(after(proj_chips[-1], act_other)))
    attns = links.gather_far(after(attns, proj_own))
    proj_term = links.first_term(proj_own, proj_came, units)
    proj_first = links.first_move(proj_term)
    proj_chips = after(proj_chips, proj_term, attns[1], attns[-1])
    proj_mine = join_rows(proj_chips)
    proj_other = links.swap_core(proj_mine)

    grad_mine, bias_mine = hidden_backward(grads, proj_chips, pre_mine)
    grad_other, bias_other = hidden_backward(after(grads, bias_mine), [proj_other], pre_other)
    fc_bias_sum = jnp.concatenate([bias_mine, bias_other])
    qkv_other = links.swap_core(after(qkv_mine, bias_mine))
    hidden_parts = hidden_sum(
        (after(grad_mine, attns), grad_other),
        [*fc_chips, fc_other],
        tok,
        links.sum_order,
        links.sum_cuts,
        4 * seq_n * tok * split * width,
    )
    hidden_far = links.sum_far(after(hidden_parts, proj_first) if z_n == 4 else hidden_parts)
    proj_term = links.second_term(proj_own, proj_came, proj_first, units, hidden_parts)
    proj_second = links.second_move(proj_term)
    fc_sent = weight_terms(after(grad_other, hidden_far, proj_second), twos, links.term_slots, units)
    fc_came = links.swap_core(fc_sent)
    fc_own = weight_terms(after(grad_mine, fc_sent, hidden_far), twos, links.term_slots, units)
    hidden_near = links.sum_near(hidden_parts, hidden_far)
    fc_term = links.first_term(fc_own, fc_came, units)
    fc_first = links.first_move(fc_term)
    mlp_parts = hidden_sum(
        (after(act_mine, fc_term), act_other), [proj_mine, proj_other], tok, tuple(range(1, seq_n)), 1, 0
    )
    mlp_came = [links.from_rel(mlp_parts[r], seq_n - r) for r in range(1, seq_n)]

    inverse_two = gate(inverse_two, fc_term)

    def middle_back(parts, far, near, normed_two, inverse_two, grad_low):
        grad_hidden = links.sum_end(parts, far, near)
        grad_out = grad_low.astype(F32)
        grad_middle = grad_out + norm_back(grad_hidden * gain_two, normed_two, inverse_two)
        sums = [
            jnp.sum(grad_middle, 0),
            jnp.sum(grad_hidden * normed_two, 0),
            jnp.sum(grad_hidden, 0),
            jnp.sum(grad_out, 0),
        ]
        low = grad_middle.astype(BF)
        return grad_middle, low, low.T, sums

    grad_middle, grad_middle_low, grad_middle_turned, early = middle_back(hidden_parts[0], hidden_far, hidden_near, normed_two, inverse_two, grad_low
    )

    def to_owners(member, needed=()):
        member = member.reshape(dp_n, seq_n, -1, tok)
        sent = [
            lax.dynamic_index_in_dim(member, links.seq_at(r), 1, False).reshape(-1, tok) for r in range(seq_n)
        ]
        return links.exchange(after(sent, needed))


    def ordered_parts(columns, rows):
        part = dot_nn(jnp.concatenate(columns, 1), jnp.concatenate(rows, 0))
        part = part.reshape(z_n, 2, -1, width)
        sent = lax.dynamic_index_in_dim(part, 1 - links.core, 1, False).astype(BF)
        return sent, lax.dynamic_index_in_dim(part, links.core, 1, False)

    def ordered_terms(kept, came):
        order = [links.z ^ k for k in (0, 2, 1, 3)] if z_n == 4 else [links.chip_before(m) for m in range(z_n)]
        return [
            jnp.concatenate([lax.dynamic_index_in_dim(member, k, 0, False) for k in order], 0)
            for member in (kept.astype(BF), came)
        ]

    def attend_back(out_full, grad_middle_low, query, pairs, attn, log_total):
        grad_attn = lax.dot_general(
            out_full, grad_middle_low, (((0,), (1,)), ((), ())), preferred_element_type=F32
        )
        grad_attn_low = grad_attn.astype(BF).reshape(HEADS, HDIM, tok)
        delta = jnp.sum(grad_attn_low.astype(F32) * attn, 1, keepdims=True)
        allowed, keys, values, scores = masked_scores(query, pairs)
        probs = jnp.where(allowed, jnp.exp(scores - log_total), 0.0)
        grad_probs = jnp.einsum("dk,hdq->hkq", values, grad_attn_low, preferred_element_type=F32)
        grad_scores = (probs * (grad_probs - delta)).astype(BF)
        grad_query = jnp.einsum("dk,hkq->hdq", keys, grad_scores, preferred_element_type=F32) * scale
        grad_keys = jnp.einsum("hkq,hdq->dk", grad_scores, query, preferred_element_type=F32) * scale
        grad_values = jnp.einsum("hkq,hdq->dk", probs.astype(BF), grad_attn_low, preferred_element_type=F32)
        grad_pair = jnp.concatenate([grad_keys, grad_values], 0)
        parts = [grad_pair[:, r * tok : (r + 1) * tok] for r in range(seq_n)]
        grad_query = grad_query.reshape(width, tok)
        return grad_query.astype(BF), jnp.sum(grad_query, 1), [parts[0]] + [part.astype(BF) for part in parts[1:]]

    grad_middle_low = gate(grad_middle_low, fc_first, mlp_parts)
    grad_query, query_sum, parts = attend_back(out_full, grad_middle_low, query, pairs, attn, log_total
    )
    came = links.exchange(after(parts, mlp_came))
    fc_second = links.second_move(links.second_term(fc_own, fc_came, fc_first, units, parts))
    out_columns = to_owners(grad_middle_turned, mlp_came[:1])
    out_sent, out_kept = ordered_parts(after(out_columns, parts), attns)
    out_came = links.swap_core(out_sent)

    def all_grads(grad_query, came):
        grad_pair = came[0]
        for member in came[1:]:
            grad_pair = grad_pair + member.astype(F32)
        return jnp.concatenate([grad_query, grad_pair.astype(BF)], 0), jnp.sum(grad_pair[HDIM:], 1)

    grad_qkv, value_sum = all_grads(grad_query, came)
    qkv_columns = to_owners(grad_qkv)
    out_rows = out_weight.shape[0]
    out_own, out_came = ordered_terms(out_kept, out_came)
    def tokens_back(grad_qkv, qkv_mine, qkv_other, grad_middle, normed_one, inverse_one):
        by_core = grad_qkv.reshape(z_n, 2, seq_n, qkv_rows, tok)

        def rows_of(core):
            rows = lax.dynamic_index_in_dim(by_core, core, 1, False)
            return rows.transpose(1, 0, 2, 3).reshape(-1, tok)

        grad_hidden = dot_tn(rows_of(links.core), qkv_mine) + dot_tn(rows_of(1 - links.core), qkv_other)
        back = grad_middle + norm_back(grad_hidden * gain_one, normed_one, inverse_one)
        return back.astype(BF), [jnp.sum(grad_hidden * normed_one, 0), jnp.sum(grad_hidden, 0)]

    tokens_grad, late = tokens_back(
        grad_qkv, qkv_mine, qkv_other, grad_middle, normed_one, inverse_one
    )
    out_first = links.first_move(links.first_term(out_own, out_came, out_rows))
    tokens_grad = tokens_grad.reshape(tokens.shape)
    fc_bias_sum = jnp.sum(jnp.where(owner[:, :, None], fc_bias_sum.reshape(dp_n, 1, units), 0.0), 0)
    fc_bias_sum = jnp.where(own_seq[None, :, None], fc_bias_sum[:, None, :], 0.0).reshape(-1)
    sums = jnp.concatenate(early + late + [query_sum, fc_bias_sum, value_sum])
    qkv_sent, qkv_kept = ordered_parts(after(qkv_columns, tokens_grad), ones)
    qkv_came = links.swap_core(qkv_sent)
    qkv_own, qkv_came = ordered_terms(qkv_kept, qkv_came)
    out_second = links.second_move(links.second_term(out_own, out_came, out_first, out_rows))
    qkv_term = links.first_term(qkv_own, qkv_came, qkv_rows)
    qkv_first = links.first_move(qkv_term, fc_second)
    sums = after(sums, qkv_term)
    bit = 1
    while bit < seq_n:
        sums = sums + links.other_seq(sums, bit)
        bit *= 2
    sums = sums + links.other_dp(sums, 1)
    bit = 2
    moved = links.other_dp(sums, bit)
    qkv_second = links.second_move(links.second_term(qkv_own, qkv_came, qkv_first, qkv_rows))
    sums = after(sums, qkv_second) + moved
    bit *= 2
    while bit < dp_n:
        sums = sums + links.other_dp(sums, bit)
        bit *= 2
    proj_grad = links.chip_sum_end(proj_own, proj_came, proj_first, proj_second, units, qkv_first)
    fc_grad = links.chip_sum_end(fc_own, fc_came, fc_first, fc_second, units, qkv_first)
    out_grad = links.chip_sum_end(out_own, out_came, out_first, out_second, out_rows)
    mlp = sum(member.astype(F32) for member in [mlp_parts[0], *after(mlp_came, fc_grad)])
    block_out = (middle + mlp + proj_shift).astype(BF).reshape(tokens.shape)
    qkv_grad = links.chip_sum_end(qkv_own, qkv_came, qkv_first, qkv_second, qkv_rows)

    wide = [sums[i * width : (i + 1) * width] for i in range(7)]
    fc_bias_grad = sums[7 * width : 7 * width + fc_bias.shape[0]]
    value_bias_grad = sums[7 * width + fc_bias.shape[0] :]
    return (
        block_out,
        tokens_grad,
        wide[4],
        wide[5],
        qkv_grad,
        wide[6],
        value_bias_grad,
        out_grad,
        wide[0],
        wide[1],
        wide[2],
        fc_grad,
        fc_bias_grad,
        proj_grad,
        wide[3],
    )


def solution(mesh):
    rows = P(("dp", "seq"), None)
    act = P("dp", "seq", None)
    return jax.shard_map(
        shards,
        mesh=mesh,
        in_specs=(
            act,
            P("dp", "seq"),
            P("dp", "seq"),
            P(),
            P(),
            rows,
            P(),
            P(),
            rows,
            P(),
            P(),
            P(),
            rows,
            P(),
            rows,
            P(),
            act,
        ),
        out_specs=(
            act,
            act,
            P(),
            P(),
            rows,
            P(),
            P(),
            rows,
            P(),
            P(),
            P(),
            rows,
            P(),
            rows,
            P(),
        ),
        check_vma=False,
    )
```
